32 devices in a mesh: seq: 4 (over x, core), head: 2 (over y), blk: 4 (over z).
Axes of the slice: x: 2, y: 2, z: 4, core: 2. Of those that a mesh axis runs over, the one named last changes fastest.
Arguments:
- tokens: bfloat16 [4096, 1024], P(('seq', 'head', 'blk')), may hold values from -6 to 6
- out_grad: bfloat16 [4096, 1024], P(('seq', 'head', 'blk')), may hold values from -6 to 6
- w_qkv: bfloat16 [1024, 3072], P(('head', 'blk')), may hold values from -0.1875 to 0.1875
- w_out: bfloat16 [1024, 1024], P(('head', 'blk')), may hold values from -9 to 9
- fc_in: bfloat16 [4096, 1024], P(('head', 'blk')), may hold values from -0.1875 to 0.1875
- fc_out: bfloat16 [4096, 1024], P(('head', 'blk')), may hold values from -0.09375 to 0.09375
- fc_in_bias: bfloat16 [4096], P(('head', 'blk')), may hold values from -3 to 3
- vectors: bfloat16 [1024, 8], P(('head', 'blk')), may hold values from -1.5 to 1.5
Outputs:
- layer_output: float32 [4096, 1024], P(('seq', 'head', 'blk'))
- input_grad: float32 [4096, 1024], P(('seq', 'head', 'blk'))
- grad_w_qkv: float32 [1024, 3072], P(('seq', 'head', 'blk'))
- grad_w_out: float32 [1024, 1024], P(('seq', 'head', 'blk'))
- grad_fc_in: float32 [4096, 1024], P(('seq', 'head', 'blk'))
- grad_fc_out: float32 [4096, 1024], P(('seq', 'head', 'blk'))
- grad_fc_in_bias: float32 [4096], P(('seq', 'head', 'blk'))
- grad_vectors: float32 [1024, 8], P(('seq', 'head', 'blk'))
The draws below stay inside these ranges and needn't reach their ends.
All inputs are finite; a program needn't handle non-finite values.
Results may differ from the reference program's by a relative error of at most 0.015.
Values may be sent and summed in bfloat16 or wider, within the bound.
No kernel may reach another device: no remote copies, remote signals or barrier semaphores. Data moves between devices by JAX's collectives and lax.ppermute only.
A program may use at most 256 MiB of HBM per device.

```python
import math
import jax
import jax.numpy as jnp
from jax import lax

D = 1024
HEADS = 16
HEAD_DIM = 64
FF = 4096
SEQ_LEN = 1024
NSEQS = 4
TOKENS = 4096


def draw_vectors(key, part):
    gain_key, shift_key = jax.random.split(jax.random.fold_in(key, 7))
    gains = jax.random.uniform(gain_key, (D, 2), jnp.float32, 0.5, 1.5)
    shifts = jnp.clip(jax.random.normal(shift_key, (D, 6), jnp.float32), -3.0, 3.0)
    column_scale = jnp.array([0.3, 0.3, 0.5, 0.02, 0.3, 0.3], jnp.float32)
    return jnp.concatenate([gains, shifts * column_scale], axis=1).astype(jnp.bfloat16)


def steps_of(key, extent, pieces, low, top_value):
    level, own = 1.0, jax.random.fold_in(key, 6)
    for axis_at, shards_of in pieces:
        steps = jnp.exp(jax.random.uniform(jax.random.fold_in(own, axis_at), (shards_of,), jnp.float32, low / len(pieces), top_value / len(pieces)))
        level = level * jnp.repeat(steps, extent[axis_at] // shards_of).reshape([-1 if axis == axis_at else 1 for axis in range(len(extent))])
    return level


def normal_values(stream_key, extent, scale, most, pieces=(), held_as=jnp.bfloat16):
    level = steps_of(stream_key, extent, pieces, -0.22, 0.18) if pieces else 1.0
    values = jax.random.normal(stream_key, extent, jnp.float32) * scale * level
    return jnp.minimum(jnp.maximum(values, -most), most).astype(held_as)


def setup_inputs(seed: int = 0) -> dict:
    seeds = jax.random.split(jax.random.key(seed), 9)
    return {
        "tokens": normal_values(seeds[0], (TOKENS, D), 1.0, 6.0, ((0, 32),)),
        "out_grad": normal_values(seeds[1], (TOKENS, D), 1.0, 6.0, ((0, 32),)),
        "w_qkv": normal_values(seeds[2], (D, 3 * D), D ** -0.5, 0.1875, ((0, 8),)),
        "w_out": normal_values(seeds[3], (D, D), 1.5, 9.0, ((0, 8),)),
        "fc_in": normal_values(seeds[4], (FF, D), D ** -0.5, 0.1875, ((0, 8),)),
        "fc_out": normal_values(seeds[5], (FF, D), FF ** -0.5, 0.09375, ((0, 8),)),
        "fc_in_bias": normal_values(seeds[6], (FF,), 0.5, 3.0, ((0, 8),)),
        "vectors": draw_vectors(jax.random.fold_in(seeds[8], 71), 0),
    }


@jax.custom_vjp
def low(v):
    return lax.optimization_barrier(v.astype(jnp.bfloat16)).astype(jnp.float32)

@jax.custom_vjp
def low_back(v):
    return v

def low_keep(v):
    return (low(v), None)

def low_pass(kept, grad):
    return (grad,)

def back_keep(v):
    return (v, None)

def back_low(kept, grad):
    return (low(grad),)
low.defvjp(low_keep, low_pass)
low_back.defvjp(back_keep, back_low)
exact_precision = lax.Precision.HIGHEST

def layer_norm(values, gain_vec, shift_vec):
    center = values - lax.optimization_barrier(jnp.mean(values, axis=-1, keepdims=True))
    spread = lax.optimization_barrier(jnp.mean(center * center, axis=-1, keepdims=True))
    return center * lax.rsqrt(spread + 1e-05) * gain_vec + shift_vec

def split_heads(values):
    return values.reshape(SEQ_LEN, HEADS, HEAD_DIM)

def attend(queries, key_rows, value_rows):
    block_rows = math.gcd(512, SEQ_LEN)
    blocks = queries.reshape(SEQ_LEN // block_rows, block_rows, HEADS, HEAD_DIM)

    def one_block(query_block):
        scores = low_back(jnp.einsum('qhd,khd->hqk', query_block, key_rows, precision=exact_precision))
        probs = jax.nn.softmax(scores, axis=-1)
        return jnp.einsum('hqk,khd->qhd', low(probs), value_rows, precision=exact_precision)
    mixed = lax.map(jax.checkpoint(one_block), blocks)
    return mixed.reshape(SEQ_LEN, D)

def forward(inputs, w_qkv, w_out, fc_in, fc_out, fc_in_bias, vectors):
    projected = jnp.dot(inputs, w_qkv, precision=exact_precision)
    scale = HEAD_DIM ** (-0.5)
    queries = low(low_back((projected[:, :D] + vectors[:, 4]) * scale))
    key_rows = low(low_back(projected[:, D:2 * D]))
    value_rows = low(low_back(projected[:, 2 * D:] + vectors[:, 5]))
    context = low(low_back(attend(split_heads(queries), split_heads(key_rows), split_heads(value_rows))))
    attn_out = low_back(jnp.dot(context, w_out, precision=exact_precision) + vectors[:, 6])
    middle = layer_norm(inputs + attn_out, vectors[:, 0], vectors[:, 2])
    middle_low = low(middle)
    pre_act = low_back(jnp.dot(middle_low, fc_in.T, precision=exact_precision) + fc_in_bias)
    act_low = low(jax.nn.gelu(pre_act, approximate=False))
    ffn_out = low_back(jnp.dot(act_low, fc_out, precision=exact_precision) + vectors[:, 7])
    return layer_norm(middle + ffn_out, vectors[:, 1], vectors[:, 3])

def reference(tokens, out_grad, w_qkv, w_out, fc_in, fc_out, fc_in_bias, vectors):
    weights = (w_qkv.astype(jnp.float32), w_out.astype(jnp.float32), fc_in.astype(jnp.float32), fc_out.astype(jnp.float32), fc_in_bias.astype(jnp.float32), vectors.astype(jnp.float32))
    inputs = tokens.astype(jnp.float32).reshape(NSEQS, SEQ_LEN, D)
    cotangents = out_grad.astype(jnp.float32).reshape(NSEQS, SEQ_LEN, D)

    def one_sequence(summed_grads, sequence_pair):
        outputs, pull_back = jax.vjp(forward, sequence_pair[0], weights[0], weights[1], weights[2], weights[3], weights[4], weights[5])
        gradients = pull_back(sequence_pair[1])
        updated = tuple((summed + gradient for summed, gradient in zip(summed_grads, gradients[1:])))
        return (updated, (outputs, gradients[0]))
    zeros_init = tuple((jnp.zeros_like(weight) for weight in weights))
    summed_grads, (layer_outs, input_grads) = lax.scan(one_sequence, zeros_init, (inputs, cotangents))
    return (layer_outs.reshape(TOKENS, D), input_grads.reshape(TOKENS, D), summed_grads[0], summed_grads[1], summed_grads[2], summed_grads[3], summed_grads[4], summed_grads[5])
```

```python
import math

import jax
import jax.numpy as jnp
from jax import lax
from jax.experimental import pallas as pl
from jax.experimental.pallas import tpu as pltpu
from jax.sharding import PartitionSpec as P

HEAD_DIM = 64


def layer_norm(values, gain_vec, shift_vec):
    center = values - jnp.mean(values, axis=-1, keepdims=True)
    spread = jnp.mean(center * center, axis=-1, keepdims=True)
    return center * lax.rsqrt(spread + 1e-05) * gain_vec + shift_vec


def gelu_exact(values):
    return jax.nn.gelu(values, approximate=False)


def split_heads(values):
    return values.reshape(values.shape[0], values.shape[1] // HEAD_DIM, HEAD_DIM)


def head_scores(left_rows, right_rows):
    return jnp.einsum("qhd,khd->hqk", left_rows, right_rows, preferred_element_type=jnp.float32)


def ffn_part(factors):
    middle_low, grad_pre_full, act_full, grad_ffn = factors
    return jnp.concatenate(
        [
            jnp.einsum("tf,td->fd", grad_pre_full, middle_low, preferred_element_type=jnp.float32),
            jnp.einsum("tf,td->fd", act_full, grad_ffn, preferred_element_type=jnp.float32),
        ],
        axis=1,
    )


def attn_part(factors, extra_cols):
    tokens, grad_proj, context, grad_attn = factors
    return jnp.concatenate(
        [
            jnp.einsum("tn,tc->nc", tokens, grad_proj, preferred_element_type=jnp.float32),
            jnp.einsum("tn,tc->nc", context, grad_attn, preferred_element_type=jnp.float32),
            extra_cols,
        ],
        axis=1,
    )


def general_body(tokens, out_grad, w_qkv, w_out, fc_in, fc_out, fc_in_bias, vectors):
    model_width = tokens.shape[1]
    hidden_units = fc_in.shape[0] * lax.axis_size(("head", "blk"))
    ratio = hidden_units // model_width
    scale = HEAD_DIM ** (-0.5)
    part_qkv = lax.all_gather(w_qkv, ("head", "blk"), axis=0, tiled=True)
    part_out = lax.all_gather(w_out, ("head", "blk"), axis=0, tiled=True)
    part_vec = lax.all_gather(vectors, ("head", "blk"), axis=0, tiled=True)
    part_rows = part_qkv.shape[0]
    projected = jnp.dot(tokens, part_qkv, preferred_element_type=jnp.float32)
    out_full = part_out
    attn_state = (projected, out_full, part_vec)
    projected = attn_state[0]
    out_full = attn_state[1]
    vec_float = attn_state[2].astype(jnp.float32)
    gain_one, gain_two = (vec_float[:, 0], vec_float[:, 1])
    shift_one, shift_two = (vec_float[:, 2], vec_float[:, 3])
    bias_query, bias_value = (vec_float[:, 4], vec_float[:, 5])
    bias_output, bias_ffn = (vec_float[:, 6], vec_float[:, 7])
    queries = ((projected[:, :model_width] + bias_query) * scale).astype(jnp.bfloat16)
    key_rows = projected[:, model_width : 2 * model_width].astype(jnp.bfloat16)
    value_rows = (projected[:, 2 * model_width :] + bias_value).astype(jnp.bfloat16)
    query_heads, key_heads, value_heads = (
        lax.all_to_all(queries, "head", split_axis=1, concat_axis=0, tiled=True),
        lax.all_to_all(key_rows, "head", split_axis=1, concat_axis=0, tiled=True),
        lax.all_to_all(value_rows, "head", split_axis=1, concat_axis=0, tiled=True),
    )
    query_split = split_heads(query_heads)
    group_rows = query_split.shape[0]
    group_width = key_heads.shape[1]
    seq_rows = group_rows * lax.axis_size("blk")
    portion = (
        lax.all_gather(key_heads, "blk", axis=0, tiled=True),
        lax.all_gather(value_heads, "blk", axis=0, tiled=True),
    )
    scores = head_scores(query_split, split_heads(portion[0]))
    run_sum = jnp.sum(jnp.exp(scores), axis=-1)
    key_all = portion[0]
    value_all = portion[1]
    run_sum, key_all, value_all = (run_sum, key_all, value_all)
    log_total = jnp.log(run_sum)
    block_rows = math.gcd(512, seq_rows)
    block_count = seq_rows // block_rows
    key_blocks = key_all.reshape(block_count, block_rows, group_width)
    value_blocks = value_all.reshape(block_count, block_rows, group_width)

    def mix_block(totals, pair):
        scores = head_scores(query_split, split_heads(pair[0]))
        probs_low = jnp.exp(scores - log_total[:, :, None]).astype(jnp.bfloat16)
        return (
            totals
            + jnp.einsum(
                "hqk,khd->qhd", probs_low, split_heads(pair[1]), preferred_element_type=jnp.float32
            ),
            None,
        )

    mixed, unused = lax.scan(
        mix_block, jnp.zeros(query_split.shape, jnp.float32), (key_blocks, value_blocks)
    )
    context = lax.all_to_all(
        mixed.reshape(group_rows, -1).astype(jnp.bfloat16),
        "head",
        split_axis=0,
        concat_axis=1,
        tiled=True,
    )
    attn_out = jnp.dot(context, out_full, preferred_element_type=jnp.float32) + bias_output
    residual_one = tokens.astype(jnp.float32) + attn_out
    middle, norm_one_back = jax.vjp(layer_norm, residual_one, gain_one, shift_one)
    middle_low = middle.astype(jnp.bfloat16)
    part_in = lax.all_gather(fc_in, ("head", "blk"), axis=0, tiled=True)
    part_out = lax.all_gather(fc_out, ("head", "blk"), axis=0, tiled=True)
    part_bias = lax.all_gather(fc_in_bias, ("head", "blk"), axis=0, tiled=True)
    pre_part = jnp.einsum("td,fd->tf", middle_low, part_in, preferred_element_type=jnp.float32)
    pre_part = pre_part + part_bias.astype(jnp.float32)
    act_part = gelu_exact(pre_part).astype(jnp.bfloat16)
    summed = jnp.dot(act_part, part_out, preferred_element_type=jnp.float32)
    ffn_pre_full = pre_part
    residual_two = middle + summed + bias_ffn
    layer_output, norm_two_back = jax.vjp(layer_norm, residual_two, gain_two, shift_two)
    grad_resid_two, grad_gain_two, grad_shift_two = norm_two_back(out_grad.astype(jnp.float32))
    grad_ffn = grad_resid_two.astype(jnp.bfloat16)
    qkv_flat = w_qkv.reshape(fc_in.shape[0], -1)
    portion = (
        lax.all_gather(fc_in, ("head", "blk"), axis=0, tiled=True),
        lax.all_gather(fc_out, ("head", "blk"), axis=0, tiled=True),
        lax.all_gather(qkv_flat, ("head", "blk"), axis=0, tiled=True),
    )
    part_in = portion[0]
    part_rows = part_in.shape[0]
    pre_part = ffn_pre_full
    grad_act = jnp.einsum("td,fd->tf", grad_ffn, portion[1], preferred_element_type=jnp.float32)
    grad_pre = jax.vjp(gelu_exact, pre_part)[1](grad_act)[0].astype(jnp.bfloat16)
    grad_mid = jnp.dot(grad_pre, part_in, preferred_element_type=jnp.float32)
    grad_mid, grad_pre_all = (grad_mid, grad_pre)
    qkv_gathered = portion[2]
    qkv_full = qkv_gathered.reshape(model_width, 3 * model_width)
    grad_resid_one, grad_gain_one, grad_shift_one = norm_one_back(grad_resid_two + grad_mid)
    grad_attn = grad_resid_one.astype(jnp.bfloat16)
    grad_context = jnp.einsum(
        "td,ed->te", grad_attn, out_full, preferred_element_type=jnp.float32
    ).astype(jnp.bfloat16)
    grad_ctx_heads = lax.all_to_all(grad_context, "head", split_axis=1, concat_axis=0, tiled=True)
    grad_ctx_split = split_heads(grad_ctx_heads)
    delta_heads = jnp.sum(grad_ctx_split.astype(jnp.float32) * mixed, axis=-1).T

    def back_block(grad_query, pair):
        key_part = split_heads(pair[0])
        value_part = split_heads(pair[1])
        scores = head_scores(query_split, key_part)
        probs = jnp.exp(scores - log_total[:, :, None])
        dprobs = head_scores(grad_ctx_split, value_part)
        dscores = (probs * (dprobs - delta_heads[:, :, None])).astype(jnp.bfloat16)
        grad_query = grad_query + jnp.einsum(
            "hqk,khd->qhd", dscores, key_part, preferred_element_type=jnp.float32
        )
        grad_key = jnp.einsum(
            "hqk,qhd->khd", dscores, query_split, preferred_element_type=jnp.float32
        )
        grad_value = jnp.einsum(
            "hqk,qhd->khd",
            probs.astype(jnp.bfloat16),
            grad_ctx_split,
            preferred_element_type=jnp.float32,
        )
        part_rows = pair[0].shape[0]
        return (
            grad_query,
            jnp.concatenate(
                [grad_key.reshape(part_rows, -1), grad_value.reshape(part_rows, -1)], axis=1
            ),
        )

    grad_query_heads, kv_terms = lax.scan(
        back_block, jnp.zeros(query_split.shape, jnp.float32), (key_blocks, value_blocks)
    )
    kv_own = lax.psum_scatter(
        kv_terms.reshape(seq_rows, 2 * group_width).astype(jnp.bfloat16),
        "blk",
        scatter_dimension=0,
        tiled=True,
    ).astype(jnp.float32)
    grad_query_tok, grad_key_tok, grad_value_tok = (
        lax.all_to_all(
            grad_query_heads.reshape(group_rows, -1).astype(jnp.bfloat16),
            "head",
            split_axis=0,
            concat_axis=1,
            tiled=True,
        ),
        lax.all_to_all(
            kv_own[:, :group_width].astype(jnp.bfloat16),
            "head",
            split_axis=0,
            concat_axis=1,
            tiled=True,
        ),
        lax.all_to_all(
            kv_own[:, group_width:].astype(jnp.bfloat16),
            "head",
            split_axis=0,
            concat_axis=1,
            tiled=True,
        ),
    )
    grad_proj = jnp.concatenate(
        [grad_query_tok * jnp.bfloat16(scale), grad_key_tok, grad_value_tok], axis=1
    )
    through_proj = jnp.einsum("tc,nc->tn", grad_proj, qkv_full, preferred_element_type=jnp.float32)
    input_grad = grad_resid_one + through_proj
    grad_proj_float = grad_proj.astype(jnp.float32)
    vec_term = jnp.stack(
        [
            grad_gain_one,
            grad_gain_two,
            grad_shift_one,
            grad_shift_two,
            jnp.sum(grad_proj_float[:, :model_width], axis=0),
            jnp.sum(grad_proj_float[:, 2 * model_width :], axis=0),
            jnp.sum(grad_attn.astype(jnp.float32), axis=0),
            jnp.sum(grad_ffn.astype(jnp.float32), axis=0),
        ],
        axis=1,
    )
    bias_term = jnp.sum(grad_pre_all.astype(jnp.float32), axis=0).reshape(model_width, -1)
    bias_cols = bias_term.shape[1]
    padding = jnp.zeros((model_width, 128 - 8 - bias_cols), jnp.float32)
    extra_cols = jnp.concatenate([vec_term, bias_term, padding], axis=1)
    rows_dev = hidden_units // lax.axis_size(("seq", "head", "blk"))
    ffn_block = ffn_part((middle_low, grad_pre_all, act_part, grad_ffn))
    attn_block = attn_part((tokens, grad_proj, context, grad_attn), extra_cols)
    merged = lax.psum_scatter(
        jnp.concatenate(
            [ffn_block, attn_block.reshape(lax.axis_size(("seq", "head", "blk")) * rows_dev, -1)],
            axis=1,
        ),
        ("seq", "head", "blk"),
        scatter_dimension=0,
        tiled=True,
    )
    grad_fc_in = merged[:, :model_width]
    grad_fc_out = merged[:, model_width : 2 * model_width]
    attn_grad = merged[:, 2 * model_width :].reshape(rows_dev // ratio, 4 * model_width + 128)
    grad_w_qkv = attn_grad[:, : 3 * model_width]
    grad_w_out = attn_grad[:, 3 * model_width : 4 * model_width]
    grad_vectors = attn_grad[:, 4 * model_width : 4 * model_width + 8]
    grad_fc_in_bias = attn_grad[:, 4 * model_width + 8 : 4 * model_width + 8 + bias_cols].reshape(
        -1
    )
    return (
        layer_output,
        input_grad,
        grad_w_qkv,
        grad_w_out,
        grad_fc_in,
        grad_fc_out,
        grad_fc_in_bias,
        grad_vectors,
    )


GROUP = ("head", "blk")
FLIP = ((0, 1), (1, 0))
PAIRS = ((0, 1), (1, 0), (2, 3), (3, 2))
INNER = ((1, 2), (2, 1))
OUTER = ((1, 0), (2, 3))
INWARD = ((0, 1), (3, 2))
CORE = tuple((at, at ^ 1) for at in range(4))
ACROSS = tuple((at, at ^ 2) for at in range(4))


def group_rank():
    return lax.axis_index("head") * 4 + lax.axis_index("blk")


def inner_blk():
    at = lax.axis_index("blk")
    return (at == 1) | (at == 2)


def gather_blk(own):
    first = lax.ppermute(own, "blk", PAIRS)
    middle = lax.ppermute(own, "blk", INNER)
    second_in = lax.ppermute(first, "blk", INNER)
    second_out = lax.ppermute(middle, "blk", OUTER)
    third = lax.ppermute(second_in, "blk", OUTER)
    inner = inner_blk()
    return [own, first, jnp.where(inner, second_in, second_out), jnp.where(inner, middle, third)]


def gather_group(own):
    slots = gather_blk(own)
    slots = slots + [lax.ppermute(slot, "head", FLIP) for slot in slots]
    rank = group_rank()
    whole = jnp.zeros((8,) + own.shape, own.dtype)
    for at, slot in enumerate(slots):
        whole = lax.dynamic_update_slice_in_dim(whole, slot[None], rank ^ at, 0)
    return whole


def scatter_group(terms):
    row, at = lax.axis_index("head"), lax.axis_index("blk")
    away = lax.dynamic_slice_in_dim(terms, (1 - row) * 4, 4, 0).astype(jnp.bfloat16)
    near = lax.dynamic_slice_in_dim(terms, row * 4, 4, 0)
    near = near.astype(jnp.float32) + lax.ppermute(away, "head", FLIP).astype(jnp.float32)
    slots = [lax.dynamic_index_in_dim(near, at ^ k, 0, keepdims=False) for k in range(4)]
    inner = inner_blk()
    low = jnp.bfloat16
    from_three = lax.ppermute(slots[3].astype(low), "blk", INWARD).astype(jnp.float32)
    from_two = lax.ppermute(slots[2].astype(low), "blk", INWARD).astype(jnp.float32)
    second = slots[2] + from_three
    third = slots[3] + from_two
    to_first = lax.ppermute(second.astype(low), "blk", INNER).astype(jnp.float32)
    to_own = lax.ppermute(third.astype(low), "blk", INNER).astype(jnp.float32)
    first = slots[1] + to_first
    return slots[0] + lax.ppermute(first.astype(low), "blk", PAIRS).astype(jnp.float32) + to_own


def gather_seq(own):
    across = lax.ppermute(own, "seq", ACROSS)
    return [own, lax.ppermute(own, "seq", CORE), across, lax.ppermute(across, "seq", CORE)]


def scatter_seq(terms):
    low = jnp.bfloat16
    sent = lax.ppermute(jnp.stack([terms[1].astype(low), terms[3].astype(low)]), "seq", CORE)
    near = terms[0].astype(jnp.float32) + sent[0].astype(jnp.float32)
    far = terms[2].astype(jnp.float32) + sent[1].astype(jnp.float32)
    return near + lax.ppermute(far.astype(low), "seq", ACROSS).astype(jnp.float32)


def put_slots(slots, rank):
    whole = jnp.zeros((len(slots),) + slots[0].shape, slots[0].dtype)
    for at, slot in enumerate(slots):
        whole = lax.dynamic_update_slice_in_dim(whole, slot[None], rank ^ at, 0)
    return whole


ROWS_DIMS = (((1,), (1,)), ((), ()))
COLS_DIMS = (((0,), (0,)), ((), ()))


def attend_kernel(q_ref, k_ref, v_ref, mixed_ref, weights_ref, inverse_ref):
    for at in range(q_ref.shape[1] // HEAD_DIM):
        cols = slice(at * HEAD_DIM, (at + 1) * HEAD_DIM)
        scores = lax.dot_general(
            q_ref[:, cols], k_ref[:, cols], ROWS_DIMS, preferred_element_type=jnp.float32
        )
        weights = jnp.exp(scores - jnp.max(scores, axis=-1, keepdims=True))
        inverse = 1.0 / jnp.sum(weights, axis=-1, keepdims=True)
        weights = weights.astype(jnp.bfloat16)
        weights_ref[at] = weights
        mixed_ref[:, cols] = (
            jnp.dot(weights, v_ref[:, cols], preferred_element_type=jnp.float32) * inverse
        )
        inverse_ref[:, cols] = jnp.broadcast_to(inverse, (inverse.shape[0], HEAD_DIM))


def attend(queries, keys, values):
    rows, width = queries.shape
    heads = width // HEAD_DIM
    block = 256
    return pl.pallas_call(
        attend_kernel,
        grid=(rows // block,),
        in_specs=[
            pl.BlockSpec((block, width), lambda i: (i, 0)),
            pl.BlockSpec((rows, width), lambda i: (0, 0)),
            pl.BlockSpec((rows, width), lambda i: (0, 0)),
        ],
        out_specs=[
            pl.BlockSpec((block, width), lambda i: (i, 0)),
            pl.BlockSpec((heads, block, rows), lambda i: (0, i, 0)),
            pl.BlockSpec((block, width), lambda i: (i, 0)),
        ],
        out_shape=[
            jax.ShapeDtypeStruct((rows, width), jnp.float32),
            jax.ShapeDtypeStruct((heads, rows, rows), jnp.bfloat16),
            jax.ShapeDtypeStruct((rows, width), jnp.float32),
        ],
        compiler_params=pltpu.CompilerParams(vmem_limit_bytes=32 * 2**20),
        cost_estimate=pl.CostEstimate(
            flops=4 * rows * rows * width,
            bytes_accessed=heads * rows * rows * 2 + 8 * rows * width * 2,
            transcendentals=heads * rows * rows,
        ),
    )(queries, keys, values)


def attend_back_kernel(
    grad_ref, mixed_ref, inverse_ref, q_ref, weights_ref, k_ref, v_ref,
    dq_ref, dk_ref, dv_ref, dk_sum, dv_sum,
):
    step = pl.program_id(0)

    @pl.when(step == 0)
    def _():
        dk_sum[...] = jnp.zeros_like(dk_sum)
        dv_sum[...] = jnp.zeros_like(dv_sum)

    for at in range(q_ref.shape[1] // HEAD_DIM):
        cols = slice(at * HEAD_DIM, (at + 1) * HEAD_DIM)
        grad = grad_ref[:, cols]
        inverse = inverse_ref[:, cols]
        delta = jnp.sum(grad.astype(jnp.float32) * mixed_ref[:, cols], axis=-1, keepdims=True)
        weights = weights_ref[at]
        dprobs = lax.dot_general(
            grad, v_ref[:, cols], ROWS_DIMS, preferred_element_type=jnp.float32
        )
        dscores = (weights.astype(jnp.float32) * (dprobs - delta)).astype(jnp.bfloat16)
        dq = jnp.dot(dscores, k_ref[:, cols], preferred_element_type=jnp.float32) * inverse
        dq_ref[:, cols] = dq.astype(jnp.bfloat16)
        q_scaled = (q_ref[:, cols].astype(jnp.float32) * inverse).astype(jnp.bfloat16)
        dk_sum[:, cols] += lax.dot_general(
            dscores, q_scaled, COLS_DIMS, preferred_element_type=jnp.float32
        )
        g_scaled = (grad.astype(jnp.float32) * inverse).astype(jnp.bfloat16)
        dv_sum[:, cols] += lax.dot_general(
            weights, g_scaled, COLS_DIMS, preferred_element_type=jnp.float32
        )

    @pl.when(step == pl.num_programs(0) - 1)
    def _():
        dk_ref[...] = dk_sum[...].astype(jnp.bfloat16)
        dv_ref[...] = dv_sum[...].astype(jnp.bfloat16)


def attend_back(grad, mixed, inverse, queries, weights, keys, values):
    rows, width = queries.shape
    heads = width // HEAD_DIM
    block = 256
    per_block = pl.BlockSpec((block, width), lambda i: (i, 0))
    whole = pl.BlockSpec((rows, width), lambda i: (0, 0))
    return pl.pallas_call(
        attend_back_kernel,
        grid=(rows // block,),
        in_specs=[
            per_block, per_block, per_block, per_block,
            pl.BlockSpec((heads, block, rows), lambda i: (0, i, 0)),
            whole, whole,
        ],
        out_specs=[per_block, whole, whole],
        out_shape=[jax.ShapeDtypeStruct((rows, width), jnp.bfloat16)] * 3,
        scratch_shapes=[pltpu.VMEM((rows, width), jnp.float32)] * 2,
        compiler_params=pltpu.CompilerParams(vmem_limit_bytes=32 * 2**20),
        cost_estimate=pl.CostEstimate(
            flops=8 * rows * rows * width,
            bytes_accessed=heads * rows * rows * 2 + 12 * rows * width * 2,
            transcendentals=0,
        ),
    )(grad, mixed, inverse, queries, weights, keys, values)


def normalize(values):
    center = values - jnp.mean(values, axis=-1, keepdims=True)
    scale = lax.rsqrt(jnp.mean(center * center, axis=-1, keepdims=True) + 1e-05)
    return center * scale, scale


def normalize_back(cotangent, gain, normed, scale):
    dn = cotangent * gain
    inner = jnp.mean(dn, axis=-1, keepdims=True)
    outer = jnp.mean(dn * normed, axis=-1, keepdims=True)
    return scale * (dn - inner - normed * outer)


def dot_rows(left, right):
    return lax.dot_general(left, right, ROWS_DIMS, preferred_element_type=jnp.float32)


def dot_cols(left, right):
    return lax.dot_general(left, right, COLS_DIMS, preferred_element_type=jnp.float32)


def dot(left, right):
    return jnp.dot(left, right, preferred_element_type=jnp.float32)


def grouped_body(tokens, out_grad, w_qkv, w_out, fc_in, fc_out, fc_in_bias, vectors):
    rows, width = tokens.shape
    low = jnp.bfloat16
    scale = HEAD_DIM ** (-0.5)
    seq_at = lax.axis_index("seq")
    core_at = lax.rem(seq_at, 2)
    rank = group_rank()
    own = width // 8

    quarter = own // 4
    qkv_rows = lax.dynamic_slice_in_dim(w_qkv, seq_at * quarter, quarter, 0)
    qkv_rows = qkv_rows.reshape(quarter, 3, 8, own).transpose(2, 0, 1, 3).reshape(8, quarter * 3, own)
    small = jnp.concatenate([vectors.T, fc_in_bias.reshape(-1, own)], axis=0)
    small = jnp.broadcast_to(small[None], (8,) + small.shape)
    swapped = lax.all_to_all(jnp.concatenate([qkv_rows, small], axis=1), GROUP, 0, 0, tiled=True)
    vec = swapped[:, quarter * 3 : quarter * 3 + 8].transpose(1, 0, 2).reshape(8, width).astype(jnp.float32)
    bias_all = swapped[:, quarter * 3 + 8 :]
    gain_one, gain_two, shift_one, shift_two = (vec[at] for at in range(4))
    bias_output, bias_ffn = vec[6], vec[7]
    bias_query, bias_value = (vectors[:, at].astype(jnp.float32) for at in (4, 5))
    qkv_parts = put_slots(gather_seq(swapped[:, : quarter * 3]), seq_at)
    qkv_cols = qkv_parts.reshape(4, 8, quarter, 3 * own).transpose(1, 0, 2, 3).reshape(width, 3 * own)

    seq_tokens = gather_group(tokens).reshape(8 * rows, width)

    out_half = gather_group(lax.dynamic_slice_in_dim(w_out, core_at * (own // 2), own // 2, 0))
    out_parts = jnp.zeros((2,) + out_half.shape, low)
    out_parts = lax.dynamic_update_slice_in_dim(out_parts, out_half[None], core_at, 0)
    out_parts = lax.dynamic_update_slice_in_dim(
        out_parts, lax.ppermute(out_half, "seq", CORE)[None], 1 - core_at, 0
    )
    out_full = out_parts.transpose(1, 0, 2, 3).reshape(width, width)

    unit_rows = fc_in.shape[0] // 4
    ffn_own = jnp.stack(
        [
            lax.dynamic_slice_in_dim(fc_in, seq_at * unit_rows, unit_rows, 0),
            lax.dynamic_slice_in_dim(fc_out, seq_at * unit_rows, unit_rows, 0),
        ]
    )
    ffn_weights = gather_group(ffn_own)
    units = 8 * unit_rows
    ffn_in = ffn_weights[:, 0].reshape(units, width)
    ffn_out = ffn_weights[:, 1].reshape(units, width)
    ffn_bias = lax.dynamic_index_in_dim(bias_all, seq_at, 1, keepdims=False).reshape(units).astype(jnp.float32)

    projected = dot(seq_tokens, qkv_cols)
    queries = ((projected[:, :own] + bias_query) * scale).astype(low)
    keys = projected[:, own : 2 * own].astype(low)
    values = (projected[:, 2 * own :] + bias_value).astype(low)
    mixed, weights, inverse = attend(queries, keys, values)
    context = lax.all_to_all(mixed.astype(low).reshape(8, rows, own), GROUP, 0, 0, tiled=True)
    context = context.transpose(1, 0, 2).reshape(rows, width)

    attn_out = dot(context, out_full) + bias_output
    norm_one, scale_one = normalize(tokens.astype(jnp.float32) + attn_out)
    middle = norm_one * gain_one + shift_one
    middle_all = jnp.concatenate(gather_seq(middle.astype(low)), axis=0)
    pre_act = dot_rows(middle_all, ffn_in) + ffn_bias
    cdf = 0.5 * (1.0 + lax.erf(pre_act * (0.5**0.5)))
    act = (pre_act * cdf).astype(low)
    slope = cdf + pre_act * jnp.exp(-0.5 * pre_act * pre_act) * ((2.0 * math.pi) ** -0.5)
    summed = scatter_seq(dot(act, ffn_out).reshape(4, rows, width))
    norm_two, scale_two = normalize(middle + summed + bias_ffn)
    layer_output = norm_two * gain_two + shift_two

    cotangent = out_grad.astype(jnp.float32)
    grad_two = normalize_back(cotangent, gain_two, norm_two, scale_two)
    grad_ffn = grad_two.astype(low)
    grad_ffn_all = jnp.concatenate(gather_seq(grad_ffn), axis=0)
    grad_pre_float = dot_rows(grad_ffn_all, ffn_out) * slope
    grad_pre = grad_pre_float.astype(low)
    grad_mid = grad_two + scatter_seq(dot(grad_pre, ffn_in).reshape(4, rows, width))
    grad_one = normalize_back(grad_mid, gain_one, norm_one, scale_one)
    grad_attn = grad_one.astype(low)
    grad_context = dot_rows(grad_attn, out_full).astype(low)
    grad_context = lax.all_to_all(
        grad_context.reshape(rows, 8, own).transpose(1, 0, 2), GROUP, 0, 0, tiled=True
    ).reshape(8 * rows, own)
    dq, dk, dv = attend_back(grad_context, mixed, inverse, queries, weights, keys, values)
    grad_cols = jnp.concatenate([dq * low(scale), dk, dv], axis=1)
    grad_proj = lax.all_to_all(grad_cols.reshape(8, rows, 3 * own), GROUP, 0, 0, tiled=True)
    grad_proj = grad_proj.reshape(8, rows, 3, own).transpose(1, 2, 0, 3).reshape(rows, 3 * width)

    qkv_quarter = gather_group(lax.dynamic_slice_in_dim(w_qkv, seq_at * quarter, quarter, 0))
    qkv_full = put_slots(gather_seq(qkv_quarter), seq_at)
    qkv_full = qkv_full.transpose(1, 0, 2, 3).reshape(width, 3 * width)
    input_grad = grad_one + dot_rows(grad_proj, qkv_full)

    ffn_terms = jnp.stack(
        [
            dot_cols(grad_pre, middle_all).reshape(8, unit_rows, width),
            dot_cols(act, grad_ffn_all).reshape(8, unit_rows, width),
        ],
        axis=1,
    )
    ffn_grads = scatter_group(ffn_terms).astype(low)
    moves = []
    for seq_from in range(4):
        for rank_from in range(8):
            moves.append((seq_from * 8 + rank_from, rank_from * 4 + seq_from))
    ffn_grads = lax.ppermute(ffn_grads, ("seq", "head", "blk"), moves).astype(jnp.float32)

    context_parts = context.reshape(rows, 4, width // 4)
    parts = [lax.dynamic_index_in_dim(context_parts, seq_at ^ at, 1, keepdims=False) for at in range(4)]
    parts = [
        parts[0],
        lax.ppermute(parts[1], "seq", CORE),
        lax.ppermute(parts[2], "seq", ACROSS),
        lax.ppermute(parts[3], "seq", tuple((at, at ^ 3) for at in range(4))),
    ]
    grad_attn_all = jnp.concatenate(gather_seq(grad_attn), axis=0)
    out_terms = dot_cols(jnp.concatenate(parts, axis=0), grad_attn_all)
    grad_w_out = scatter_group(out_terms.reshape(8, quarter, width))

    qkv_terms = dot_cols(seq_tokens, grad_cols).reshape(32, quarter * 3, own)
    grad_cols_sum = jnp.sum(grad_cols.astype(jnp.float32), axis=0).reshape(3, own)
    col_sums = lax.dynamic_update_slice(
        jnp.zeros((2, width), jnp.float32),
        jnp.stack([grad_cols_sum[0], grad_cols_sum[2]]),
        (0, rank * own),
    )
    token_sums = jnp.stack(
        [
            jnp.sum(grad_mid * norm_one, axis=0),
            jnp.sum(cotangent * norm_two, axis=0),
            jnp.sum(grad_mid, axis=0),
            jnp.sum(cotangent, axis=0),
            col_sums[0],
            col_sums[1],
            jnp.sum(grad_attn.astype(jnp.float32), axis=0),
            jnp.sum(grad_ffn.astype(jnp.float32), axis=0),
        ]
    )
    token_sums = token_sums.reshape(8, 32, quarter).transpose(1, 0, 2).reshape(32, -1, own)
    unit_sums = jnp.sum(grad_pre.astype(jnp.float32), axis=0).reshape(8, 1, unit_rows)
    unit_sums = lax.dynamic_update_slice(
        jnp.zeros((8, 4, unit_rows), jnp.float32), unit_sums, (0, seq_at, 0)
    ).reshape(32, 1, unit_rows)
    payload = jnp.concatenate([qkv_terms, token_sums, unit_sums], axis=1).reshape(4, 8, -1, own)
    payload = scatter_seq([lax.dynamic_index_in_dim(payload, seq_at ^ at, 0, keepdims=False) for at in range(4)])
    payload = lax.all_to_all(payload.astype(low), GROUP, 0, 0, tiled=True).astype(jnp.float32)
    grad_w_qkv = payload[:, : quarter * 3].reshape(8, quarter, 3, own).transpose(1, 2, 0, 3).reshape(quarter, -1)
    sums = jnp.sum(payload[:, quarter * 3 :], axis=0)
    grad_vectors = sums[:2].reshape(8, quarter).T
    grad_bias = sums[2]
    return (
        layer_output,
        input_grad,
        grad_w_qkv,
        grad_w_out,
        ffn_grads[0],
        ffn_grads[1],
        grad_bias,
        grad_vectors,
    )


def solution(mesh):
    sizes = tuple(mesh.shape[name] for name in ("seq", "head", "blk"))
    return jax.shard_map(
        grouped_body if sizes == (4, 2, 4) else general_body,
        mesh=mesh,
        in_specs=(
            P(("seq", "head", "blk"), None),
            P(("seq", "head", "blk"), None),
            P(("head", "blk"), None),
            P(("head", "blk"), None),
            P(("head", "blk"), None),
            P(("head", "blk"), None),
            P(("head", "blk")),
            P(("head", "blk"), None),
        ),
        out_specs=(
            P(("seq", "head", "blk"), None),
            P(("seq", "head", "blk"), None),
            P(("seq", "head", "blk"), None),
            P(("seq", "head", "blk"), None),
            P(("seq", "head", "blk"), None),
            P(("seq", "head", "blk"), None),
            P(("seq", "head", "blk")),
            P(("seq", "head", "blk"), None),
        ),
        check_vma=False,
    )
```

```python
import math

import jax
import jax.numpy as jnp
from jax import lax
from jax.experimental import pallas as pl
from jax.experimental.pallas import tpu as pltpu
from jax.sharding import PartitionSpec as P

HEAD_DIM = 64


def layer_norm(values, gain_vec, shift_vec):
    center = values - jnp.mean(values, axis=-1, keepdims=True)
    spread = jnp.mean(center * center, axis=-1, keepdims=True)
    return center * lax.rsqrt(spread + 1e-05) * gain_vec + shift_vec


def gelu_exact(values):
    return jax.nn.gelu(values, approximate=False)


def split_heads(values):
    return values.reshape(values.shape[0], values.shape[1] // HEAD_DIM, HEAD_DIM)


def head_scores(left_rows, right_rows):
    return jnp.einsum("qhd,khd->hqk", left_rows, right_rows, preferred_element_type=jnp.float32)


def ffn_part(factors):
    middle_low, grad_pre_full, act_full, grad_ffn = factors
    return jnp.concatenate(
        [
            jnp.einsum("tf,td->fd", grad_pre_full, middle_low, preferred_element_type=jnp.float32),
            jnp.einsum("tf,td->fd", act_full, grad_ffn, preferred_element_type=jnp.float32),
        ],
        axis=1,
    )


def attn_part(factors, extra_cols):
    tokens, grad_proj, context, grad_attn = factors
    return jnp.concatenate(
        [
            jnp.einsum("tn,tc->nc", tokens, grad_proj, preferred_element_type=jnp.float32),
            jnp.einsum("tn,tc->nc", context, grad_attn, preferred_element_type=jnp.float32),
            extra_cols,
        ],
        axis=1,
    )


def general_body(tokens, out_grad, w_qkv, w_out, fc_in, fc_out, fc_in_bias, vectors):
    model_width = tokens.shape[1]
    hidden_units = fc_in.shape[0] * lax.axis_size(("head", "blk"))
    ratio = hidden_units // model_width
    scale = HEAD_DIM ** (-0.5)
    part_qkv = lax.all_gather(w_qkv, ("head", "blk"), axis=0, tiled=True)
    part_out = lax.all_gather(w_out, ("head", "blk"), axis=0, tiled=True)
    part_vec = lax.all_gather(vectors, ("head", "blk"), axis=0, tiled=True)
    part_rows = part_qkv.shape[0]
    projected = jnp.dot(tokens, part_qkv, preferred_element_type=jnp.float32)
    out_full = part_out
    attn_state = (projected, out_full, part_vec)
    projected = attn_state[0]
    out_full = attn_state[1]
    vec_float = attn_state[2].astype(jnp.float32)
    gain_one, gain_two = (vec_float[:, 0], vec_float[:, 1])
    shift_one, shift_two = (vec_float[:, 2], vec_float[:, 3])
    bias_query, bias_value = (vec_float[:, 4], vec_float[:, 5])
    bias_output, bias_ffn = (vec_float[:, 6], vec_float[:, 7])
    queries = ((projected[:, :model_width] + bias_query) * scale).astype(jnp.bfloat16)
    key_rows = projected[:, model_width : 2 * model_width].astype(jnp.bfloat16)
    value_rows = (projected[:, 2 * model_width :] + bias_value).astype(jnp.bfloat16)
    query_heads, key_heads, value_heads = (
        lax.all_to_all(queries, "head", split_axis=1, concat_axis=0, tiled=True),
        lax.all_to_all(key_rows, "head", split_axis=1, concat_axis=0, tiled=True),
        lax.all_to_all(value_rows, "head", split_axis=1, concat_axis=0, tiled=True),
    )
    query_split = split_heads(query_heads)
    group_rows = query_split.shape[0]
    group_width = key_heads.shape[1]
    seq_rows = group_rows * lax.axis_size("blk")
    portion = (
        lax.all_gather(key_heads, "blk", axis=0, tiled=True),
        lax.all_gather(value_heads, "blk", axis=0, tiled=True),
    )
    scores = head_scores(query_split, split_heads(portion[0]))
    run_sum = jnp.sum(jnp.exp(scores), axis=-1)
    key_all = portion[0]
    value_all = portion[1]
    run_sum, key_all, value_all = (run_sum, key_all, value_all)
    log_total = jnp.log(run_sum)
    block_rows = math.gcd(512, seq_rows)
    block_count = seq_rows // block_rows
    key_blocks = key_all.reshape(block_count, block_rows, group_width)
    value_blocks = value_all.reshape(block_count, block_rows, group_width)

    def mix_block(totals, pair):
        scores = head_scores(query_split, split_heads(pair[0]))
        probs_low = jnp.exp(scores - log_total[:, :, None]).astype(jnp.bfloat16)
        return (
            totals
            + jnp.einsum(
                "hqk,khd->qhd", probs_low, split_heads(pair[1]), preferred_element_type=jnp.float32
            ),
            None,
        )

    mixed, unused = lax.scan(
        mix_block, jnp.zeros(query_split.shape, jnp.float32), (key_blocks, value_blocks)
    )
    context = lax.all_to_all(
        mixed.reshape(group_rows, -1).astype(jnp.bfloat16),
        "head",
        split_axis=0,
        concat_axis=1,
        tiled=True,
    )
    attn_out = jnp.dot(context, out_full, preferred_element_type=jnp.float32) + bias_output
    residual_one = tokens.astype(jnp.float32) + attn_out
    middle, norm_one_back = jax.vjp(layer_norm, residual_one, gain_one, shift_one)
    middle_low = middle.astype(jnp.bfloat16)
    part_in = lax.all_gather(fc_in, ("head", "blk"), axis=0, tiled=True)
    part_out = lax.all_gather(fc_out, ("head", "blk"), axis=0, tiled=True)
    part_bias = lax.all_gather(fc_in_bias, ("head", "blk"), axis=0, tiled=True)
    pre_part = jnp.einsum("td,fd->tf", middle_low, part_in, preferred_element_type=jnp.float32)
    pre_part = pre_part + part_bias.astype(jnp.float32)
    act_part = gelu_exact(pre_part).astype(jnp.bfloat16)
    summed = jnp.dot(act_part, part_out, preferred_element_type=jnp.float32)
    ffn_pre_full = pre_part
    residual_two = middle + summed + bias_ffn
    layer_output, norm_two_back = jax.vjp(layer_norm, residual_two, gain_two, shift_two)
    grad_resid_two, grad_gain_two, grad_shift_two = norm_two_back(out_grad.astype(jnp.float32))
    grad_ffn = grad_resid_two.astype(jnp.bfloat16)
    qkv_flat = w_qkv.reshape(fc_in.shape[0], -1)
    portion = (
        lax.all_gather(fc_in, ("head", "blk"), axis=0, tiled=True),
        lax.all_gather(fc_out, ("head", "blk"), axis=0, tiled=True),
        lax.all_gather(qkv_flat, ("head", "blk"), axis=0, tiled=True),
    )
    part_in = portion[0]
    part_rows = part_in.shape[0]
    pre_part = ffn_pre_full
    grad_act = jnp.einsum("td,fd->tf", grad_ffn, portion[1], preferred_element_type=jnp.float32)
    grad_pre = jax.vjp(gelu_exact, pre_part)[1](grad_act)[0].astype(jnp.bfloat16)
    grad_mid = jnp.dot(grad_pre, part_in, preferred_element_type=jnp.float32)
    grad_mid, grad_pre_all = (grad_mid, grad_pre)
    qkv_gathered = portion[2]
    qkv_full = qkv_gathered.reshape(model_width, 3 * model_width)
    grad_resid_one, grad_gain_one, grad_shift_one = norm_one_back(grad_resid_two + grad_mid)
    grad_attn = grad_resid_one.astype(jnp.bfloat16)
    grad_context = jnp.einsum(
        "td,ed->te", grad_attn, out_full, preferred_element_type=jnp.float32
    ).astype(jnp.bfloat16)
    grad_ctx_heads = lax.all_to_all(grad_context, "head", split_axis=1, concat_axis=0, tiled=True)
    grad_ctx_split = split_heads(grad_ctx_heads)
    delta_heads = jnp.sum(grad_ctx_split.astype(jnp.float32) * mixed, axis=-1).T

    def back_block(grad_query, pair):
        key_part = split_heads(pair[0])
        value_part = split_heads(pair[1])
        scores = head_scores(query_split, key_part)
        probs = jnp.exp(scores - log_total[:, :, None])
        dprobs = head_scores(grad_ctx_split, value_part)
        dscores = (probs * (dprobs - delta_heads[:, :, None])).astype(jnp.bfloat16)
        grad_query = grad_query + jnp.einsum(
            "hqk,khd->qhd", dscores, key_part, preferred_element_type=jnp.float32
        )
        grad_key = jnp.einsum(
            "hqk,qhd->khd", dscores, query_split, preferred_element_type=jnp.float32
        )
        grad_value = jnp.einsum(
            "hqk,qhd->khd",
            probs.astype(jnp.bfloat16),
            grad_ctx_split,
            preferred_element_type=jnp.float32,
        )
        part_rows = pair[0].shape[0]
        return (
            grad_query,
            jnp.concatenate(
                [grad_key.reshape(part_rows, -1), grad_value.reshape(part_rows, -1)], axis=1
            ),
        )

    grad_query_heads, kv_terms = lax.scan(
        back_block, jnp.zeros(query_split.shape, jnp.float32), (key_blocks, value_blocks)
    )
    kv_own = lax.psum_scatter(
        kv_terms.reshape(seq_rows, 2 * group_width).astype(jnp.bfloat16),
        "blk",
        scatter_dimension=0,
        tiled=True,
    ).astype(jnp.float32)
    grad_query_tok, grad_key_tok, grad_value_tok = (
        lax.all_to_all(
            grad_query_heads.reshape(group_rows, -1).astype(jnp.bfloat16),
            "head",
            split_axis=0,
            concat_axis=1,
            tiled=True,
        ),
        lax.all_to_all(
            kv_own[:, :group_width].astype(jnp.bfloat16),
            "head",
            split_axis=0,
            concat_axis=1,
            tiled=True,
        ),
        lax.all_to_all(
            kv_own[:, group_width:].astype(jnp.bfloat16),
            "head",
            split_axis=0,
            concat_axis=1,
            tiled=True,
        ),
    )
    grad_proj = jnp.concatenate(
        [grad_query_tok * jnp.bfloat16(scale), grad_key_tok, grad_value_tok], axis=1
    )
    through_proj = jnp.einsum("tc,nc->tn", grad_proj, qkv_full, preferred_element_type=jnp.float32)
    input_grad = grad_resid_one + through_proj
    grad_proj_float = grad_proj.astype(jnp.float32)
    vec_term = jnp.stack(
        [
            grad_gain_one,
            grad_gain_two,
            grad_shift_one,
            grad_shift_two,
            jnp.sum(grad_proj_float[:, :model_width], axis=0),
            jnp.sum(grad_proj_float[:, 2 * model_width :], axis=0),
            jnp.sum(grad_attn.astype(jnp.float32), axis=0),
            jnp.sum(grad_ffn.astype(jnp.float32), axis=0),
        ],
        axis=1,
    )
    bias_term = jnp.sum(grad_pre_all.astype(jnp.float32), axis=0).reshape(model_width, -1)
    bias_cols = bias_term.shape[1]
    padding = jnp.zeros((model_width, 128 - 8 - bias_cols), jnp.float32)
    extra_cols = jnp.concatenate([vec_term, bias_term, padding], axis=1)
    rows_dev = hidden_units // lax.axis_size(("seq", "head", "blk"))
    ffn_block = ffn_part((middle_low, grad_pre_all, act_part, grad_ffn))
    attn_block = attn_part((tokens, grad_proj, context, grad_attn), extra_cols)
    merged = lax.psum_scatter(
        jnp.concatenate(
            [ffn_block, attn_block.reshape(lax.axis_size(("seq", "head", "blk")) * rows_dev, -1)],
            axis=1,
        ),
        ("seq", "head", "blk"),
        scatter_dimension=0,
        tiled=True,
    )
    grad_fc_in = merged[:, :model_width]
    grad_fc_out = merged[:, model_width : 2 * model_width]
    attn_grad = merged[:, 2 * model_width :].reshape(rows_dev // ratio, 4 * model_width + 128)
    grad_w_qkv = attn_grad[:, : 3 * model_width]
    grad_w_out = attn_grad[:, 3 * model_width : 4 * model_width]
    grad_vectors = attn_grad[:, 4 * model_width : 4 * model_width + 8]
    grad_fc_in_bias = attn_grad[:, 4 * model_width + 8 : 4 * model_width + 8 + bias_cols].reshape(
        -1
    )
    return (
        layer_output,
        input_grad,
        grad_w_qkv,
        grad_w_out,
        grad_fc_in,
        grad_fc_out,
        grad_fc_in_bias,
        grad_vectors,
    )


GROUP = ("head", "blk")
FLIP = ((0, 1), (1, 0))
PAIRS = ((0, 1), (1, 0), (2, 3), (3, 2))
INNER = ((1, 2), (2, 1))
OUTER = ((1, 0), (2, 3))
INWARD = ((0, 1), (3, 2))
TWO_ON = ((0, 2), (2, 0), (1, 3), (3, 1))
CORE = tuple((at, at ^ 1) for at in range(4))
ACROSS = tuple((at, at ^ 2) for at in range(4))
LOW = jnp.bfloat16
FULL = jnp.float32
ROWS_DIMS = (((1,), (1,)), ((), ()))
COLS_DIMS = (((0,), (0,)), ((), ()))


def dot(left, right):
    return jnp.dot(left, right, preferred_element_type=FULL)


def dot_rows(left, right):
    return lax.dot_general(left, right, ROWS_DIMS, preferred_element_type=FULL)


def dot_cols(left, right):
    return lax.dot_general(left, right, COLS_DIMS, preferred_element_type=FULL)


def after(values, *others):
    if not isinstance(values, (list, tuple)):
        return lax.optimization_barrier((values,) + others)[0]
    return lax.optimization_barrier(tuple(values) + others)[: len(values)]


def inner_blk():
    at = lax.axis_index("blk")
    return (at == 1) | (at == 2)


def flip_head(value):
    return lax.ppermute(value, "head", FLIP)


def scatter_group(near, away):
    across_3 = flip_head(away[3])
    third = near[3] + across_3.astype(FULL)
    away_2 = after(away[2], across_3)
    ends_third = lax.ppermute(third.astype(LOW), "blk", INWARD)
    across_2 = flip_head(away_2)
    second = near[2] + across_2.astype(FULL) + ends_third.astype(FULL)
    second_low, away_1 = after((second.astype(LOW), away[1]), across_2)
    ends_second = lax.ppermute(second_low, "blk", INWARD)
    inner_second = lax.ppermute(second_low, "blk", INNER)
    across_1 = flip_head(away_1)
    third = third + ends_second.astype(FULL)
    first = near[1] + across_1.astype(FULL) + inner_second.astype(FULL)
    third_low, first_low, away_0 = after((third.astype(LOW), first.astype(LOW), away[0]))
    inner_third = lax.ppermute(third_low, "blk", INNER)
    last = lax.ppermute(first_low, "blk", PAIRS)
    across_0 = flip_head(away_0)
    return [near[0], across_0, inner_third, last]


def gather_seq(own):
    across = lax.ppermute(own, "seq", ACROSS)
    return [own, lax.ppermute(own, "seq", CORE), across, lax.ppermute(across, "seq", CORE)]


def gather_four(own):
    across = flip_head(own)
    beside = lax.ppermute(own, "blk", PAIRS)
    return [own, beside, across, lax.ppermute(across, "blk", PAIRS)]


def gather_cores(own):
    across = flip_head(own)
    return [own, lax.ppermute(own, "seq", CORE), across, lax.ppermute(across, "seq", CORE)]


def shape_of(shape, dtype):
    return jax.ShapeDtypeStruct(shape, dtype)


def call(kernel, outs, place, *args, scratch=(), flops=0, vmem=28, far_in=0, far_out=0):
    moved = sum(arg.size * arg.dtype.itemsize for arg in args)
    moved += sum(math.prod(out.shape) * jnp.dtype(out.dtype).itemsize for out in outs)
    near = pl.BlockSpec(memory_space=pltpu.VMEM)
    far = pl.BlockSpec(memory_space=pltpu.HBM)
    return pl.pallas_call(
        kernel,
        out_shape=outs,
        in_specs=[pl.BlockSpec(memory_space=pltpu.SMEM)]
        + [near] * (len(args) - far_in)
        + [far] * far_in,
        out_specs=[near] * (len(outs) - far_out) + [far] * far_out,
        scratch_shapes=scratch,
        compiler_params=pltpu.CompilerParams(vmem_limit_bytes=vmem * 2**20),
        cost_estimate=pl.CostEstimate(flops=flops, bytes_accessed=moved, transcendentals=0),
    )(place, *args)


def fetch(sources, held, sems):
    copies = [pltpu.make_async_copy(*both, sems.at[at]) for at, both in enumerate(zip(sources, held))]
    for copy in copies:
        copy.start()
    return copies


def put_columns(core, own_half, other_half, cols_ref):
    half, own = own_half.shape[2:]
    for at in range(8):
        for side, half_ref in ((core, own_half), (1 - core, other_half)):
            span = pl.ds(pl.multiple_of((2 * at + side) * half, half), half)
            for which in range(3):
                cols_ref[span, which * own : (which + 1) * own] = half_ref[at, which]


def attend_kernel(place, *refs):
    slots, refs = refs[:8], refs[8:]
    own_half, other_half, bias_ref = refs[:3]
    context_ref, kept, refs = refs[3], refs[4:10], refs[10:]
    q_ref, k_ref, v_ref, mixed_ref, inverse_ref, weights_ref, cols_ref, sems = refs
    rank, core = place[0], place[2]
    half = own_half.shape[2]
    width = q_ref.shape[1]
    rows = slots[0].shape[0]
    put_columns(core, own_half, other_half, cols_ref)
    scale = HEAD_DIM ** (-0.5)
    for pair in range(4):
        span = slice(pair * 2 * rows, (pair + 1) * 2 * rows)
        both = jnp.concatenate([slots[2 * pair][...], slots[2 * pair + 1][...]], axis=0)
        projected = dot(both, cols_ref[...])
        q_ref[span] = ((projected[:, :width] + bias_ref[0]) * scale).astype(LOW)
        k_ref[span] = projected[:, width : 2 * width].astype(LOW)
        v_ref[span] = (projected[:, 2 * width :] + bias_ref[1]).astype(LOW)

    @pl.loop(0, 4)
    def _(pair):
        span = pl.ds(pl.multiple_of(pair * 2 * rows, 2 * rows), 2 * rows)
        for at in range(width // HEAD_DIM):
            cols = slice(at * HEAD_DIM, (at + 1) * HEAD_DIM)
            scores = dot_rows(q_ref[span, cols], k_ref[:, cols])
            weights = jnp.exp(scores - jnp.max(scores, axis=-1, keepdims=True))
            inverse = 1.0 / jnp.sum(weights, axis=-1, keepdims=True)
            weights = weights.astype(LOW)
            weights_ref[at, span] = weights
            mixed_ref[span, cols] = dot(weights, v_ref[:, cols]) * inverse
            inverse_ref[span, cols] = jnp.broadcast_to(inverse, (2 * rows, HEAD_DIM))
        first = lax.bitwise_xor(rank, 2 * pair)
        mixed = mixed_ref[span].astype(LOW)
        context_ref[first] = mixed[:rows]
        context_ref[lax.bitwise_xor(first, 1)] = mixed[rows:]
        pltpu.make_async_copy(
            weights_ref.at[:, span], kept[5].at[:, span], sems.at[pair]
        ).start()

    copies = []
    for at, ref in enumerate((q_ref, k_ref, v_ref, mixed_ref, inverse_ref)):
        copies.append(pltpu.make_async_copy(ref, kept[at], sems.at[4 + at]))
    for pair in range(4):
        span = slice(pair * 2 * rows, (pair + 1) * 2 * rows)
        copies.append(
            pltpu.make_async_copy(weights_ref.at[:, span], kept[5].at[:, span], sems.at[pair])
        )
    for copy in copies[:5]:
        copy.start()
    for copy in copies:
        copy.wait()


def attend_back_kernel(place, grad_ref, own_half, other_half, *refs):
    kept, refs = refs[:6], refs[6:]
    out_ref, near_ref, away_ref, cols_ref, refs = refs[0], refs[1], refs[2], refs[3], refs[4:]
    q_ref, k_ref, v_ref, mixed_ref, inverse_ref, weights_ref, dk_sum, dv_sum, sems = refs
    rank = place[0]
    rows, width = grad_ref.shape[1:]
    scale = HEAD_DIM ** (-0.5)
    copies = []
    for at, ref in enumerate((q_ref, k_ref, v_ref, mixed_ref, inverse_ref)):
        copies.append(pltpu.make_async_copy(kept[at], ref, sems.at[4 + at]))

    def block_copy(pair, span):
        return pltpu.make_async_copy(kept[5].at[:, span], weights_ref.at[:, span], sems.at[pair])

    for copy in copies:
        copy.start()
    for pair in range(4):
        block_copy(pair, slice(pair * 2 * rows, (pair + 1) * 2 * rows)).start()
    dk_sum[...] = jnp.zeros_like(dk_sum)
    dv_sum[...] = jnp.zeros_like(dv_sum)
    for copy in copies:
        copy.wait()

    @pl.loop(0, 4)
    def _(pair):
        span = pl.ds(pl.multiple_of(pair * 2 * rows, 2 * rows), 2 * rows)
        block_copy(pair, span).wait()
        first = lax.bitwise_xor(rank, 2 * pair)
        second = lax.bitwise_xor(first, 1)
        grad_all = jnp.concatenate([grad_ref[first], grad_ref[second]], axis=0)
        inverse = inverse_ref[span]
        q_scaled = (q_ref[span].astype(FULL) * inverse).astype(LOW)
        g_scaled = (grad_all.astype(FULL) * inverse).astype(LOW)
        product = grad_all.astype(FULL) * mixed_ref[span]
        for at in range(width // HEAD_DIM):
            cols = slice(at * HEAD_DIM, (at + 1) * HEAD_DIM)
            delta = jnp.sum(product[:, cols], axis=-1, keepdims=True)
            weights = weights_ref[at, span]
            dprobs = dot_rows(grad_all[:, cols], v_ref[:, cols])
            dscores = (weights.astype(FULL) * (dprobs - delta)).astype(LOW)
            dq = (dot(dscores, k_ref[:, cols]) * inverse[:, cols]).astype(LOW) * LOW(scale)
            out_ref[first, :, cols] = dq[:rows]
            out_ref[second, :, cols] = dq[rows:]
            dk_sum[cols] += dot_cols(q_scaled[:, cols], dscores)
            dv_sum[cols] += dot_cols(g_scaled[:, cols], weights)

    dk = dk_sum[...].T.astype(LOW)
    dv = dv_sum[...].T.astype(LOW)
    for at in range(8):
        whose = lax.bitwise_xor(rank, at)
        out_ref[whose, :, width : 2 * width] = dk[at * rows : (at + 1) * rows]
        out_ref[whose, :, 2 * width :] = dv[at * rows : (at + 1) * rows]
    put_columns(place[2], own_half, other_half, cols_ref)
    for pair in (2, 3, 0, 1):
        left = [out_ref[lax.bitwise_xor(rank, 2 * pair + at)] for at in range(2)]
        term = dot_rows(jnp.concatenate(left, axis=0), cols_ref[...])
        for at in range(2):
            if pair < 2:
                near_ref[2 * pair + at] = term[at * rows : (at + 1) * rows]
            else:
                away_ref[2 * pair + at - 4] = term[at * rows : (at + 1) * rows].astype(LOW)


def normalize(values):
    center = values - jnp.mean(values, axis=-1, keepdims=True)
    scale = lax.rsqrt(jnp.mean(center * center, axis=-1, keepdims=True) + 1e-05)
    return center * scale, scale


def normalize_back(cotangent, gain, normed, scale):
    dn = cotangent * gain
    inner = jnp.mean(dn, axis=-1, keepdims=True)
    outer = jnp.mean(dn * normed, axis=-1, keepdims=True)
    return scale * (dn - inner - normed * outer)


def quarter_span(place, at, size):
    return pl.ds(pl.multiple_of(lax.bitwise_xor(place[1], at) * size, size), size)


def fetch_out(place, sources, held, sems):
    own = held.shape[1]
    copies = []
    for at, source in enumerate(sources):
        for part in range(2):
            start = (2 * lax.bitwise_xor(place[1], at) + part) * own
            span = pl.ds(pl.multiple_of(start, own), own)
            copies.append(
                pltpu.make_async_copy(
                    source.at[:, part], held.at[:, :, span], sems.at[2 * at + part]
                )
            )
    for copy in copies:
        copy.start()
    return copies


def mix_kernel(
    place, context_ref, tokens_ref, vec_ref, *refs
):
    sources, refs = refs[:4], refs[4:]
    middle_ref, low_ref, norm_ref, scale_ref, left_ref, out_ref, sems = refs
    copies = fetch_out(place, sources, out_ref, sems)
    own = context_ref.shape[2]
    for at in range(8):
        left_ref[:, at * own : (at + 1) * own] = context_ref[at]
    for copy in copies:
        copy.wait()
    attended = dot(left_ref[...], out_ref[...].reshape(8 * own, 8 * own))
    norm, scale = normalize(tokens_ref[...].astype(FULL) + (attended + vec_ref[6:7]))
    middle = norm * vec_ref[0:1] + vec_ref[2:3]
    middle_ref[...] = middle
    low_ref[...] = middle.astype(LOW)
    norm_ref[...] = norm
    scale_ref[...] = scale


def fetch_units(place, sources, w_in, w_out, sems, first):
    ins = [(sources[0], w_in.at[0])]
    outs = [(sources[1], w_out.at[0])]
    for at, source in enumerate(sources[2:]):
        span = quarter_span(place, at, source.shape[1])
        ins.append((source.at[0], w_in.at[1, span]))
        outs.append((source.at[1], w_out.at[1, span]))
    order = ins[:1] + outs[:1] + ins[1:] + outs[1:]
    if first == 1:
        order = outs[:1] + ins[:1] + outs[1:] + ins[1:]
    copies = [pltpu.make_async_copy(*both, sems.at[at]) for at, both in enumerate(order)]
    for copy in copies:
        copy.start()

    def wait(part, which):
        if part % 2 == 0:
            start = 2 + 4 * which if part else which
            for copy in copies[start : start + 4] if part else copies[start : start + 1]:
                copy.wait()

    return wait


def ffn_kernel(place, first_ref, second_ref, *refs):
    bias_ref, sources, refs = refs[0], refs[1:7], refs[7:]
    pre_ref, act_ref, near_ref, away_ref, sum_ref, w_in, w_out, sems = refs
    wait = fetch_units(place, sources, w_in, w_out, sems, 0)
    rows = first_ref.shape[0]
    step = bias_ref.shape[2]
    both = jnp.concatenate([first_ref[...], second_ref[...]], axis=0)
    for part in range(4):
        span = slice(part * 2 * step, (part + 1) * 2 * step)
        shard, rows_of = part // 2, slice(part % 2 * 2 * step, (part % 2 + 1) * 2 * step)
        whose = place[4] * 4 + lax.bitwise_xor(place[5], 2 * shard)
        bias = [bias_ref[whose * 4 + part % 2 * 2 + at] for at in range(2)]
        wait(part, 0)
        pre = dot_rows(both, w_in[shard, rows_of]) + jnp.concatenate(bias, axis=1)
        pre_ref[:, span] = pre
        act = (pre * (0.5 * (1.0 + lax.erf(pre * (0.5**0.5))))).astype(LOW)
        act_ref[:, span] = act
        wait(part, 1)
        term = dot(act, w_out[shard, rows_of])
        if part == 0:
            sum_ref[...] = term
        else:
            sum_ref[...] += term
    near_ref[...] = sum_ref[:rows]
    away_ref[...] = sum_ref[rows:].astype(LOW)


def ffn_back_kernel(place, first_ref, second_ref, slope_ref, *refs):
    sources, refs = refs[:6], refs[6:]
    grad_ref, near_ref, away_ref, units_ref, sum_ref, w_in, w_out, sems = refs
    wait = fetch_units(place, sources, w_in, w_out, sems, 1)
    rows = first_ref.shape[0]
    step = units_ref.shape[2]
    both = jnp.concatenate([first_ref[...], second_ref[...]], axis=0)
    for part in range(4):
        span = slice(part * 2 * step, (part + 1) * 2 * step)
        shard, rows_of = part // 2, slice(part % 2 * 2 * step, (part % 2 + 1) * 2 * step)
        wait(part, 0)
        grad = (dot_rows(both, w_out[shard, rows_of]) * slope_ref[:, span]).astype(LOW)
        grad_ref[:, span] = grad
        sums = jnp.sum(grad.astype(FULL), axis=0, keepdims=True)
        for at in range(2):
            half = lax.bitwise_xor(place[7], shard)
            units_ref[half * 4 + part % 2 * 2 + at] = sums[:, at * step : (at + 1) * step]
        wait(part, 1)
        term = dot(grad, w_in[shard, rows_of])
        if part == 0:
            sum_ref[...] = term
        else:
            sum_ref[...] += term
    near_ref[...] = sum_ref[:rows]
    away_ref[...] = sum_ref[rows:].astype(LOW)


def top_kernel(
    place, near_ref, sent_ref, far_ref, middle_ref, vec_ref, cotangent_ref,
    layer_ref, grad_ref, low_ref, sums_ref,
):
    summed = near_ref[...] + sent_ref[...].astype(FULL) + far_ref[...].astype(FULL)
    norm, scale = normalize(middle_ref[...] + summed + vec_ref[7:8])
    layer_ref[...] = norm * vec_ref[1:2] + vec_ref[3:4]
    cotangent = cotangent_ref[...].astype(FULL)
    grad = normalize_back(cotangent, vec_ref[1:2], norm, scale)
    grad_ref[...] = grad
    low_ref[...] = grad.astype(LOW)
    sums_ref[0:1] = jnp.sum(cotangent * norm, axis=0, keepdims=True)
    sums_ref[1:2] = jnp.sum(cotangent, axis=0, keepdims=True)
    sums_ref[2:3] = jnp.sum(grad.astype(LOW).astype(FULL), axis=0, keepdims=True)


def mix_back_kernel(
    place, near_ref, sent_ref, far_ref, grad_two_ref, norm_ref, scale_ref, vec_ref, *refs
):
    sources, refs = refs[:4], refs[4:]
    grad_ref, low_ref, context_ref, sums_ref, out_ref, sems = refs
    copies = fetch_out(place, sources, out_ref, sems)
    summed = near_ref[...] + sent_ref[...].astype(FULL) + far_ref[...].astype(FULL)
    grad_mid = grad_two_ref[...] + summed
    norm = norm_ref[...]
    grad = normalize_back(grad_mid, vec_ref[0:1], norm, scale_ref[...])
    grad_ref[...] = grad
    low_ref[...] = grad.astype(LOW)
    sums_ref[0:1] = jnp.sum(grad_mid * norm, axis=0, keepdims=True)
    sums_ref[1:2] = jnp.sum(grad_mid, axis=0, keepdims=True)
    sums_ref[2:3] = jnp.sum(grad.astype(LOW).astype(FULL), axis=0, keepdims=True)
    own = context_ref.shape[2]
    for copy in copies:
        copy.wait()
    total = dot_rows(low_ref[...], out_ref[...].reshape(8 * own, 8 * own)).astype(LOW)
    own = context_ref.shape[2]
    for at in range(8):
        context_ref[at] = total[:, at * own : (at + 1) * own]


def weight_grad_kernel(place, left_0, left_1, *refs):
    right, near_ref, away_ref = refs[:4], refs[4], refs[5]
    rows = near_ref.shape[1]
    first = jnp.concatenate([right[0][...], right[1][...]], axis=0)
    second = jnp.concatenate([right[2][...], right[3][...]], axis=0)
    for stays in range(2):
        shard = place[6] if stays else 1 - place[6]
        for half in range(2):
            span = pl.ds(pl.multiple_of((2 * shard + half) * 2 * rows, 2 * rows), 2 * rows)
            both = dot_cols(left_0[:, span], first) + dot_cols(left_1[:, span], second)
            for at in range(2):
                part = both[at * rows : (at + 1) * rows]
                slot = 2 * lax.bitwise_xor(place[3], at) + lax.bitwise_xor(place[7], half)
                if stays:
                    near_ref[slot] = part
                else:
                    away_ref[slot] = part.astype(LOW)


def out_grad_kernel(place, *refs):
    parts, grads, near_ref, away_ref = refs[:4], refs[4:8], refs[8], refs[9]
    step = near_ref.shape[1]
    right = jnp.concatenate([grad[...] for grad in grads], axis=0)
    for stays in range(2):
        which = place[3] if stays else 1 - place[3]
        total = dot_cols(jnp.concatenate([part[which] for part in parts], axis=0), right)
        for at in range(4):
            if stays:
                near_ref[at] = total[at * step : (at + 1) * step]
            else:
                away_ref[at] = total[at * step : (at + 1) * step].astype(LOW)


def qkv_grad_kernel(place, *refs):
    slots, refs = refs[:8], refs[8:]
    grad_ref, top_ref, mid_ref, units_a, units_b = refs[:5]
    near_ref, away_ref, total_ref, sums_ref = refs[5:]
    rank, seq_at = place[0], place[1]
    rows = slots[0].shape[0]
    width = sums_ref.shape[1]
    own = width // 8
    quarter = width // 4
    col_sum = 0.0
    for pair in range(4):
        grads = [grad_ref[lax.bitwise_xor(rank, 2 * pair + at)] for at in range(2)]
        grads = jnp.concatenate(grads, axis=0)
        both = jnp.concatenate([slots[2 * pair][...], slots[2 * pair + 1][...]], axis=0)
        term = dot_cols(both, grads)
        col_sum += jnp.sum(grads.astype(FULL), axis=0, keepdims=True)
        if pair == 0:
            total_ref[...] = term
        else:
            total_ref[...] += term
    sums_ref[...] = jnp.zeros_like(sums_ref)
    sums_ref[0:1] = mid_ref[0:1]
    sums_ref[1:2] = top_ref[0:1]
    sums_ref[2:3] = mid_ref[1:2]
    sums_ref[3:4] = top_ref[1:2]
    own_cols = pl.ds(pl.multiple_of(rank * own, own), own)
    sums_ref[4:5, own_cols] = col_sum[:, :own]
    sums_ref[5:6, own_cols] = col_sum[:, 2 * own :]
    sums_ref[6:7] = mid_ref[2:3]
    sums_ref[7:8] = top_ref[2:3]
    row_at = lax.broadcasted_iota(jnp.int32, (8, own), 0)
    for at in (1, 3, 0, 2):
        whose = lax.bitwise_xor(seq_at, at)
        part = total_ref[quarter_span(place, at, quarter)]
        sums = sums_ref[:, quarter_span(place, at, quarter)]
        here = lax.shift_right_logical(whose, 1) == place[4]
        first = 4 * lax.bitwise_and(whose, 1)
        units = [units_a[first + row] + units_b[first + row] for row in range(4)]
        mine = (row_at >= 4 * place[8]) & (row_at < 4 * place[8] + 4)
        units = jnp.where(mine & here, jnp.concatenate(units + units, axis=0), 0.0)
        sums = jnp.concatenate([sums, units], axis=1)
        sums = jnp.concatenate([sums, jnp.zeros_like(sums)], axis=0)
        if at % 2:
            away_ref[at // 2, :quarter] = part.astype(LOW)
            away_ref[at // 2, quarter:] = sums.astype(LOW)
        else:
            near_ref[at // 2, :quarter] = part
            near_ref[at // 2, quarter:] = sums


def qkv_send_kernel(place, near_ref, far_ref, out_ref):
    total = near_ref[...] + far_ref[...].astype(FULL)
    rows = total.shape[0] - 16
    step = rows // 8
    sums = total[rows:].astype(LOW)
    for at in range(8):
        out_ref[at, :step] = total[at * step : (at + 1) * step].astype(LOW)
        out_ref[at, step:] = sums


def qkv_last_kernel(place, parts_ref, grad_ref, sums_ref):
    step = grad_ref.shape[0]
    own = parts_ref.shape[2] // 3
    for at in range(8):
        for which in range(3):
            cols = slice((which * 8 + at) * own, (which * 8 + at + 1) * own)
            grad_ref[:, cols] = parts_ref[at, :step, which * own : (which + 1) * own].astype(FULL)
    sums = parts_ref[0, step:].astype(FULL)
    for at in range(1, 8):
        sums += parts_ref[at, step:].astype(FULL)
    sums_ref[...] = sums


def grouped_body(tokens, out_grad, w_qkv, w_out, fc_in, fc_out, fc_in_bias, vectors):
    rows, width = tokens.shape
    own = width // 8
    seq_at = lax.axis_index("seq")
    core_at, across_at = lax.rem(seq_at, 2), seq_at // 2
    head_at, blk_at = lax.axis_index("head"), lax.axis_index("blk")
    rank = head_at * 4 + blk_at
    far_at, near_at = blk_at // 2, lax.rem(blk_at, 2)
    place = jnp.stack(
        [rank, seq_at, core_at, across_at, head_at, blk_at, far_at ^ core_at, far_at, near_at]
    ).astype(jnp.int32)
    unit_rows = fc_in.shape[0] // 4
    units = 8 * unit_rows

    half = own // 2
    qkv_half = lax.dynamic_slice_in_dim(w_qkv, core_at * half, half, 0)
    qkv_half = qkv_half.reshape(half, 3, 8, own).transpose(2, 1, 0, 3).reshape(8, 3 * half, own)
    small = jnp.concatenate([vectors.T, fc_in_bias.reshape(-1, own)], axis=0)
    small = jnp.broadcast_to(small[None], (8, 12, own))
    out_quarter = lax.dynamic_slice_in_dim(w_out, seq_at * 2 * own, 2 * own, 1)
    out_quarter = out_quarter.reshape(own, 2, own).transpose(1, 0, 2).reshape(1, 2 * own, own)
    out_quarter = jnp.broadcast_to(out_quarter, (8, 2 * own, own))
    to_swap = jnp.concatenate(
        [qkv_half, out_quarter, small, jnp.zeros((8, 4, own), LOW)], axis=1
    )
    units_away = jnp.stack(
        [lax.dynamic_slice_in_dim(w, seq_at * unit_rows, unit_rows, 0) for w in (fc_in, fc_out)]
    )

    inner = inner_blk()
    first = lax.ppermute(tokens, "blk", PAIRS)
    middle = lax.ppermute(tokens, "blk", INNER)
    across_0 = flip_head(tokens)
    first, middle, across_0, to_swap = after((first, middle, across_0, to_swap))
    second_in = lax.ppermute(first, "blk", INNER)
    second_out = lax.ppermute(middle, "blk", OUTER)
    across_1 = flip_head(first)
    swapped = lax.all_to_all(to_swap, GROUP, 0, 0, tiled=True)
    second_in, second_out, across_1 = after((second_in, second_out, across_1))
    third = lax.ppermute(second_in, "blk", OUTER)
    second = jnp.where(inner, second_in, second_out)
    across_2 = flip_head(second)
    third, across_2, swapped, units_away = after((third, across_2, swapped, units_away))
    third = jnp.where(inner, middle, third)
    across_3 = flip_head(third)
    own_half = swapped[:, : 3 * half].reshape(8, 3, half, own)
    other_half = lax.ppermute(own_half, "seq", CORE)
    out_quarter = swapped[:, 3 * half : 3 * half + 2 * own].reshape(8, 2, own, own)
    small = swapped[:, 3 * half + 2 * own : 3 * half + 2 * own + 12].astype(FULL)
    vec = small[:, :8].transpose(1, 0, 2).reshape(8, width)
    bias_all = small[:, 8:].reshape(32, 1, own)
    across_3, other_half = after((across_3, other_half))
    slots = [tokens, first, second, third, across_0, across_1, across_2, across_3]

    units_two_on = lax.ppermute(units_away, "blk", TWO_ON)
    out_slots = gather_seq(out_quarter)

    bias = vectors.T.reshape(8, 1, own)[4:6].astype(FULL)
    seq_rows = 8 * rows
    heads = own // HEAD_DIM
    kept_shapes = [((seq_rows, own), LOW)] * 3 + [((seq_rows, own), FULL)] * 2
    kept_shapes.append(((heads, seq_rows, seq_rows), LOW))
    kept_scratch = [pltpu.VMEM(*shape) for shape in kept_shapes]
    context, *kept = call(
        attend_kernel,
        [shape_of((8, rows, own), LOW)] + [shape_of(*shape) for shape in kept_shapes],
        place, *slots, own_half, other_half, bias,
        scratch=kept_scratch + [pltpu.VMEM((width, 3 * own), LOW), pltpu.SemaphoreType.DMA((9,))],
        flops=8 * 10**9,
        far_out=6,
    )
    context, units_two_on = after((context, units_two_on), *out_slots[1:])
    context = lax.all_to_all(context, GROUP, 0, 0, tiled=True)
    ffn_weights = [fc_in, fc_out] + gather_seq(units_two_on)
    out_scratch = [pltpu.VMEM((8, own, width), LOW), pltpu.SemaphoreType.DMA((8,))]

    per_row = shape_of((rows, width), FULL)
    per_row_low = shape_of((rows, width), LOW)
    middle, middle_low, norm_one, scale_one = call(
        mix_kernel,
        [per_row, per_row_low, per_row, shape_of((rows, 1), FULL)],
        place, context, tokens, vec, *out_slots,
        scratch=[pltpu.VMEM((rows, width), LOW)] + out_scratch,
        flops=2 * 10**9,
        far_in=4,
    )

    both_rows = shape_of((2 * rows, units), FULL)
    both_rows_low = shape_of((2 * rows, units), LOW)
    middle_slots = gather_four(middle_low)
    ffn_scratch = [pltpu.VMEM((2 * rows, width), FULL)]
    ffn_scratch += [pltpu.VMEM((2, 4 * unit_rows, width), LOW)] * 2
    ffn_scratch += [pltpu.SemaphoreType.DMA((10,))]
    ffn_parts = []
    for at in (0, 2):
        ffn_parts.append(
            call(
                ffn_kernel,
                [both_rows, both_rows_low, per_row, per_row_low],
                place, middle_slots[at], middle_slots[at + 1], bias_all, *ffn_weights,
                scratch=ffn_scratch,
                flops=3 * 10**9,
                far_in=6,
            )
        )

    def features_of(core, head):
        both = lax.dynamic_index_in_dim(context.reshape(2, 2, 2, rows, own), core, 1, False)
        return lax.dynamic_index_in_dim(both, head, 1, False)

    diagonal = []
    for seq in range(4):
        for head in range(2):
            diagonal.append((seq * 2 + head, (seq ^ 1) * 2 + 1 - head))
    parts = [
        features_of(core_at, head_at),
        features_of(1 - core_at, head_at),
        features_of(core_at, 1 - head_at),
        features_of(1 - core_at, 1 - head_at),
    ]
    parts[1:] = after(parts[1:], ffn_parts[0][1])
    parts = [
        parts[0],
        lax.ppermute(parts[1], "seq", CORE),
        flip_head(parts[2]),
        lax.ppermute(parts[3], ("seq", "head"), tuple(diagonal)),
    ]

    def scatter_parts(near_part, far_part):
        sent_far = lax.ppermute(far_part[1], "blk", PAIRS).astype(FULL)
        far = flip_head((far_part[0] + sent_far).astype(LOW))
        return near_part[0], lax.ppermute(near_part[1], "blk", PAIRS), far

    def scatter_units(near, away):
        near = near + lax.ppermute(away, "seq", CORE).astype(FULL)
        near = near[:2] + lax.ppermute(near[2:].astype(LOW), "seq", ACROSS).astype(FULL)
        return near[0] + lax.ppermute(near[1].astype(LOW), "blk", TWO_ON).astype(FULL)

    summed = scatter_parts(ffn_parts[0][2:4], ffn_parts[1][2:4])
    three_sums = shape_of((3, width), FULL)
    layer_output, grad_two, grad_ffn, top_sums = call(
        top_kernel,
        [per_row, per_row, per_row_low, three_sums],
        place, *summed, middle, vec, out_grad,
        flops=10**9,
    )

    grad_ffn_slots = gather_four(grad_ffn)
    back_parts = []
    for at in (0, 2):
        pre = ffn_parts[at // 2][0]
        cdf = 0.5 * (1.0 + lax.erf(pre * (0.5**0.5)))
        slope = cdf + pre * jnp.exp(-0.5 * pre * pre) * ((2.0 * math.pi) ** -0.5)
        back_parts.append(
            call(
                ffn_back_kernel,
                [both_rows_low, per_row, per_row_low, shape_of((8, 1, unit_rows), FULL)],
                place, grad_ffn_slots[at], grad_ffn_slots[at + 1], slope, *ffn_weights,
                scratch=ffn_scratch,
                flops=3 * 10**9,
                far_in=6,
            )
        )
    summed = scatter_parts(back_parts[0][1:3], back_parts[1][1:3])
    terms = [shape_of((4, unit_rows, width), FULL), shape_of((4, unit_rows, width), LOW)]
    out_near_grad, out_away_grad = call(
        weight_grad_kernel, terms, place, ffn_parts[0][1], ffn_parts[1][1], *grad_ffn_slots,
        flops=2 * 10**9,
    )
    grad_fc_out = scatter_units(out_near_grad, out_away_grad)
    in_near_grad, in_away_grad = call(
        weight_grad_kernel, terms, place, back_parts[0][0], back_parts[1][0], *middle_slots,
        flops=2 * 10**9,
    )
    summed = after(summed, in_away_grad)
    grad_one, grad_attn, grad_context, mid_sums = call(
        mix_back_kernel,
        [per_row, per_row_low, shape_of((8, rows, own), LOW), three_sums],
        place, *summed, grad_two, norm_one, scale_one, vec, *out_slots,
        scratch=out_scratch,
        flops=2 * 10**9,
        far_in=4,
    )
    grad_context = lax.all_to_all(grad_context, GROUP, 0, 0, tiled=True)
    grad_fc_in = scatter_units(in_near_grad, in_away_grad)
    grad_attn_slots = gather_cores(grad_attn)

    grad_cols, near_terms, away_terms = call(
        attend_back_kernel,
        [
            shape_of((8, rows, 3 * own), LOW),
            shape_of((4, rows, width), FULL),
            shape_of((4, rows, width), LOW),
        ],
        place, grad_context, own_half, other_half, *kept,
        scratch=[pltpu.VMEM((width, 3 * own), LOW)]
        + kept_scratch
        + [pltpu.VMEM((own, seq_rows), FULL)] * 2
        + [pltpu.SemaphoreType.DMA((9,))],
        flops=8 * 10**9,
        far_in=6,
    )
    terms = scatter_group(near_terms, away_terms)
    input_grad = grad_one + terms[0]
    for term in terms[1:]:
        input_grad = input_grad + term.astype(FULL)

    payload_rows = 2 * own + 16
    near, away = call(
        qkv_grad_kernel,
        [shape_of((2, payload_rows, 3 * own), FULL), shape_of((2, payload_rows, 3 * own), LOW)],
        place, *slots, grad_cols, top_sums, mid_sums, back_parts[0][3], back_parts[1][3],
        scratch=[pltpu.VMEM((width, 3 * own), FULL), pltpu.VMEM((8, width), FULL)],
        flops=2 * 10**9,
    )
    sent = lax.ppermute(away, "seq", CORE).astype(FULL)
    far = lax.ppermute((near[1] + sent[1]).astype(LOW), "seq", ACROSS)

    out_terms = [shape_of((4, own // 4, width), FULL), shape_of((4, own // 4, width), LOW)]
    near_rows, away_rows = call(
        out_grad_kernel, out_terms, place, *parts, *grad_attn_slots, flops=10**9
    )
    near_rows = near_rows + lax.ppermute(away_rows, "seq", ACROSS).astype(FULL)
    grad_w_out = lax.all_to_all(near_rows.astype(LOW), "blk", 0, 0, tiled=True)
    grad_w_out = jnp.sum(grad_w_out.astype(FULL), axis=0)

    moves = []
    for across in range(2):
        for core in range(2):
            for head in range(2):
                for two_on in range(2):
                    for near_by in range(2):
                        start = (across * 2 + core) * 8 + head * 4 + two_on * 2 + near_by
                        stop = (head * 2 + core) * 8 + near_by * 4 + two_on * 2 + across
                        if start != stop:
                            moves.append((start, stop))
    stays = (across_at == head_at) & (head_at == near_at)

    def to_owner(grad):
        moved = lax.ppermute(grad.astype(LOW), ("seq", "head", "blk"), moves).astype(FULL)
        return jnp.where(stays, grad, moved)

    grad_fc_out, grad_fc_in = to_owner(grad_fc_out), to_owner(grad_fc_in)

    (payload,) = call(
        qkv_send_kernel,
        [shape_of((8, own // 4 + 16, 3 * own), LOW)],
        place, near[0] + sent[0], far,
    )
    payload = lax.all_to_all(payload, GROUP, 0, 0, tiled=True)
    grad_w_qkv, sums = call(
        qkv_last_kernel,
        [shape_of((own // 4, 3 * width), FULL), shape_of((16, 3 * own), FULL)],
        place, payload,
    )
    grad_vectors = lax.dynamic_slice(sums, (0, rank * (own // 4)), (8, own // 4)).T
    grad_bias = lax.dynamic_slice(sums, (rank, 2 * own), (1, own)).reshape(own)
    return (
        layer_output,
        input_grad,
        grad_w_qkv,
        grad_w_out,
        grad_fc_in,
        grad_fc_out,
        grad_bias,
        grad_vectors,
    )


def solution(mesh):
    sizes = tuple(mesh.shape[name] for name in ("seq", "head", "blk"))
    return jax.shard_map(
        grouped_body if sizes == (4, 2, 4) else general_body,
        mesh=mesh,
        in_specs=(
            P(("seq", "head", "blk"), None),
            P(("seq", "head", "blk"), None),
            P(("head", "blk"), None),
            P(("head", "blk"), None),
            P(("head", "blk"), None),
            P(("head", "blk"), None),
            P(("head", "blk")),
            P(("head", "blk"), None),
        ),
        out_specs=(
            P(("seq", "head", "blk"), None),
            P(("seq", "head", "blk"), None),
            P(("seq", "head", "blk"), None),
            P(("seq", "head", "blk"), None),
            P(("seq", "head", "blk"), None),
            P(("seq", "head", "blk"), None),
            P(("seq", "head", "blk")),
            P(("seq", "head", "blk"), None),
        ),
        check_vma=False,
    )
```

```python
import math

import jax
import jax.numpy as jnp
from jax import lax
from jax.experimental import pallas as pl
from jax.experimental.pallas import tpu as pltpu
from jax.sharding import PartitionSpec as P

HEAD_DIM = 64


def layer_norm(values, gain_vec, shift_vec):
    center = values - jnp.mean(values, axis=-1, keepdims=True)
    spread = jnp.mean(center * center, axis=-1, keepdims=True)
    return center * lax.rsqrt(spread + 1e-05) * gain_vec + shift_vec


def gelu_exact(values):
    return jax.nn.gelu(values, approximate=False)


def split_heads(values):
    return values.reshape(values.shape[0], values.shape[1] // HEAD_DIM, HEAD_DIM)


def head_scores(left_rows, right_rows):
    return jnp.einsum("qhd,khd->hqk", left_rows, right_rows, preferred_element_type=jnp.float32)


def ffn_part(factors):
    middle_low, grad_pre_full, act_full, grad_ffn = factors
    return jnp.concatenate(
        [
            jnp.einsum("tf,td->fd", grad_pre_full, middle_low, preferred_element_type=jnp.float32),
            jnp.einsum("tf,td->fd", act_full, grad_ffn, preferred_element_type=jnp.float32),
        ],
        axis=1,
    )


def attn_part(factors, extra_cols):
    tokens, grad_proj, context, grad_attn = factors
    return jnp.concatenate(
        [
            jnp.einsum("tn,tc->nc", tokens, grad_proj, preferred_element_type=jnp.float32),
            jnp.einsum("tn,tc->nc", context, grad_attn, preferred_element_type=jnp.float32),
            extra_cols,
        ],
        axis=1,
    )


def general_body(tokens, out_grad, w_qkv, w_out, fc_in, fc_out, fc_in_bias, vectors):
    model_width = tokens.shape[1]
    hidden_units = fc_in.shape[0] * lax.axis_size(("head", "blk"))
    ratio = hidden_units // model_width
    scale = HEAD_DIM ** (-0.5)
    part_qkv = lax.all_gather(w_qkv, ("head", "blk"), axis=0, tiled=True)
    part_out = lax.all_gather(w_out, ("head", "blk"), axis=0, tiled=True)
    part_vec = lax.all_gather(vectors, ("head", "blk"), axis=0, tiled=True)
    part_rows = part_qkv.shape[0]
    projected = jnp.dot(tokens, part_qkv, preferred_element_type=jnp.float32)
    out_full = part_out
    attn_state = (projected, out_full, part_vec)
    projected = attn_state[0]
    out_full = attn_state[1]
    vec_float = attn_state[2].astype(jnp.float32)
    gain_one, gain_two = (vec_float[:, 0], vec_float[:, 1])
    shift_one, shift_two = (vec_float[:, 2], vec_float[:, 3])
    bias_query, bias_value = (vec_float[:, 4], vec_float[:, 5])
    bias_output, bias_ffn = (vec_float[:, 6], vec_float[:, 7])
    queries = ((projected[:, :model_width] + bias_query) * scale).astype(jnp.bfloat16)
    key_rows = projected[:, model_width : 2 * model_width].astype(jnp.bfloat16)
    value_rows = (projected[:, 2 * model_width :] + bias_value).astype(jnp.bfloat16)
    query_heads, key_heads, value_heads = (
        lax.all_to_all(queries, "head", split_axis=1, concat_axis=0, tiled=True),
        lax.all_to_all(key_rows, "head", split_axis=1, concat_axis=0, tiled=True),
        lax.all_to_all(value_rows, "head", split_axis=1, concat_axis=0, tiled=True),
    )
    query_split = split_heads(query_heads)
    group_rows = query_split.shape[0]
    group_width = key_heads.shape[1]
    seq_rows = group_rows * lax.axis_size("blk")
    portion = (
        lax.all_gather(key_heads, "blk", axis=0, tiled=True),
        lax.all_gather(value_heads, "blk", axis=0, tiled=True),
    )
    scores = head_scores(query_split, split_heads(portion[0]))
    run_sum = jnp.sum(jnp.exp(scores), axis=-1)
    key_all = portion[0]
    value_all = portion[1]
    run_sum, key_all, value_all = (run_sum, key_all, value_all)
    log_total = jnp.log(run_sum)
    block_rows = math.gcd(512, seq_rows)
    block_count = seq_rows // block_rows
    key_blocks = key_all.reshape(block_count, block_rows, group_width)
    value_blocks = value_all.reshape(block_count, block_rows, group_width)

    def mix_block(totals, pair):
        scores = head_scores(query_split, split_heads(pair[0]))
        probs_low = jnp.exp(scores - log_total[:, :, None]).astype(jnp.bfloat16)
        return (
            totals
            + jnp.einsum(
                "hqk,khd->qhd", probs_low, split_heads(pair[1]), preferred_element_type=jnp.float32
            ),
            None,
        )

    mixed, unused = lax.scan(
        mix_block, jnp.zeros(query_split.shape, jnp.float32), (key_blocks, value_blocks)
    )
    context = lax.all_to_all(
        mixed.reshape(group_rows, -1).astype(jnp.bfloat16),
        "head",
        split_axis=0,
        concat_axis=1,
        tiled=True,
    )
    attn_out = jnp.dot(context, out_full, preferred_element_type=jnp.float32) + bias_output
    residual_one = tokens.astype(jnp.float32) + attn_out
    middle, norm_one_back = jax.vjp(layer_norm, residual_one, gain_one, shift_one)
    middle_low = middle.astype(jnp.bfloat16)
    part_in = lax.all_gather(fc_in, ("head", "blk"), axis=0, tiled=True)
    part_out = lax.all_gather(fc_out, ("head", "blk"), axis=0, tiled=True)
    part_bias = lax.all_gather(fc_in_bias, ("head", "blk"), axis=0, tiled=True)
    pre_part = jnp.einsum("td,fd->tf", middle_low, part_in, preferred_element_type=jnp.float32)
    pre_part = pre_part + part_bias.astype(jnp.float32)
    act_part = gelu_exact(pre_part).astype(jnp.bfloat16)
    summed = jnp.dot(act_part, part_out, preferred_element_type=jnp.float32)
    ffn_pre_full = pre_part
    residual_two = middle + summed + bias_ffn
    layer_output, norm_two_back = jax.vjp(layer_norm, residual_two, gain_two, shift_two)
    grad_resid_two, grad_gain_two, grad_shift_two = norm_two_back(out_grad.astype(jnp.float32))
    grad_ffn = grad_resid_two.astype(jnp.bfloat16)
    qkv_flat = w_qkv.reshape(fc_in.shape[0], -1)
    portion = (
        lax.all_gather(fc_in, ("head", "blk"), axis=0, tiled=True),
        lax.all_gather(fc_out, ("head", "blk"), axis=0, tiled=True),
        lax.all_gather(qkv_flat, ("head", "blk"), axis=0, tiled=True),
    )
    part_in = portion[0]
    part_rows = part_in.shape[0]
    pre_part = ffn_pre_full
    grad_act = jnp.einsum("td,fd->tf", grad_ffn, portion[1], preferred_element_type=jnp.float32)
    grad_pre = jax.vjp(gelu_exact, pre_part)[1](grad_act)[0].astype(jnp.bfloat16)
    grad_mid = jnp.dot(grad_pre, part_in, preferred_element_type=jnp.float32)
    grad_mid, grad_pre_all = (grad_mid, grad_pre)
    qkv_gathered = portion[2]
    qkv_full = qkv_gathered.reshape(model_width, 3 * model_width)
    grad_resid_one, grad_gain_one, grad_shift_one = norm_one_back(grad_resid_two + grad_mid)
    grad_attn = grad_resid_one.astype(jnp.bfloat16)
    grad_context = jnp.einsum(
        "td,ed->te", grad_attn, out_full, preferred_element_type=jnp.float32
    ).astype(jnp.bfloat16)
    grad_ctx_heads = lax.all_to_all(grad_context, "head", split_axis=1, concat_axis=0, tiled=True)
    grad_ctx_split = split_heads(grad_ctx_heads)
    delta_heads = jnp.sum(grad_ctx_split.astype(jnp.float32) * mixed, axis=-1).T

    def back_block(grad_query, pair):
        key_part = split_heads(pair[0])
        value_part = split_heads(pair[1])
        scores = head_scores(query_split, key_part)
        probs = jnp.exp(scores - log_total[:, :, None])
        dprobs = head_scores(grad_ctx_split, value_part)
        dscores = (probs * (dprobs - delta_heads[:, :, None])).astype(jnp.bfloat16)
        grad_query = grad_query + jnp.einsum(
            "hqk,khd->qhd", dscores, key_part, preferred_element_type=jnp.float32
        )
        grad_key = jnp.einsum(
            "hqk,qhd->khd", dscores, query_split, preferred_element_type=jnp.float32
        )
        grad_value = jnp.einsum(
            "hqk,qhd->khd",
            probs.astype(jnp.bfloat16),
            grad_ctx_split,
            preferred_element_type=jnp.float32,
        )
        part_rows = pair[0].shape[0]
        return (
            grad_query,
            jnp.concatenate(
                [grad_key.reshape(part_rows, -1), grad_value.reshape(part_rows, -1)], axis=1
            ),
        )

    grad_query_heads, kv_terms = lax.scan(
        back_block, jnp.zeros(query_split.shape, jnp.float32), (key_blocks, value_blocks)
    )
    kv_own = lax.psum_scatter(
        kv_terms.reshape(seq_rows, 2 * group_width).astype(jnp.bfloat16),
        "blk",
        scatter_dimension=0,
        tiled=True,
    ).astype(jnp.float32)
    grad_query_tok, grad_key_tok, grad_value_tok = (
        lax.all_to_all(
            grad_query_heads.reshape(group_rows, -1).astype(jnp.bfloat16),
            "head",
            split_axis=0,
            concat_axis=1,
            tiled=True,
        ),
        lax.all_to_all(
            kv_own[:, :group_width].astype(jnp.bfloat16),
            "head",
            split_axis=0,
            concat_axis=1,
            tiled=True,
        ),
        lax.all_to_all(
            kv_own[:, group_width:].astype(jnp.bfloat16),
            "head",
            split_axis=0,
            concat_axis=1,
            tiled=True,
        ),
    )
    grad_proj = jnp.concatenate(
        [grad_query_tok * jnp.bfloat16(scale), grad_key_tok, grad_value_tok], axis=1
    )
    through_proj = jnp.einsum("tc,nc->tn", grad_proj, qkv_full, preferred_element_type=jnp.float32)
    input_grad = grad_resid_one + through_proj
    grad_proj_float = grad_proj.astype(jnp.float32)
    vec_term = jnp.stack(
        [
            grad_gain_one,
            grad_gain_two,
            grad_shift_one,
            grad_shift_two,
            jnp.sum(grad_proj_float[:, :model_width], axis=0),
            jnp.sum(grad_proj_float[:, 2 * model_width :], axis=0),
            jnp.sum(grad_attn.astype(jnp.float32), axis=0),
            jnp.sum(grad_ffn.astype(jnp.float32), axis=0),
        ],
        axis=1,
    )
    bias_term = jnp.sum(grad_pre_all.astype(jnp.float32), axis=0).reshape(model_width, -1)
    bias_cols = bias_term.shape[1]
    padding = jnp.zeros((model_width, 128 - 8 - bias_cols), jnp.float32)
    extra_cols = jnp.concatenate([vec_term, bias_term, padding], axis=1)
    rows_dev = hidden_units // lax.axis_size(("seq", "head", "blk"))
    ffn_block = ffn_part((middle_low, grad_pre_all, act_part, grad_ffn))
    attn_block = attn_part((tokens, grad_proj, context, grad_attn), extra_cols)
    merged = lax.psum_scatter(
        jnp.concatenate(
            [ffn_block, attn_block.reshape(lax.axis_size(("seq", "head", "blk")) * rows_dev, -1)],
            axis=1,
        ),
        ("seq", "head", "blk"),
        scatter_dimension=0,
        tiled=True,
    )
    grad_fc_in = merged[:, :model_width]
    grad_fc_out = merged[:, model_width : 2 * model_width]
    attn_grad = merged[:, 2 * model_width :].reshape(rows_dev // ratio, 4 * model_width + 128)
    grad_w_qkv = attn_grad[:, : 3 * model_width]
    grad_w_out = attn_grad[:, 3 * model_width : 4 * model_width]
    grad_vectors = attn_grad[:, 4 * model_width : 4 * model_width + 8]
    grad_fc_in_bias = attn_grad[:, 4 * model_width + 8 : 4 * model_width + 8 + bias_cols].reshape(
        -1
    )
    return (
        layer_output,
        input_grad,
        grad_w_qkv,
        grad_w_out,
        grad_fc_in,
        grad_fc_out,
        grad_fc_in_bias,
        grad_vectors,
    )


GROUP = ("head", "blk")
FLIP = ((0, 1), (1, 0))
PAIRS = ((0, 1), (1, 0), (2, 3), (3, 2))
INNER = ((1, 2), (2, 1))
OUTER = ((1, 0), (2, 3))
INWARD = ((0, 1), (3, 2))
TWO_ON = ((0, 2), (2, 0), (1, 3), (3, 1))
CORE = tuple((at, at ^ 1) for at in range(4))
ACROSS = tuple((at, at ^ 2) for at in range(4))
LOW = jnp.bfloat16
FULL = jnp.float32
ROWS_DIMS = (((1,), (1,)), ((), ()))
COLS_DIMS = (((0,), (0,)), ((), ()))


def dot(left, right):
    return jnp.dot(left, right, preferred_element_type=FULL)


def dot_rows(left, right):
    return lax.dot_general(left, right, ROWS_DIMS, preferred_element_type=FULL)


def dot_cols(left, right):
    return lax.dot_general(left, right, COLS_DIMS, preferred_element_type=FULL)


def after(values, *others):
    if not isinstance(values, (list, tuple)):
        return lax.optimization_barrier((values,) + others)[0]
    return lax.optimization_barrier(tuple(values) + others)[: len(values)]


def inner_blk():
    at = lax.axis_index("blk")
    return (at == 1) | (at == 2)


def flip_head(value):
    return lax.ppermute(value, "head", FLIP)


def gather_seq(own):
    across = lax.ppermute(own, "seq", ACROSS)
    return [own, lax.ppermute(own, "seq", CORE), across, lax.ppermute(across, "seq", CORE)]


def gather_four(own):
    across = flip_head(own)
    beside = lax.ppermute(own, "blk", PAIRS)
    return [own, beside, across, lax.ppermute(across, "blk", PAIRS)]


def gather_cores(own):
    across = flip_head(own)
    return [own, lax.ppermute(own, "seq", CORE), across, lax.ppermute(across, "seq", CORE)]


def shape_of(shape, dtype):
    return jax.ShapeDtypeStruct(shape, dtype)


def call(kernel, outs, place, *args, scratch=(), flops=0, vmem=28, far_in=0, far_out=0):
    moved = sum(arg.size * arg.dtype.itemsize for arg in args)
    moved += sum(math.prod(out.shape) * jnp.dtype(out.dtype).itemsize for out in outs)
    near = pl.BlockSpec(memory_space=pltpu.VMEM)
    far = pl.BlockSpec(memory_space=pltpu.HBM)
    return pl.pallas_call(
        kernel,
        out_shape=outs,
        in_specs=[pl.BlockSpec(memory_space=pltpu.SMEM)]
        + [near] * (len(args) - far_in)
        + [far] * far_in,
        out_specs=[near] * (len(outs) - far_out) + [far] * far_out,
        scratch_shapes=scratch,
        compiler_params=pltpu.CompilerParams(vmem_limit_bytes=vmem * 2**20),
        cost_estimate=pl.CostEstimate(flops=flops // 2, bytes_accessed=moved, transcendentals=0),
    )(place, *args)


def fetch(sources, held, sems):
    copies = [pltpu.make_async_copy(*both, sems.at[at]) for at, both in enumerate(zip(sources, held))]
    for copy in copies:
        copy.start()
    return copies


def put_columns(place, parts, cols_ref):
    step, width = parts.shape[3:]
    for at in range(8):
        for part in range(4):
            start = (4 * at + lax.bitwise_xor(place[1], part)) * step
            span = pl.ds(pl.multiple_of(start, step), step)
            for which in range(3):
                cols_ref[span, which * width : (which + 1) * width] = parts[part, at, which]


def attend_kernel(place, *refs):
    bias_ref, refs = refs[0], refs[1:]
    quarters, slots, refs = refs[:4], refs[4:12], refs[12:]
    context_ref, kept, refs = refs[0], refs[1:8], refs[8:]
    q_ref, k_ref, v_ref, mixed_ref, inverse_ref, cols_ref, weights_ref, tokens_ref = refs[:8]
    parts, sems, slot_sems = refs[8], refs[9], refs[10]
    rank = place[0]
    width = q_ref.shape[1]
    rows = context_ref.shape[1]
    step = parts.shape[3]
    spans = [slice(pair * 2 * rows, (pair + 1) * 2 * rows) for pair in range(4)]
    fetched = fetch(quarters, [parts.at[at] for at in range(4)], slot_sems)
    held = [tokens_ref.at[at * rows : (at + 1) * rows] for at in range(8)]
    fetched_slots = fetch(slots, held, slot_sems.at[4:12])
    for copy in fetched:
        copy.wait()
    put_columns(place, parts, cols_ref)
    scale = HEAD_DIM ** (-0.5)
    for pair, span in enumerate(spans):
        fetched_slots[2 * pair].wait()
        fetched_slots[2 * pair + 1].wait()
        projected = dot(tokens_ref[span], cols_ref[...])
        q_ref[span] = ((projected[:, :width] + bias_ref[0]) * scale).astype(LOW)
        k_ref[span] = projected[:, width : 2 * width].astype(LOW)
        v_ref[span] = (projected[:, 2 * width :] + bias_ref[1]).astype(LOW)
    copies = []
    for at, ref in enumerate((q_ref, k_ref, v_ref, cols_ref)):
        copies.append(pltpu.make_async_copy(ref, kept[at + 2 * (at == 3)], sems.at[12 + at]))
    for copy in copies:
        copy.start()

    def block_copies(pair, span):
        pairs = (
            (mixed_ref.at[span], kept[3].at[span]),
            (inverse_ref.at[span], kept[4].at[span]),
            (weights_ref.at[:, span], kept[6].at[:, span]),
        )
        return [
            pltpu.make_async_copy(*both, sems.at[pair + 4 * at]) for at, both in enumerate(pairs)
        ]

    @pl.loop(0, 4)
    def _(pair):
        span = pl.ds(pl.multiple_of(pair * 2 * rows, 2 * rows), 2 * rows)
        for at in range(width // HEAD_DIM):
            cols = slice(at * HEAD_DIM, (at + 1) * HEAD_DIM)
            scores = dot_rows(q_ref[span, cols], k_ref[:, cols])
            weights = jnp.exp(scores - jnp.max(scores, axis=-1, keepdims=True))
            inverse = 1.0 / jnp.sum(weights, axis=-1, keepdims=True)
            weights = weights.astype(LOW)
            weights_ref[at, span] = weights
            mixed_ref[span, cols] = dot(weights, v_ref[:, cols]) * inverse
            inverse_ref[span, cols] = jnp.broadcast_to(inverse, (2 * rows, HEAD_DIM))
        first = lax.bitwise_xor(rank, 2 * pair)
        mixed = mixed_ref[span].astype(LOW)
        context_ref[first] = mixed[:rows]
        context_ref[lax.bitwise_xor(first, 1)] = mixed[rows:]
        for copy in block_copies(pair, span):
            copy.start()

    for pair, span in enumerate(spans):
        copies += block_copies(pair, span)
    for copy in copies:
        copy.wait()


def attend_back_kernel(place, grad_ref, *refs):
    kept, refs = refs[:6], refs[6:]
    out_ref, q_ref, k_ref, v_ref, mixed_ref, inverse_ref, weights_ref = refs[:7]
    dk_sum, dv_sum, sems = refs[7:]
    rank = place[0]
    rows, width = grad_ref.shape[1:]
    scale = HEAD_DIM ** (-0.5)
    copies = []
    for at, ref in enumerate((q_ref, k_ref, v_ref, mixed_ref, inverse_ref)):
        copies.append(pltpu.make_async_copy(kept[at], ref, sems.at[4 + at]))

    def block_copy(pair, span):
        return pltpu.make_async_copy(kept[5].at[:, span], weights_ref.at[:, span], sems.at[pair])

    for copy in copies:
        copy.start()
    for pair in range(4):
        block_copy(pair, slice(pair * 2 * rows, (pair + 1) * 2 * rows)).start()
    dk_sum[...] = jnp.zeros_like(dk_sum)
    dv_sum[...] = jnp.zeros_like(dv_sum)
    for copy in copies:
        copy.wait()

    @pl.loop(0, 4)
    def _(pair):
        span = pl.ds(pl.multiple_of(pair * 2 * rows, 2 * rows), 2 * rows)
        block_copy(pair, span).wait()
        first = lax.bitwise_xor(rank, 2 * pair)
        second = lax.bitwise_xor(first, 1)
        grad_all = jnp.concatenate([grad_ref[first], grad_ref[second]], axis=0)
        inverse = inverse_ref[span]
        q_scaled = (q_ref[span].astype(FULL) * inverse).astype(LOW)
        g_scaled = (grad_all.astype(FULL) * inverse).astype(LOW)
        product = grad_all.astype(FULL) * mixed_ref[span]
        for at in range(width // HEAD_DIM):
            cols = slice(at * HEAD_DIM, (at + 1) * HEAD_DIM)
            delta = jnp.sum(product[:, cols], axis=-1, keepdims=True)
            weights = weights_ref[at, span]
            dprobs = dot_rows(grad_all[:, cols], v_ref[:, cols])
            dscores = (weights.astype(FULL) * (dprobs - delta)).astype(LOW)
            dq = (dot(dscores, k_ref[:, cols]) * inverse[:, cols]).astype(LOW) * LOW(scale)
            out_ref[first, :, cols] = dq[:rows]
            out_ref[second, :, cols] = dq[rows:]
            dk_sum[cols] += dot_cols(q_scaled[:, cols], dscores)
            dv_sum[cols] += dot_cols(g_scaled[:, cols], weights)

    dk = dk_sum[...].T.astype(LOW)
    dv = dv_sum[...].T.astype(LOW)
    for at in range(8):
        whose = lax.bitwise_xor(rank, at)
        out_ref[whose, :, width : 2 * width] = dk[at * rows : (at + 1) * rows]
        out_ref[whose, :, 2 * width :] = dv[at * rows : (at + 1) * rows]


def normalize(values):
    center = values - jnp.mean(values, axis=-1, keepdims=True)
    scale = lax.rsqrt(jnp.mean(center * center, axis=-1, keepdims=True) + 1e-05)
    return center * scale, scale


def normalize_back(cotangent, gain, normed, scale):
    dn = cotangent * gain
    inner = jnp.mean(dn, axis=-1, keepdims=True)
    outer = jnp.mean(dn * normed, axis=-1, keepdims=True)
    return scale * (dn - inner - normed * outer)


def quarter_span(place, at, size):
    return pl.ds(pl.multiple_of(lax.bitwise_xor(place[1], at) * size, size), size)


def fetch_out(place, sources, held, sems):
    own = held.shape[1]
    copies = []
    for at, source in enumerate(sources):
        for part in range(2):
            start = (2 * lax.bitwise_xor(place[1], at) + part) * own
            span = pl.ds(pl.multiple_of(start, own), own)
            copies.append(
                pltpu.make_async_copy(
                    source.at[:, part], held.at[:, :, span], sems.at[2 * at + part]
                )
            )
    for copy in copies:
        copy.start()
    return copies


def mix_kernel(
    place, context_ref, tokens_ref, vec_ref, *refs
):
    sources, refs = refs[:4], refs[4:]
    middle_ref, low_ref, norm_ref, scale_ref, left_ref, out_ref, sems = refs
    copies = fetch_out(place, sources, out_ref, sems)
    own = context_ref.shape[2]
    for at in range(8):
        left_ref[:, at * own : (at + 1) * own] = context_ref[at]
    for copy in copies:
        copy.wait()
    attended = dot(left_ref[...], out_ref[...].reshape(8 * own, 8 * own))
    norm, scale = normalize(tokens_ref[...].astype(FULL) + (attended + vec_ref[6:7]))
    middle = norm * vec_ref[0:1] + vec_ref[2:3]
    middle_ref[...] = middle
    low_ref[...] = middle.astype(LOW)
    norm_ref[...] = norm
    scale_ref[...] = scale


def fetch_units(place, sources, w_in, w_out, sems, first):
    ins = [(sources[0], w_in.at[0])]
    outs = [(sources[1], w_out.at[0])]
    for at, source in enumerate(sources[2:]):
        span = quarter_span(place, at, source.shape[1])
        ins.append((source.at[0], w_in.at[1, span]))
        outs.append((source.at[1], w_out.at[1, span]))
    order = ins[:1] + outs[:1] + ins[1:] + outs[1:]
    if first == 1:
        order = outs[:1] + ins[:1] + outs[1:] + ins[1:]
    copies = [pltpu.make_async_copy(*both, sems.at[at]) for at, both in enumerate(order)]
    for copy in copies:
        copy.start()

    def wait(part, which):
        if part % 2 == 0:
            start = 2 + 4 * which if part else which
            for copy in copies[start : start + 4] if part else copies[start : start + 1]:
                copy.wait()

    return wait


def ffn_kernel(place, first_ref, second_ref, *refs):
    bias_ref, sources, refs = refs[0], refs[1:7], refs[7:]
    pre_ref, act_ref, near_ref, away_ref, sum_ref, w_in, w_out, sems = refs
    wait = fetch_units(place, sources, w_in, w_out, sems, 0)
    rows = first_ref.shape[0]
    step = bias_ref.shape[2]
    both = jnp.concatenate([first_ref[...], second_ref[...]], axis=0)
    for part in range(4):
        span = slice(part * 2 * step, (part + 1) * 2 * step)
        shard, rows_of = part // 2, slice(part % 2 * 2 * step, (part % 2 + 1) * 2 * step)
        whose = place[4] * 4 + lax.bitwise_xor(place[5], 2 * shard)
        bias = [bias_ref[whose * 4 + part % 2 * 2 + at] for at in range(2)]
        wait(part, 0)
        pre = dot_rows(both, w_in[shard, rows_of]) + jnp.concatenate(bias, axis=1)
        pre_ref[:, span] = pre
        act = (pre * (0.5 * (1.0 + lax.erf(pre * (0.5**0.5))))).astype(LOW)
        act_ref[:, span] = act
        wait(part, 1)
        term = dot(act, w_out[shard, rows_of])
        if part == 0:
            sum_ref[...] = term
        else:
            sum_ref[...] += term
    near_ref[...] = sum_ref[:rows]
    away_ref[...] = sum_ref[rows:].astype(LOW)


def ffn_back_kernel(place, first_ref, second_ref, slope_ref, *refs):
    sources, refs = refs[:6], refs[6:]
    grad_ref, near_ref, away_ref, units_ref, sum_ref, w_in, w_out, sems = refs
    wait = fetch_units(place, sources, w_in, w_out, sems, 1)
    rows = first_ref.shape[0]
    step = units_ref.shape[2]
    both = jnp.concatenate([first_ref[...], second_ref[...]], axis=0)
    for part in range(4):
        span = slice(part * 2 * step, (part + 1) * 2 * step)
        shard, rows_of = part // 2, slice(part % 2 * 2 * step, (part % 2 + 1) * 2 * step)
        wait(part, 0)
        grad = (dot_rows(both, w_out[shard, rows_of]) * slope_ref[:, span]).astype(LOW)
        grad_ref[:, span] = grad
        sums = jnp.sum(grad.astype(FULL), axis=0, keepdims=True)
        for at in range(2):
            half = lax.bitwise_xor(place[7], shard)
            units_ref[half * 4 + part % 2 * 2 + at] = sums[:, at * step : (at + 1) * step]
        wait(part, 1)
        term = dot(grad, w_in[shard, rows_of])
        if part == 0:
            sum_ref[...] = term
        else:
            sum_ref[...] += term
    near_ref[...] = sum_ref[:rows]
    away_ref[...] = sum_ref[rows:].astype(LOW)


def top_kernel(
    place, near_ref, sent_ref, far_ref, middle_ref, vec_ref, cotangent_ref,
    layer_ref, grad_ref, low_ref, sums_ref,
):
    summed = near_ref[...] + sent_ref[...].astype(FULL) + far_ref[...].astype(FULL)
    norm, scale = normalize(middle_ref[...] + summed + vec_ref[7:8])
    layer_ref[...] = norm * vec_ref[1:2] + vec_ref[3:4]
    cotangent = cotangent_ref[...].astype(FULL)
    grad = normalize_back(cotangent, vec_ref[1:2], norm, scale)
    grad_ref[...] = grad
    low_ref[...] = grad.astype(LOW)
    sums_ref[0:1] = jnp.sum(cotangent * norm, axis=0, keepdims=True)
    sums_ref[1:2] = jnp.sum(cotangent, axis=0, keepdims=True)
    sums_ref[2:3] = jnp.sum(grad.astype(LOW).astype(FULL), axis=0, keepdims=True)


def mix_back_kernel(
    place, near_ref, sent_ref, far_ref, grad_two_ref, norm_ref, scale_ref, vec_ref, *refs
):
    sources, refs = refs[:4], refs[4:]
    grad_ref, low_ref, context_ref, sums_ref, out_ref, sems = refs
    copies = fetch_out(place, sources, out_ref, sems)
    summed = near_ref[...] + sent_ref[...].astype(FULL) + far_ref[...].astype(FULL)
    grad_mid = grad_two_ref[...] + summed
    norm = norm_ref[...]
    grad = normalize_back(grad_mid, vec_ref[0:1], norm, scale_ref[...])
    grad_ref[...] = grad
    low_ref[...] = grad.astype(LOW)
    sums_ref[0:1] = jnp.sum(grad_mid * norm, axis=0, keepdims=True)
    sums_ref[1:2] = jnp.sum(grad_mid, axis=0, keepdims=True)
    sums_ref[2:3] = jnp.sum(grad.astype(LOW).astype(FULL), axis=0, keepdims=True)
    own = context_ref.shape[2]
    for copy in copies:
        copy.wait()
    total = dot_rows(low_ref[...], out_ref[...].reshape(8 * own, 8 * own)).astype(LOW)
    own = context_ref.shape[2]
    for at in range(8):
        context_ref[at] = total[:, at * own : (at + 1) * own]


def weight_grad_kernel(place, left_0, left_1, *refs):
    right, near_ref, away_ref = refs[:4], refs[4], refs[5]
    held_0, held_1, first, second, sems = refs[6:]
    rows = near_ref.shape[1]
    parts = [side.at[at * rows : (at + 1) * rows] for side in (first, second) for at in range(2)]
    for copy in fetch((left_0, left_1) + tuple(right), [held_0, held_1] + parts, sems):
        copy.wait()
    for stays in range(2):
        shard = place[6] if stays else 1 - place[6]
        for half in range(2):
            span = pl.ds(pl.multiple_of((2 * shard + half) * 2 * rows, 2 * rows), 2 * rows)
            both = dot_cols(held_0[:, span], first[...])
            both += dot_cols(held_1[:, span], second[...])
            for at in range(2):
                part = both[at * rows : (at + 1) * rows]
                slot = 2 * lax.bitwise_xor(place[3], at) + lax.bitwise_xor(place[7], half)
                if stays:
                    near_ref[slot] = part
                else:
                    away_ref[slot] = part.astype(LOW)


def out_grad_kernel(place, *refs):
    parts, grads, near_ref, away_ref, held, right, sems = refs[:4], refs[4:8], *refs[8:]
    step = near_ref.shape[1]
    rows = held.shape[2]
    sides = [right.at[at * rows : (at + 1) * rows] for at in range(4)]
    for copy in fetch(parts + grads, [held.at[at] for at in range(4)] + sides, sems):
        copy.wait()
    for stays in range(2):
        which = place[3] if stays else 1 - place[3]
        left = jnp.concatenate([held[at, which] for at in range(4)], axis=0)
        total = dot_cols(left, right[...])
        for at in range(4):
            slot = lax.bitwise_xor(place[5], at)
            if stays:
                near_ref[slot] = total[at * step : (at + 1) * step]
            else:
                away_ref[slot] = total[at * step : (at + 1) * step].astype(LOW)


def qkv_grad_kernel(place, *refs):
    grad_ref, top_ref, mid_ref, units_a, units_b = refs[:5]
    slots, refs = refs[5:13], refs[13:]
    near_ref, away_ref, total_ref, sums_ref, tokens_ref, sems = refs
    rows = grad_ref.shape[1]
    held = [tokens_ref.at[at * rows : (at + 1) * rows] for at in range(8)]
    copies = fetch(slots, held, sems)
    rank, seq_at = place[0], place[1]
    width = sums_ref.shape[1]
    own = width // 8
    quarter = width // 4
    col_sum = 0.0
    for pair in range(4):
        grads = [grad_ref[lax.bitwise_xor(rank, 2 * pair + at)] for at in range(2)]
        grads = jnp.concatenate(grads, axis=0)
        copies[2 * pair].wait()
        copies[2 * pair + 1].wait()
        term = dot_cols(tokens_ref[2 * pair * rows : 2 * (pair + 1) * rows], grads)
        col_sum += jnp.sum(grads.astype(FULL), axis=0, keepdims=True)
        if pair == 0:
            total_ref[...] = term
        else:
            total_ref[...] += term
    sums_ref[...] = jnp.zeros_like(sums_ref)
    sums_ref[0:1] = mid_ref[0:1]
    sums_ref[1:2] = top_ref[0:1]
    sums_ref[2:3] = mid_ref[1:2]
    sums_ref[3:4] = top_ref[1:2]
    own_cols = pl.ds(pl.multiple_of(rank * own, own), own)
    sums_ref[4:5, own_cols] = col_sum[:, :own]
    sums_ref[5:6, own_cols] = col_sum[:, 2 * own :]
    sums_ref[6:7] = mid_ref[2:3]
    sums_ref[7:8] = top_ref[2:3]
    row_at = lax.broadcasted_iota(jnp.int32, (8, own), 0)
    for at in (1, 3, 0, 2):
        whose = lax.bitwise_xor(seq_at, at)
        part = total_ref[quarter_span(place, at, quarter)]
        sums = sums_ref[:, quarter_span(place, at, quarter)]
        here = lax.shift_right_logical(whose, 1) == place[4]
        first = 4 * lax.bitwise_and(whose, 1)
        units = [units_a[first + row] + units_b[first + row] for row in range(4)]
        mine = (row_at >= 4 * place[8]) & (row_at < 4 * place[8] + 4)
        units = jnp.where(mine & here, jnp.concatenate(units + units, axis=0), 0.0)
        sums = jnp.concatenate([sums, units], axis=1)
        sums = jnp.concatenate([sums, jnp.zeros_like(sums)], axis=0)
        if at % 2:
            away_ref[at // 2, :quarter] = part.astype(LOW)
            away_ref[at // 2, quarter:] = sums.astype(LOW)
        else:
            near_ref[at // 2, :quarter] = part
            near_ref[at // 2, quarter:] = sums


def input_terms_kernel(place, across_ref, own_ref, *refs):
    sources, refs = refs[:5], refs[5:]
    near_ref, away_ref, cols_ref, beyond_ref, parts, sems = refs
    copies = fetch(sources, [cols_ref] + [parts.at[at] for at in range(4)], sems)
    rows = own_ref.shape[1]
    for copy in copies:
        copy.wait()
    put_columns(place, parts, beyond_ref)
    for slots in ((1, 3), (0, 2)):
        whose = [lax.bitwise_xor(place[5], slot) for slot in slots]
        left = jnp.concatenate([own_ref[place[4] * 4 + at] for at in whose], axis=0)
        term = dot_rows(left, cols_ref[...])
        left = jnp.concatenate([across_ref[at] for at in whose], axis=0)
        term += dot_rows(left, beyond_ref[...])
        for at, slot in enumerate(slots):
            part = term[at * rows : (at + 1) * rows]
            if slot % 2:
                away_ref[at] = part.astype(LOW)
            else:
                near_ref[at] = part


def qkv_send_kernel(place, near_ref, far_ref, out_ref):
    total = near_ref[...] + far_ref[...].astype(FULL)
    rows = total.shape[0] - 16
    step = rows // 8
    sums = total[rows:].astype(LOW)
    for at in range(8):
        out_ref[at, :step] = total[at * step : (at + 1) * step].astype(LOW)
        out_ref[at, step:] = sums


def qkv_last_kernel(place, parts_ref, grad_ref, sums_ref):
    step = grad_ref.shape[0]
    own = parts_ref.shape[2] // 3
    for at in range(8):
        for which in range(3):
            cols = slice((which * 8 + at) * own, (which * 8 + at + 1) * own)
            grad_ref[:, cols] = parts_ref[at, :step, which * own : (which + 1) * own].astype(FULL)
    sums = parts_ref[0, step:].astype(FULL)
    for at in range(1, 8):
        sums += parts_ref[at, step:].astype(FULL)
    sums_ref[...] = sums


def grouped_body(tokens, out_grad, w_qkv, w_out, fc_in, fc_out, fc_in_bias, vectors):
    rows, width = tokens.shape
    own = width // 8
    seq_at = lax.axis_index("seq")
    core_at, across_at = lax.rem(seq_at, 2), seq_at // 2
    head_at, blk_at = lax.axis_index("head"), lax.axis_index("blk")
    rank = head_at * 4 + blk_at
    far_at, near_at = blk_at // 2, lax.rem(blk_at, 2)
    place = jnp.stack(
        [rank, seq_at, core_at, across_at, head_at, blk_at, far_at ^ core_at, far_at, near_at]
    ).astype(jnp.int32)
    unit_rows = fc_in.shape[0] // 4
    units = 8 * unit_rows

    quarter = own // 4
    qkv_rows = lax.dynamic_slice_in_dim(w_qkv, seq_at * quarter, quarter, 0)
    qkv_rows = qkv_rows.reshape(quarter, 3, 8, own).transpose(2, 1, 0, 3)
    qkv_rows = qkv_rows.reshape(8, 3 * quarter, own)
    small = jnp.concatenate([vectors.T, fc_in_bias.reshape(-1, own)], axis=0)
    small = jnp.broadcast_to(small[None], (8, 12, own))
    to_swap = jnp.concatenate([qkv_rows, small, jnp.zeros((8, 4, own), LOW)], axis=1)
    out_quarter = lax.dynamic_slice_in_dim(w_out, seq_at * 2 * own, 2 * own, 1)
    out_quarter = out_quarter.reshape(own, 2, own).transpose(1, 0, 2).reshape(1, 2 * own, own)
    out_quarter = jnp.broadcast_to(out_quarter, (8, 2 * own, own))
    units_away = jnp.stack(
        [lax.dynamic_slice_in_dim(w, seq_at * unit_rows, unit_rows, 0) for w in (fc_in, fc_out)]
    )

    inner = inner_blk()
    first = lax.ppermute(tokens, "blk", PAIRS)
    middle = lax.ppermute(tokens, "blk", INNER)
    across_0 = flip_head(tokens)
    first, middle, across_0, to_swap = after((first, middle, across_0, to_swap))
    second_in = lax.ppermute(first, "blk", INNER)
    second_out = lax.ppermute(middle, "blk", OUTER)
    across_1 = flip_head(first)
    swapped = lax.all_to_all(to_swap, GROUP, 0, 0, tiled=True)
    second_in, second_out, across_1, swapped, out_quarter = after(
        (second_in, second_out, across_1, swapped, out_quarter)
    )
    out_quarter = lax.all_to_all(out_quarter, GROUP, 0, 0, tiled=True).reshape(8, 2, own, own)
    third = lax.ppermute(second_in, "blk", OUTER)
    second = jnp.where(inner, second_in, second_out)
    across_2 = flip_head(second)
    qkv_own = swapped[:, : 3 * quarter].reshape(8, 3, quarter, own)
    qkv_across = lax.ppermute(qkv_own, "seq", ACROSS)
    small = swapped[:, 3 * quarter : 3 * quarter + 12].astype(FULL)
    vec = small[:, :8].transpose(1, 0, 2).reshape(8, width)
    bias_all = small[:, 8:].reshape(32, 1, own)
    third, across_2, qkv_own, qkv_across = after((third, across_2, qkv_own, qkv_across))
    third = jnp.where(inner, middle, third)
    across_3 = flip_head(third)
    qkv_quarters = [qkv_own, lax.ppermute(qkv_own, "seq", CORE)]
    qkv_quarters += [qkv_across, lax.ppermute(qkv_across, "seq", CORE)]
    across_3, out_quarter, units_away, *qkv_quarters = after(
        [across_3, out_quarter, units_away] + qkv_quarters
    )
    beyond = flip_head(qkv_quarters[0])
    slots = [tokens, first, second, third, across_0, across_1, across_2, across_3]

    units_two_on = lax.ppermute(units_away, "blk", TWO_ON)
    bias = vectors.T.reshape(8, 1, own)[4:6].astype(FULL)
    seq_rows = 8 * rows
    heads = own // HEAD_DIM
    kept_shapes = [((seq_rows, own), LOW)] * 3 + [((seq_rows, own), FULL)] * 2
    kept_shapes.append(((width, 3 * own), LOW))
    kept_shapes.append(((heads, seq_rows, seq_rows), LOW))
    kept_scratch = [pltpu.VMEM(*shape) for shape in kept_shapes]
    context, *kept = call(
        attend_kernel,
        [shape_of((8, rows, own), LOW)] + [shape_of(*shape) for shape in kept_shapes],
        place, bias, *qkv_quarters, *slots,
        scratch=kept_scratch
        + [pltpu.VMEM((seq_rows, width), LOW), pltpu.VMEM((4, 8, 3, quarter, own), LOW)]
        + [pltpu.SemaphoreType.DMA((16,)), pltpu.SemaphoreType.DMA((12,))],
        flops=8 * 10**9,
        far_in=12,
        far_out=7,
        vmem=56,
    )
    out_across = lax.ppermute(out_quarter, "seq", ACROSS)
    context, out_across, out_quarter = after((context, out_across, out_quarter))
    out_slots = [out_quarter, lax.ppermute(out_quarter, "seq", CORE)]
    out_slots += [out_across, lax.ppermute(out_across, "seq", CORE)]
    context = lax.all_to_all(context, GROUP, 0, 0, tiled=True)
    beyond = after(beyond, *out_slots[1:])
    beyond_across = lax.ppermute(beyond, "seq", ACROSS)
    beyond_quarters = [beyond, lax.ppermute(beyond, "seq", CORE)]
    beyond_quarters += [beyond_across, lax.ppermute(beyond_across, "seq", CORE)]
    ffn_weights = [fc_in, fc_out] + gather_seq(units_two_on)
    out_scratch = [pltpu.VMEM((8, own, width), LOW), pltpu.SemaphoreType.DMA((8,))]

    per_row = shape_of((rows, width), FULL)
    per_row_low = shape_of((rows, width), LOW)
    middle, middle_low, norm_one, scale_one = call(
        mix_kernel,
        [per_row, per_row_low, per_row, shape_of((rows, 1), FULL)],
        place, context, tokens, vec, *out_slots,
        scratch=[pltpu.VMEM((rows, width), LOW)] + out_scratch,
        flops=2 * 10**9,
        far_in=4,
    )

    both_rows = shape_of((2 * rows, units), FULL)
    both_rows_low = shape_of((2 * rows, units), LOW)
    middle_slots = gather_four(middle_low)
    ffn_scratch = [pltpu.VMEM((2 * rows, width), FULL)]
    ffn_scratch += [pltpu.VMEM((2, 4 * unit_rows, width), LOW)] * 2
    ffn_scratch += [pltpu.SemaphoreType.DMA((10,))]
    ffn_parts = []
    for at in (0, 2):
        ffn_parts.append(
            call(
                ffn_kernel,
                [both_rows, both_rows_low, per_row, per_row_low],
                place, middle_slots[at], middle_slots[at + 1], bias_all, *ffn_weights,
                scratch=ffn_scratch,
                flops=3 * 10**9,
                far_in=6,
            )
        )

    def features_of(core, head):
        both = lax.dynamic_index_in_dim(context.reshape(2, 2, 2, rows, own), core, 1, False)
        return lax.dynamic_index_in_dim(both, head, 1, False)

    diagonal = []
    for seq in range(4):
        for head in range(2):
            diagonal.append((seq * 2 + head, (seq ^ 1) * 2 + 1 - head))
    parts = [
        features_of(core_at, head_at),
        features_of(1 - core_at, head_at),
        features_of(core_at, 1 - head_at),
        features_of(1 - core_at, 1 - head_at),
    ]
    parts[1:] = after(parts[1:], ffn_parts[0][1])
    parts = [
        parts[0],
        lax.ppermute(parts[1], "seq", CORE),
        flip_head(parts[2]),
        lax.ppermute(parts[3], ("seq", "head"), tuple(diagonal)),
    ]

    def scatter_parts(near_part, far_part):
        sent_far = lax.ppermute(far_part[1], "blk", PAIRS).astype(FULL)
        far = flip_head((far_part[0] + sent_far).astype(LOW))
        return near_part[0], lax.ppermute(near_part[1], "blk", PAIRS), far

    weight_scratch = [pltpu.VMEM((2 * rows, units), LOW)] * 2
    weight_scratch += [pltpu.VMEM((2 * rows, width), LOW)] * 2 + [pltpu.SemaphoreType.DMA((6,))]
    terms = [shape_of((4, unit_rows, width), FULL), shape_of((4, unit_rows, width), LOW)]

    def weight_grads(lefts, rights):
        return call(
            weight_grad_kernel, terms, place, *lefts, *rights,
            scratch=weight_scratch, flops=2 * 10**9, far_in=6,
        )

    def add_low(near, sent):
        return near + sent.astype(FULL)

    summed = scatter_parts(ffn_parts[0][2:4], ffn_parts[1][2:4])
    three_sums = shape_of((3, width), FULL)
    layer_output, grad_two, grad_ffn, top_sums = call(
        top_kernel,
        [per_row, per_row, per_row_low, three_sums],
        place, *summed, middle, vec, out_grad,
        flops=10**9,
    )

    grad_ffn_slots = gather_four(grad_ffn)
    back_parts = []
    for at in (0, 2):
        pre = ffn_parts[at // 2][0]
        cdf = 0.5 * (1.0 + lax.erf(pre * (0.5**0.5)))
        slope = cdf + pre * jnp.exp(-0.5 * pre * pre) * ((2.0 * math.pi) ** -0.5)
        back_parts.append(
            call(
                ffn_back_kernel,
                [both_rows_low, per_row, per_row_low, shape_of((8, 1, unit_rows), FULL)],
                place, grad_ffn_slots[at], grad_ffn_slots[at + 1], slope, *ffn_weights,
                scratch=ffn_scratch,
                flops=3 * 10**9,
                far_in=6,
            )
        )
    summed = scatter_parts(back_parts[0][1:3], back_parts[1][1:3])
    summed = after(summed, *beyond_quarters)
    acts = after((ffn_parts[0][1], ffn_parts[1][1]), back_parts[1][0])
    out_near_grad, out_away_grad = weight_grads(acts, grad_ffn_slots)
    out_sent = lax.ppermute(out_away_grad, "seq", CORE)
    summed = after(summed, out_sent)
    grad_one, grad_attn, grad_context, mid_sums = call(
        mix_back_kernel,
        [per_row, per_row_low, shape_of((8, rows, own), LOW), three_sums],
        place, *summed, grad_two, norm_one, scale_one, vec, *out_slots,
        scratch=out_scratch,
        flops=2 * 10**9,
        far_in=4,
    )
    grad_context = lax.all_to_all(grad_context, GROUP, 0, 0, tiled=True)
    out_across = lax.ppermute(
        add_low(out_near_grad[2:], out_sent[2:]).astype(LOW), "seq", ACROSS
    )
    in_near_grad, in_away_grad = weight_grads((back_parts[0][0], back_parts[1][0]), middle_slots)
    in_sent = lax.ppermute(in_away_grad, "seq", CORE)
    attn_across = flip_head(grad_attn)

    def kept_here(near, sent, across, at):
        return add_low(near[at] + sent[at].astype(FULL), across[at])

    in_across = add_low(in_near_grad[2:], in_sent[2:]).astype(LOW)
    out_last = kept_here(out_near_grad, out_sent, out_across, 1).astype(LOW)
    grad_context, in_across, out_last, attn_across = after(
        (grad_context, in_across, out_last, attn_across)
    )
    in_across = lax.ppermute(in_across, "seq", ACROSS)
    out_last = lax.ppermute(out_last, "blk", TWO_ON)
    grad_attn_slots = [grad_attn, lax.ppermute(grad_attn, "seq", CORE)]
    grad_attn_slots += [attn_across, lax.ppermute(attn_across, "seq", CORE)]
    (grad_cols,) = call(
        attend_back_kernel,
        [shape_of((8, rows, 3 * own), LOW)],
        place, grad_context, *kept[:5], kept[6],
        scratch=kept_scratch[:5]
        + kept_scratch[6:]
        + [pltpu.VMEM((own, seq_rows), FULL)] * 2
        + [pltpu.SemaphoreType.DMA((9,))],
        flops=8 * 10**9,
        far_in=6,
        vmem=56,
    )

    cols_sent = lax.dynamic_slice_in_dim(grad_cols, (1 - head_at) * 4, 4, 0)
    cols_sent = flip_head(cols_sent)
    in_last = kept_here(in_near_grad, in_sent, in_across, 1).astype(LOW)
    in_last = lax.ppermute(in_last, "blk", TWO_ON)
    payload_rows = 2 * own + 16
    near, away = call(
        qkv_grad_kernel,
        [shape_of((2, payload_rows, 3 * own), FULL), shape_of((2, payload_rows, 3 * own), LOW)],
        place, grad_cols, top_sums, mid_sums, back_parts[0][3], back_parts[1][3], *slots,
        scratch=[pltpu.VMEM((width, 3 * own), FULL), pltpu.VMEM((8, width), FULL)]
        + [pltpu.VMEM((seq_rows, width), LOW), pltpu.SemaphoreType.DMA((8,))],
        flops=2 * 10**9,
        far_in=8,
    )
    sent = lax.ppermute(away, "seq", CORE)
    near_terms, away_terms = call(
        input_terms_kernel,
        [
            shape_of((2, rows, width), FULL),
            shape_of((2, rows, width), LOW),
        ],
        place, cols_sent, grad_cols, kept[5], *beyond_quarters,
        scratch=[pltpu.VMEM((width, 3 * own), LOW)] * 2
        + [pltpu.VMEM((4, 8, 3, quarter, own), LOW), pltpu.SemaphoreType.DMA((5,))],
        flops=2 * 10**9,
        far_in=5,
    )
    sent_terms = lax.ppermute(away_terms, "blk", PAIRS)
    out_terms = [shape_of((4, own // 4, width), FULL), shape_of((4, own // 4, width), LOW)]
    near_rows, away_rows = call(
        out_grad_kernel, out_terms, place, *parts, *after(grad_attn_slots, away_terms),
        scratch=[pltpu.VMEM((4, 2, rows, own), LOW), pltpu.VMEM((4 * rows, width), LOW)]
        + [pltpu.SemaphoreType.DMA((8,))],
        flops=10**9,
        far_in=8,
    )
    sent_rows = lax.ppermute(away_rows, "seq", ACROSS)

    last_terms = after(add_low(near_terms[1], sent_terms[1]).astype(LOW), in_last)
    last_terms = lax.ppermute(last_terms, "blk", TWO_ON)
    out_rows = add_low(near_rows, sent_rows)
    sent_rows = lax.ppermute(out_rows.reshape(2, 2, -1, width)[:, 1].astype(LOW), "blk", PAIRS)
    last_rows = lax.ppermute(add_low(out_rows[2], sent_rows[1]).astype(LOW), "blk", TWO_ON)
    grad_w_out = add_low(add_low(out_rows[0], sent_rows[0]), last_rows)
    far = lax.ppermute(add_low(near[1], sent[1]).astype(LOW), "seq", ACROSS)
    unit_grads = jnp.stack(
        [
            add_low(kept_here(in_near_grad, in_sent, in_across, 0), in_last),
            add_low(kept_here(out_near_grad, out_sent, out_across, 0), out_last),
        ]
    )
    (payload,) = call(
        qkv_send_kernel,
        [shape_of((8, own // 4 + 16, 3 * own), LOW)],
        place, add_low(near[0], sent[0]), far,
    )
    payload = lax.all_to_all(payload, GROUP, 0, 0, tiled=True)
    input_grad = grad_one + add_low(add_low(near_terms[0], sent_terms[0]), last_terms)

    moves = []
    for across in range(2):
        for core in range(2):
            for head in range(2):
                for two_on in range(2):
                    for near_by in range(2):
                        start = (across * 2 + core) * 8 + head * 4 + two_on * 2 + near_by
                        stop = (head * 2 + core) * 8 + near_by * 4 + two_on * 2 + across
                        if start != stop:
                            moves.append((start, stop))
    stays = (across_at == head_at) & (head_at == near_at)

    moved = lax.ppermute(unit_grads.astype(LOW), ("seq", "head", "blk"), moves).astype(FULL)
    grad_fc_in, grad_fc_out = jnp.where(stays, unit_grads, moved)

    grad_w_qkv, sums = call(
        qkv_last_kernel,
        [shape_of((own // 4, 3 * width), FULL), shape_of((16, 3 * own), FULL)],
        place, payload,
    )
    grad_vectors = lax.dynamic_slice(sums, (0, rank * (own // 4)), (8, own // 4)).T
    grad_bias = lax.dynamic_slice(sums, (rank, 2 * own), (1, own)).reshape(own)
    return (
        layer_output,
        input_grad,
        grad_w_qkv,
        grad_w_out,
        grad_fc_in,
        grad_fc_out,
        grad_bias,
        grad_vectors,
    )


def solution(mesh):
    sizes = tuple(mesh.shape[name] for name in ("seq", "head", "blk"))
    return jax.shard_map(
        grouped_body if sizes == (4, 2, 4) else general_body,
        mesh=mesh,
        in_specs=(
            P(("seq", "head", "blk"), None),
            P(("seq", "head", "blk"), None),
            P(("head", "blk"), None),
            P(("head", "blk"), None),
            P(("head", "blk"), None),
            P(("head", "blk"), None),
            P(("head", "blk")),
            P(("head", "blk"), None),
        ),
        out_specs=(
            P(("seq", "head", "blk"), None),
            P(("seq", "head", "blk"), None),
            P(("seq", "head", "blk"), None),
            P(("seq", "head", "blk"), None),
            P(("seq", "head", "blk"), None),
            P(("seq", "head", "blk"), None),
            P(("seq", "head", "blk")),
            P(("seq", "head", "blk"), None),
        ),
        check_vma=False,
    )
```

```python
import math

import jax
import jax.numpy as jnp
from jax import lax
from jax.experimental import pallas as pl
from jax.experimental.pallas import tpu as pltpu
from jax.sharding import PartitionSpec as P

HEAD_DIM = 64


def layer_norm(values, gain_vec, shift_vec):
    center = values - jnp.mean(values, axis=-1, keepdims=True)
    spread = jnp.mean(center * center, axis=-1, keepdims=True)
    return center * lax.rsqrt(spread + 1e-05) * gain_vec + shift_vec


def gelu_exact(values):
    return jax.nn.gelu(values, approximate=False)


def split_heads(values):
    return values.reshape(values.shape[0], values.shape[1] // HEAD_DIM, HEAD_DIM)


def head_scores(left_rows, right_rows):
    return jnp.einsum("qhd,khd->hqk", left_rows, right_rows, preferred_element_type=jnp.float32)


def ffn_part(factors):
    middle_low, grad_pre_full, act_full, grad_ffn = factors
    return jnp.concatenate(
        [
            jnp.einsum("tf,td->fd", grad_pre_full, middle_low, preferred_element_type=jnp.float32),
            jnp.einsum("tf,td->fd", act_full, grad_ffn, preferred_element_type=jnp.float32),
        ],
        axis=1,
    )


def attn_part(factors, extra_cols):
    tokens, grad_proj, context, grad_attn = factors
    return jnp.concatenate(
        [
            jnp.einsum("tn,tc->nc", tokens, grad_proj, preferred_element_type=jnp.float32),
            jnp.einsum("tn,tc->nc", context, grad_attn, preferred_element_type=jnp.float32),
            extra_cols,
        ],
        axis=1,
    )


def general_body(tokens, out_grad, w_qkv, w_out, fc_in, fc_out, fc_in_bias, vectors):
    model_width = tokens.shape[1]
    hidden_units = fc_in.shape[0] * lax.axis_size(("head", "blk"))
    ratio = hidden_units // model_width
    scale = HEAD_DIM ** (-0.5)
    part_qkv = lax.all_gather(w_qkv, ("head", "blk"), axis=0, tiled=True)
    part_out = lax.all_gather(w_out, ("head", "blk"), axis=0, tiled=True)
    part_vec = lax.all_gather(vectors, ("head", "blk"), axis=0, tiled=True)
    part_rows = part_qkv.shape[0]
    projected = jnp.dot(tokens, part_qkv, preferred_element_type=jnp.float32)
    out_full = part_out
    attn_state = (projected, out_full, part_vec)
    projected = attn_state[0]
    out_full = attn_state[1]
    vec_float = attn_state[2].astype(jnp.float32)
    gain_one, gain_two = (vec_float[:, 0], vec_float[:, 1])
    shift_one, shift_two = (vec_float[:, 2], vec_float[:, 3])
    bias_query, bias_value = (vec_float[:, 4], vec_float[:, 5])
    bias_output, bias_ffn = (vec_float[:, 6], vec_float[:, 7])
    queries = ((projected[:, :model_width] + bias_query) * scale).astype(jnp.bfloat16)
    key_rows = projected[:, model_width : 2 * model_width].astype(jnp.bfloat16)
    value_rows = (projected[:, 2 * model_width :] + bias_value).astype(jnp.bfloat16)
    query_heads, key_heads, value_heads = (
        lax.all_to_all(queries, "head", split_axis=1, concat_axis=0, tiled=True),
        lax.all_to_all(key_rows, "head", split_axis=1, concat_axis=0, tiled=True),
        lax.all_to_all(value_rows, "head", split_axis=1, concat_axis=0, tiled=True),
    )
    query_split = split_heads(query_heads)
    group_rows = query_split.shape[0]
    group_width = key_heads.shape[1]
    seq_rows = group_rows * lax.axis_size("blk")
    portion = (
        lax.all_gather(key_heads, "blk", axis=0, tiled=True),
        lax.all_gather(value_heads, "blk", axis=0, tiled=True),
    )
    scores = head_scores(query_split, split_heads(portion[0]))
    run_sum = jnp.sum(jnp.exp(scores), axis=-1)
    key_all = portion[0]
    value_all = portion[1]
    run_sum, key_all, value_all = (run_sum, key_all, value_all)
    log_total = jnp.log(run_sum)
    block_rows = math.gcd(512, seq_rows)
    block_count = seq_rows // block_rows
    key_blocks = key_all.reshape(block_count, block_rows, group_width)
    value_blocks = value_all.reshape(block_count, block_rows, group_width)

    def mix_block(totals, pair):
        scores = head_scores(query_split, split_heads(pair[0]))
        probs_low = jnp.exp(scores - log_total[:, :, None]).astype(jnp.bfloat16)
        return (
            totals
            + jnp.einsum(
                "hqk,khd->qhd", probs_low, split_heads(pair[1]), preferred_element_type=jnp.float32
            ),
            None,
        )

    mixed, unused = lax.scan(
        mix_block, jnp.zeros(query_split.shape, jnp.float32), (key_blocks, value_blocks)
    )
    context = lax.all_to_all(
        mixed.reshape(group_rows, -1).astype(jnp.bfloat16),
        "head",
        split_axis=0,
        concat_axis=1,
        tiled=True,
    )
    attn_out = jnp.dot(context, out_full, preferred_element_type=jnp.float32) + bias_output
    residual_one = tokens.astype(jnp.float32) + attn_out
    middle, norm_one_back = jax.vjp(layer_norm, residual_one, gain_one, shift_one)
    middle_low = middle.astype(jnp.bfloat16)
    part_in = lax.all_gather(fc_in, ("head", "blk"), axis=0, tiled=True)
    part_out = lax.all_gather(fc_out, ("head", "blk"), axis=0, tiled=True)
    part_bias = lax.all_gather(fc_in_bias, ("head", "blk"), axis=0, tiled=True)
    pre_part = jnp.einsum("td,fd->tf", middle_low, part_in, preferred_element_type=jnp.float32)
    pre_part = pre_part + part_bias.astype(jnp.float32)
    act_part = gelu_exact(pre_part).astype(jnp.bfloat16)
    summed = jnp.dot(act_part, part_out, preferred_element_type=jnp.float32)
    ffn_pre_full = pre_part
    residual_two = middle + summed + bias_ffn
    layer_output, norm_two_back = jax.vjp(layer_norm, residual_two, gain_two, shift_two)
    grad_resid_two, grad_gain_two, grad_shift_two = norm_two_back(out_grad.astype(jnp.float32))
    grad_ffn = grad_resid_two.astype(jnp.bfloat16)
    qkv_flat = w_qkv.reshape(fc_in.shape[0], -1)
    portion = (
        lax.all_gather(fc_in, ("head", "blk"), axis=0, tiled=True),
        lax.all_gather(fc_out, ("head", "blk"), axis=0, tiled=True),
        lax.all_gather(qkv_flat, ("head", "blk"), axis=0, tiled=True),
    )
    part_in = portion[0]
    part_rows = part_in.shape[0]
    pre_part = ffn_pre_full
    grad_act = jnp.einsum("td,fd->tf", grad_ffn, portion[1], preferred_element_type=jnp.float32)
    grad_pre = jax.vjp(gelu_exact, pre_part)[1](grad_act)[0].astype(jnp.bfloat16)
    grad_mid = jnp.dot(grad_pre, part_in, preferred_element_type=jnp.float32)
    grad_mid, grad_pre_all = (grad_mid, grad_pre)
    qkv_gathered = portion[2]
    qkv_full = qkv_gathered.reshape(model_width, 3 * model_width)
    grad_resid_one, grad_gain_one, grad_shift_one = norm_one_back(grad_resid_two + grad_mid)
    grad_attn = grad_resid_one.astype(jnp.bfloat16)
    grad_context = jnp.einsum(
        "td,ed->te", grad_attn, out_full, preferred_element_type=jnp.float32
    ).astype(jnp.bfloat16)
    grad_ctx_heads = lax.all_to_all(grad_context, "head", split_axis=1, concat_axis=0, tiled=True)
    grad_ctx_split = split_heads(grad_ctx_heads)
    delta_heads = jnp.sum(grad_ctx_split.astype(jnp.float32) * mixed, axis=-1).T

    def back_block(grad_query, pair):
        key_part = split_heads(pair[0])
        value_part = split_heads(pair[1])
        scores = head_scores(query_split, key_part)
        probs = jnp.exp(scores - log_total[:, :, None])
        dprobs = head_scores(grad_ctx_split, value_part)
        dscores = (probs * (dprobs - delta_heads[:, :, None])).astype(jnp.bfloat16)
        grad_query = grad_query + jnp.einsum(
            "hqk,khd->qhd", dscores, key_part, preferred_element_type=jnp.float32
        )
        grad_key = jnp.einsum(
            "hqk,qhd->khd", dscores, query_split, preferred_element_type=jnp.float32
        )
        grad_value = jnp.einsum(
            "hqk,qhd->khd",
            probs.astype(jnp.bfloat16),
            grad_ctx_split,
            preferred_element_type=jnp.float32,
        )
        part_rows = pair[0].shape[0]
        return (
            grad_query,
            jnp.concatenate(
                [grad_key.reshape(part_rows, -1), grad_value.reshape(part_rows, -1)], axis=1
            ),
        )

    grad_query_heads, kv_terms = lax.scan(
        back_block, jnp.zeros(query_split.shape, jnp.float32), (key_blocks, value_blocks)
    )
    kv_own = lax.psum_scatter(
        kv_terms.reshape(seq_rows, 2 * group_width).astype(jnp.bfloat16),
        "blk",
        scatter_dimension=0,
        tiled=True,
    ).astype(jnp.float32)
    grad_query_tok, grad_key_tok, grad_value_tok = (
        lax.all_to_all(
            grad_query_heads.reshape(group_rows, -1).astype(jnp.bfloat16),
            "head",
            split_axis=0,
            concat_axis=1,
            tiled=True,
        ),
        lax.all_to_all(
            kv_own[:, :group_width].astype(jnp.bfloat16),
            "head",
            split_axis=0,
            concat_axis=1,
            tiled=True,
        ),
        lax.all_to_all(
            kv_own[:, group_width:].astype(jnp.bfloat16),
            "head",
            split_axis=0,
            concat_axis=1,
            tiled=True,
        ),
    )
    grad_proj = jnp.concatenate(
        [grad_query_tok * jnp.bfloat16(scale), grad_key_tok, grad_value_tok], axis=1
    )
    through_proj = jnp.einsum("tc,nc->tn", grad_proj, qkv_full, preferred_element_type=jnp.float32)
    input_grad = grad_resid_one + through_proj
    grad_proj_float = grad_proj.astype(jnp.float32)
    vec_term = jnp.stack(
        [
            grad_gain_one,
            grad_gain_two,
            grad_shift_one,
            grad_shift_two,
            jnp.sum(grad_proj_float[:, :model_width], axis=0),
            jnp.sum(grad_proj_float[:, 2 * model_width :], axis=0),
            jnp.sum(grad_attn.astype(jnp.float32), axis=0),
            jnp.sum(grad_ffn.astype(jnp.float32), axis=0),
        ],
        axis=1,
    )
    bias_term = jnp.sum(grad_pre_all.astype(jnp.float32), axis=0).reshape(model_width, -1)
    bias_cols = bias_term.shape[1]
    padding = jnp.zeros((model_width, 128 - 8 - bias_cols), jnp.float32)
    extra_cols = jnp.concatenate([vec_term, bias_term, padding], axis=1)
    rows_dev = hidden_units // lax.axis_size(("seq", "head", "blk"))
    ffn_block = ffn_part((middle_low, grad_pre_all, act_part, grad_ffn))
    attn_block = attn_part((tokens, grad_proj, context, grad_attn), extra_cols)
    merged = lax.psum_scatter(
        jnp.concatenate(
            [ffn_block, attn_block.reshape(lax.axis_size(("seq", "head", "blk")) * rows_dev, -1)],
            axis=1,
        ),
        ("seq", "head", "blk"),
        scatter_dimension=0,
        tiled=True,
    )
    grad_fc_in = merged[:, :model_width]
    grad_fc_out = merged[:, model_width : 2 * model_width]
    attn_grad = merged[:, 2 * model_width :].reshape(rows_dev // ratio, 4 * model_width + 128)
    grad_w_qkv = attn_grad[:, : 3 * model_width]
    grad_w_out = attn_grad[:, 3 * model_width : 4 * model_width]
    grad_vectors = attn_grad[:, 4 * model_width : 4 * model_width + 8]
    grad_fc_in_bias = attn_grad[:, 4 * model_width + 8 : 4 * model_width + 8 + bias_cols].reshape(
        -1
    )
    return (
        layer_output,
        input_grad,
        grad_w_qkv,
        grad_w_out,
        grad_fc_in,
        grad_fc_out,
        grad_fc_in_bias,
        grad_vectors,
    )


GROUP = ("head", "blk")
FLIP = ((0, 1), (1, 0))
PAIRS = ((0, 1), (1, 0), (2, 3), (3, 2))
INNER = ((1, 2), (2, 1))
OUTER = ((1, 0), (2, 3))
INWARD = ((0, 1), (3, 2))
TWO_ON = ((0, 2), (2, 0), (1, 3), (3, 1))
CORE = tuple((at, at ^ 1) for at in range(4))
ACROSS = tuple((at, at ^ 2) for at in range(4))
LOW = jnp.bfloat16
FULL = jnp.float32
ROWS_DIMS = (((1,), (1,)), ((), ()))
COLS_DIMS = (((0,), (0,)), ((), ()))


def dot(left, right):
    return jnp.dot(left, right, preferred_element_type=FULL)


def dot_rows(left, right):
    return lax.dot_general(left, right, ROWS_DIMS, preferred_element_type=FULL)


def dot_cols(left, right):
    return lax.dot_general(left, right, COLS_DIMS, preferred_element_type=FULL)


def after(values, *others):
    if not isinstance(values, (list, tuple)):
        return lax.optimization_barrier((values,) + others)[0]
    return lax.optimization_barrier(tuple(values) + others)[: len(values)]


def inner_blk():
    at = lax.axis_index("blk")
    return (at == 1) | (at == 2)


def flip_head(value):
    return lax.ppermute(value, "head", FLIP)


def gather_seq(own):
    across = lax.ppermute(own, "seq", ACROSS)
    return [own, lax.ppermute(own, "seq", CORE), across, lax.ppermute(across, "seq", CORE)]


def gather_four(own):
    across = flip_head(own)
    beside = lax.ppermute(own, "blk", PAIRS)
    return [own, beside, across, lax.ppermute(across, "blk", PAIRS)]


def gather_cores(own):
    across = flip_head(own)
    return [own, lax.ppermute(own, "seq", CORE), across, lax.ppermute(across, "seq", CORE)]


def shape_of(shape, dtype):
    return jax.ShapeDtypeStruct(shape, dtype)


def call(kernel, outs, place, *args, scratch=(), flops=0, vmem=28, far_in=0, far_out=0):
    moved = sum(arg.size * arg.dtype.itemsize for arg in args)
    moved += sum(math.prod(out.shape) * jnp.dtype(out.dtype).itemsize for out in outs)
    near = pl.BlockSpec(memory_space=pltpu.VMEM)
    far = pl.BlockSpec(memory_space=pltpu.HBM)
    return pl.pallas_call(
        kernel,
        out_shape=outs,
        in_specs=[pl.BlockSpec(memory_space=pltpu.SMEM)]
        + [near] * (len(args) - far_in)
        + [far] * far_in,
        out_specs=[near] * (len(outs) - far_out) + [far] * far_out,
        scratch_shapes=scratch,
        compiler_params=pltpu.CompilerParams(vmem_limit_bytes=vmem * 2**20),
        cost_estimate=pl.CostEstimate(flops=flops // 2, bytes_accessed=moved, transcendentals=0),
    )(place, *args)


def fetch(sources, held, sems):
    copies = [pltpu.make_async_copy(*both, sems.at[at]) for at, both in enumerate(zip(sources, held))]
    for copy in copies:
        copy.start()
    return copies


def put_columns(place, parts, cols_ref):
    step, width = parts.shape[3:]
    for at in range(8):
        for part in range(4):
            start = (4 * at + lax.bitwise_xor(place[1], part)) * step
            span = pl.ds(pl.multiple_of(start, step), step)
            for which in range(3):
                cols_ref[span, which * width : (which + 1) * width] = parts[part, at, which]


def attend_kernel(place, *refs):
    bias_ref, refs = refs[0], refs[1:]
    quarters, slots, refs = refs[:4], refs[4:12], refs[12:]
    context_ref, kept, refs = refs[0], refs[1:8], refs[8:]
    q_ref, k_ref, v_ref, mixed_ref, inverse_ref, cols_ref, weights_ref, tokens_ref = refs[:8]
    parts, sems, slot_sems = refs[8], refs[9], refs[10]
    rank = place[0]
    width = q_ref.shape[1]
    rows = context_ref.shape[1]
    step = parts.shape[3]
    spans = [slice(pair * 2 * rows, (pair + 1) * 2 * rows) for pair in range(4)]
    fetched = fetch(quarters, [parts.at[at] for at in range(4)], slot_sems)
    held = [tokens_ref.at[at * rows : (at + 1) * rows] for at in range(8)]
    fetched_slots = fetch(slots, held, slot_sems.at[4:12])
    for copy in fetched:
        copy.wait()
    put_columns(place, parts, cols_ref)
    scale = HEAD_DIM ** (-0.5)
    for pair, span in enumerate(spans):
        fetched_slots[2 * pair].wait()
        fetched_slots[2 * pair + 1].wait()
        projected = dot(tokens_ref[span], cols_ref[...])
        q_ref[span] = ((projected[:, :width] + bias_ref[0]) * scale).astype(LOW)
        k_ref[span] = projected[:, width : 2 * width].astype(LOW)
        v_ref[span] = (projected[:, 2 * width :] + bias_ref[1]).astype(LOW)
    copies = []
    for at, ref in enumerate((q_ref, k_ref, v_ref, cols_ref)):
        copies.append(pltpu.make_async_copy(ref, kept[at + 2 * (at == 3)], sems.at[12 + at]))
    for copy in copies:
        copy.start()

    def block_copies(pair, span):
        pairs = (
            (mixed_ref.at[span], kept[3].at[span]),
            (inverse_ref.at[span], kept[4].at[span]),
            (weights_ref.at[:, span], kept[6].at[:, span]),
        )
        return [
            pltpu.make_async_copy(*both, sems.at[pair + 4 * at]) for at, both in enumerate(pairs)
        ]

    @pl.loop(0, 4)
    def _(pair):
        span = pl.ds(pl.multiple_of(pair * 2 * rows, 2 * rows), 2 * rows)
        for at in range(width // HEAD_DIM):
            cols = slice(at * HEAD_DIM, (at + 1) * HEAD_DIM)
            scores = dot_rows(q_ref[span, cols], k_ref[:, cols])
            weights = jnp.exp(scores - jnp.max(scores, axis=-1, keepdims=True))
            inverse = 1.0 / jnp.sum(weights, axis=-1, keepdims=True)
            weights = weights.astype(LOW)
            weights_ref[at, span] = weights
            mixed_ref[span, cols] = dot(weights, v_ref[:, cols]) * inverse
            inverse_ref[span, cols] = jnp.broadcast_to(inverse, (2 * rows, HEAD_DIM))
        first = lax.bitwise_xor(rank, 2 * pair)
        mixed = mixed_ref[span].astype(LOW)
        context_ref[first] = mixed[:rows]
        context_ref[lax.bitwise_xor(first, 1)] = mixed[rows:]
        for copy in block_copies(pair, span):
            copy.start()

    for pair, span in enumerate(spans):
        copies += block_copies(pair, span)
    for copy in copies:
        copy.wait()


def attend_back_kernel(place, grad_ref, *refs):
    kept, refs = refs[:6], refs[6:]
    out_ref, q_ref, k_ref, v_ref, mixed_ref, inverse_ref, weights_ref = refs[:7]
    dk_sum, dv_sum, sems = refs[7:]
    rank = place[0]
    rows, width = grad_ref.shape[1:]
    scale = HEAD_DIM ** (-0.5)
    copies = []
    for at, ref in enumerate((q_ref, k_ref, v_ref, mixed_ref, inverse_ref)):
        copies.append(pltpu.make_async_copy(kept[at], ref, sems.at[4 + at]))

    def block_copy(pair, span):
        return pltpu.make_async_copy(kept[5].at[:, span], weights_ref.at[:, span], sems.at[pair])

    for copy in copies:
        copy.start()
    for pair in range(4):
        block_copy(pair, slice(pair * 2 * rows, (pair + 1) * 2 * rows)).start()
    dk_sum[...] = jnp.zeros_like(dk_sum)
    dv_sum[...] = jnp.zeros_like(dv_sum)
    for copy in copies:
        copy.wait()

    @pl.loop(0, 4)
    def _(pair):
        span = pl.ds(pl.multiple_of(pair * 2 * rows, 2 * rows), 2 * rows)
        block_copy(pair, span).wait()
        first = lax.bitwise_xor(rank, 2 * pair)
        second = lax.bitwise_xor(first, 1)
        grad_all = jnp.concatenate([grad_ref[first], grad_ref[second]], axis=0)
        inverse = inverse_ref[span]
        q_scaled = (q_ref[span].astype(FULL) * inverse).astype(LOW)
        g_scaled = (grad_all.astype(FULL) * inverse).astype(LOW)
        product = grad_all.astype(FULL) * mixed_ref[span]
        for at in range(width // HEAD_DIM):
            cols = slice(at * HEAD_DIM, (at + 1) * HEAD_DIM)
            delta = jnp.sum(product[:, cols], axis=-1, keepdims=True)
            weights = weights_ref[at, span]
            dprobs = dot_rows(grad_all[:, cols], v_ref[:, cols])
            dscores = (weights.astype(FULL) * (dprobs - delta)).astype(LOW)
            dq = (dot(dscores, k_ref[:, cols]) * inverse[:, cols]).astype(LOW) * LOW(scale)
            out_ref[first, :, cols] = dq[:rows]
            out_ref[second, :, cols] = dq[rows:]
            dk_sum[cols] += dot_cols(q_scaled[:, cols], dscores)
            dv_sum[cols] += dot_cols(g_scaled[:, cols], weights)

    dk = dk_sum[...].T.astype(LOW)
    dv = dv_sum[...].T.astype(LOW)
    for at in range(8):
        whose = lax.bitwise_xor(rank, at)
        out_ref[whose, :, width : 2 * width] = dk[at * rows : (at + 1) * rows]
        out_ref[whose, :, 2 * width :] = dv[at * rows : (at + 1) * rows]


def normalize(values):
    center = values - jnp.mean(values, axis=-1, keepdims=True)
    scale = lax.rsqrt(jnp.mean(center * center, axis=-1, keepdims=True) + 1e-05)
    return center * scale, scale


def normalize_back(cotangent, gain, normed, scale):
    dn = cotangent * gain
    inner = jnp.mean(dn, axis=-1, keepdims=True)
    outer = jnp.mean(dn * normed, axis=-1, keepdims=True)
    return scale * (dn - inner - normed * outer)


def quarter_span(place, at, size):
    return pl.ds(pl.multiple_of(lax.bitwise_xor(place[1], at) * size, size), size)


def fetch_out(place, sources, held, sems):
    own = held.shape[1]
    copies = []
    for at, source in enumerate(sources):
        for part in range(2):
            start = (2 * lax.bitwise_xor(place[1], at) + part) * own
            span = pl.ds(pl.multiple_of(start, own), own)
            copies.append(
                pltpu.make_async_copy(
                    source.at[:, part], held.at[:, :, span], sems.at[2 * at + part]
                )
            )
    for copy in copies:
        copy.start()
    return copies


def mix_kernel(
    place, context_ref, tokens_ref, vec_ref, *refs
):
    sources, refs = refs[:4], refs[4:]
    middle_ref, low_ref, norm_ref, scale_ref, left_ref, out_ref, sems = refs
    copies = fetch_out(place, sources, out_ref, sems)
    own = context_ref.shape[2]
    for at in range(8):
        left_ref[:, at * own : (at + 1) * own] = context_ref[at]
    for copy in copies:
        copy.wait()
    attended = dot(left_ref[...], out_ref[...].reshape(8 * own, 8 * own))
    norm, scale = normalize(tokens_ref[...].astype(FULL) + (attended + vec_ref[6:7]))
    middle = norm * vec_ref[0:1] + vec_ref[2:3]
    middle_ref[...] = middle
    low_ref[...] = middle.astype(LOW)
    norm_ref[...] = norm
    scale_ref[...] = scale


def fetch_units(place, sources, w_in, w_out, sems, first):
    ins = [(sources[0], w_in.at[0])]
    outs = [(sources[1], w_out.at[0])]
    for at, source in enumerate(sources[2:]):
        span = quarter_span(place, at, source.shape[1])
        ins.append((source.at[0], w_in.at[1, span]))
        outs.append((source.at[1], w_out.at[1, span]))
    order = ins[:1] + outs[:1] + ins[1:] + outs[1:]
    if first == 1:
        order = outs[:1] + ins[:1] + outs[1:] + ins[1:]
    copies = [pltpu.make_async_copy(*both, sems.at[at]) for at, both in enumerate(order)]
    for copy in copies:
        copy.start()

    def wait(part, which):
        if part % 2 == 0:
            start = 2 + 4 * which if part else which
            for copy in copies[start : start + 4] if part else copies[start : start + 1]:
                copy.wait()

    return wait


def ffn_kernel(place, first_ref, second_ref, *refs):
    bias_ref, sources, refs = refs[0], refs[1:7], refs[7:]
    pre_ref, act_ref, near_ref, away_ref, sum_ref, w_in, w_out, sems = refs
    wait = fetch_units(place, sources, w_in, w_out, sems, 0)
    rows = first_ref.shape[0]
    step = bias_ref.shape[2]
    both = jnp.concatenate([first_ref[...], second_ref[...]], axis=0)
    for part in range(4):
        span = slice(part * 2 * step, (part + 1) * 2 * step)
        shard, rows_of = part // 2, slice(part % 2 * 2 * step, (part % 2 + 1) * 2 * step)
        whose = place[4] * 4 + lax.bitwise_xor(place[5], 2 * shard)
        bias = [bias_ref[whose * 4 + part % 2 * 2 + at] for at in range(2)]
        wait(part, 0)
        pre = dot_rows(both, w_in[shard, rows_of]) + jnp.concatenate(bias, axis=1)
        pre_ref[:, span] = pre
        act = (pre * (0.5 * (1.0 + lax.erf(pre * (0.5**0.5))))).astype(LOW)
        act_ref[:, span] = act
        wait(part, 1)
        term = dot(act, w_out[shard, rows_of])
        if part == 0:
            sum_ref[...] = term
        else:
            sum_ref[...] += term
    near_ref[...] = sum_ref[:rows]
    away_ref[...] = sum_ref[rows:].astype(LOW)


def ffn_back_kernel(place, first_ref, second_ref, slope_ref, *refs):
    sources, refs = refs[:6], refs[6:]
    grad_ref, near_ref, away_ref, units_ref, sum_ref, w_in, w_out, sems = refs
    wait = fetch_units(place, sources, w_in, w_out, sems, 1)
    rows = first_ref.shape[0]
    step = units_ref.shape[2]
    both = jnp.concatenate([first_ref[...], second_ref[...]], axis=0)
    for part in range(4):
        span = slice(part * 2 * step, (part + 1) * 2 * step)
        shard, rows_of = part // 2, slice(part % 2 * 2 * step, (part % 2 + 1) * 2 * step)
        wait(part, 0)
        grad = (dot_rows(both, w_out[shard, rows_of]) * slope_ref[:, span]).astype(LOW)
        grad_ref[:, span] = grad
        sums = jnp.sum(grad.astype(FULL), axis=0, keepdims=True)
        for at in range(2):
            half = lax.bitwise_xor(place[7], shard)
            units_ref[half * 4 + part % 2 * 2 + at] = sums[:, at * step : (at + 1) * step]
        wait(part, 1)
        term = dot(grad, w_in[shard, rows_of])
        if part == 0:
            sum_ref[...] = term
        else:
            sum_ref[...] += term
    near_ref[...] = sum_ref[:rows]
    away_ref[...] = sum_ref[rows:].astype(LOW)


def top_kernel(
    place, near_ref, sent_ref, far_ref, middle_ref, vec_ref, cotangent_ref,
    layer_ref, grad_ref, low_ref, sums_ref,
):
    summed = near_ref[...] + sent_ref[...].astype(FULL) + far_ref[...].astype(FULL)
    norm, scale = normalize(middle_ref[...] + summed + vec_ref[7:8])
    layer_ref[...] = norm * vec_ref[1:2] + vec_ref[3:4]
    cotangent = cotangent_ref[...].astype(FULL)
    grad = normalize_back(cotangent, vec_ref[1:2], norm, scale)
    grad_ref[...] = grad
    low_ref[...] = grad.astype(LOW)
    sums_ref[0:1] = jnp.sum(cotangent * norm, axis=0, keepdims=True)
    sums_ref[1:2] = jnp.sum(cotangent, axis=0, keepdims=True)
    sums_ref[2:3] = jnp.sum(grad.astype(LOW).astype(FULL), axis=0, keepdims=True)


def mix_back_kernel(
    place, near_ref, sent_ref, far_ref, grad_two_ref, norm_ref, scale_ref, vec_ref, *refs
):
    sources, refs = refs[:4], refs[4:]
    grad_ref, low_ref, context_ref, sums_ref, out_ref, sems = refs
    copies = fetch_out(place, sources, out_ref, sems)
    summed = near_ref[...] + sent_ref[...].astype(FULL) + far_ref[...].astype(FULL)
    grad_mid = grad_two_ref[...] + summed
    norm = norm_ref[...]
    grad = normalize_back(grad_mid, vec_ref[0:1], norm, scale_ref[...])
    grad_ref[...] = grad
    low_ref[...] = grad.astype(LOW)
    sums_ref[0:1] = jnp.sum(grad_mid * norm, axis=0, keepdims=True)
    sums_ref[1:2] = jnp.sum(grad_mid, axis=0, keepdims=True)
    sums_ref[2:3] = jnp.sum(grad.astype(LOW).astype(FULL), axis=0, keepdims=True)
    own = context_ref.shape[2]
    for copy in copies:
        copy.wait()
    total = dot_rows(low_ref[...], out_ref[...].reshape(8 * own, 8 * own)).astype(LOW)
    own = context_ref.shape[2]
    for at in range(8):
        context_ref[at] = total[:, at * own : (at + 1) * own]


def weight_grad_kernel(place, left_0, left_1, *refs):
    right, near_ref, away_ref = refs[:4], refs[4], refs[5]
    held_0, held_1, first, second, sems = refs[6:]
    rows = near_ref.shape[1]
    parts = [side.at[at * rows : (at + 1) * rows] for side in (first, second) for at in range(2)]
    for copy in fetch((left_0, left_1) + tuple(right), [held_0, held_1] + parts, sems):
        copy.wait()
    for stays in range(2):
        shard = place[6] if stays else 1 - place[6]
        for half in range(2):
            span = pl.ds(pl.multiple_of((2 * shard + half) * 2 * rows, 2 * rows), 2 * rows)
            both = dot_cols(held_0[:, span], first[...])
            both += dot_cols(held_1[:, span], second[...])
            for at in range(2):
                part = both[at * rows : (at + 1) * rows]
                slot = 2 * lax.bitwise_xor(place[3], at) + lax.bitwise_xor(place[7], half)
                if stays:
                    near_ref[slot] = part
                else:
                    away_ref[slot] = part.astype(LOW)


def out_grad_kernel(place, *refs):
    parts, grads, near_ref, away_ref, held, right, sems = refs[:4], refs[4:8], *refs[8:]
    step = near_ref.shape[1]
    rows = held.shape[2]
    sides = [right.at[at * rows : (at + 1) * rows] for at in range(4)]
    for copy in fetch(parts + grads, [held.at[at] for at in range(4)] + sides, sems):
        copy.wait()
    for stays in range(2):
        which = place[3] if stays else 1 - place[3]
        left = jnp.concatenate([held[at, which] for at in range(4)], axis=0)
        total = dot_cols(left, right[...])
        for at in range(4):
            slot = lax.bitwise_xor(place[5], at)
            if stays:
                near_ref[slot] = total[at * step : (at + 1) * step]
            else:
                away_ref[slot] = total[at * step : (at + 1) * step].astype(LOW)


def qkv_grad_kernel(place, *refs):
    grad_ref, top_ref, mid_ref, units_a, units_b = refs[:5]
    slots, refs = refs[5:13], refs[13:]
    near_ref, away_ref, total_ref, sums_ref, tokens_ref, sems = refs
    rows = grad_ref.shape[1]
    held = [tokens_ref.at[at * rows : (at + 1) * rows] for at in range(8)]
    copies = fetch(slots, held, sems)
    rank, seq_at = place[0], place[1]
    width = sums_ref.shape[1]
    own = width // 8
    quarter = width // 4
    col_sum = 0.0
    for pair in range(4):
        grads = [grad_ref[lax.bitwise_xor(rank, 2 * pair + at)] for at in range(2)]
        grads = jnp.concatenate(grads, axis=0)
        copies[2 * pair].wait()
        copies[2 * pair + 1].wait()
        term = dot_cols(tokens_ref[2 * pair * rows : 2 * (pair + 1) * rows], grads)
        col_sum += jnp.sum(grads.astype(FULL), axis=0, keepdims=True)
        if pair == 0:
            total_ref[...] = term
        else:
            total_ref[...] += term
    sums_ref[...] = jnp.zeros_like(sums_ref)
    sums_ref[0:1] = mid_ref[0:1]
    sums_ref[1:2] = top_ref[0:1]
    sums_ref[2:3] = mid_ref[1:2]
    sums_ref[3:4] = top_ref[1:2]
    own_cols = pl.ds(pl.multiple_of(rank * own, own), own)
    sums_ref[4:5, own_cols] = col_sum[:, :own]
    sums_ref[5:6, own_cols] = col_sum[:, 2 * own :]
    sums_ref[6:7] = mid_ref[2:3]
    sums_ref[7:8] = top_ref[2:3]
    row_at = lax.broadcasted_iota(jnp.int32, (8, own), 0)
    for at in (1, 3, 0, 2):
        whose = lax.bitwise_xor(seq_at, at)
        part = total_ref[quarter_span(place, at, quarter)]
        sums = sums_ref[:, quarter_span(place, at, quarter)]
        here = lax.shift_right_logical(whose, 1) == place[4]
        first = 4 * lax.bitwise_and(whose, 1)
        units = [units_a[first + row] + units_b[first + row] for row in range(4)]
        mine = (row_at >= 4 * place[8]) & (row_at < 4 * place[8] + 4)
        units = jnp.where(mine & here, jnp.concatenate(units + units, axis=0), 0.0)
        sums = jnp.concatenate([sums, units], axis=1)
        sums = jnp.concatenate([sums, jnp.zeros_like(sums)], axis=0)
        if at % 2:
            away_ref[at // 2, :quarter] = part.astype(LOW)
            away_ref[at // 2, quarter:] = sums.astype(LOW)
        else:
            near_ref[at // 2, :quarter] = part
            near_ref[at // 2, quarter:] = sums


def input_terms_kernel(place, across_ref, own_ref, *refs):
    sources, refs = refs[:5], refs[5:]
    near_ref, away_ref, cols_ref, beyond_ref, parts, sems = refs
    copies = fetch(sources, [cols_ref] + [parts.at[at] for at in range(4)], sems)
    rows = own_ref.shape[1]
    for copy in copies:
        copy.wait()
    put_columns(place, parts, beyond_ref)
    for slots in ((1, 3), (0, 2)):
        whose = [lax.bitwise_xor(place[5], slot) for slot in slots]
        left = jnp.concatenate([own_ref[place[4] * 4 + at] for at in whose], axis=0)
        term = dot_rows(left, cols_ref[...])
        left = jnp.concatenate([across_ref[at] for at in whose], axis=0)
        term += dot_rows(left, beyond_ref[...])
        for at, slot in enumerate(slots):
            part = term[at * rows : (at + 1) * rows]
            if slot % 2:
                away_ref[at] = part.astype(LOW)
            else:
                near_ref[at] = part


def qkv_send_kernel(place, near_ref, far_ref, out_ref):
    total = near_ref[...] + far_ref[...].astype(FULL)
    rows = total.shape[0] - 16
    step = rows // 8
    sums = total[rows:].astype(LOW)
    for at in range(8):
        out_ref[at, :step] = total[at * step : (at + 1) * step].astype(LOW)
        out_ref[at, step:] = sums


def qkv_last_kernel(place, parts_ref, grad_ref, sums_ref):
    step = grad_ref.shape[0]
    own = parts_ref.shape[2] // 3
    for at in range(8):
        for which in range(3):
            cols = slice((which * 8 + at) * own, (which * 8 + at + 1) * own)
            grad_ref[:, cols] = parts_ref[at, :step, which * own : (which + 1) * own].astype(FULL)
    sums = parts_ref[0, step:].astype(FULL)
    for at in range(1, 8):
        sums += parts_ref[at, step:].astype(FULL)
    sums_ref[...] = sums


def grouped_body(tokens, out_grad, w_qkv, w_out, fc_in, fc_out, fc_in_bias, vectors):
    rows, width = tokens.shape
    own = width // 8
    seq_at = lax.axis_index("seq")
    core_at, across_at = lax.rem(seq_at, 2), seq_at // 2
    head_at, blk_at = lax.axis_index("head"), lax.axis_index("blk")
    rank = head_at * 4 + blk_at
    far_at, near_at = blk_at // 2, lax.rem(blk_at, 2)
    place = jnp.stack(
        [rank, seq_at, core_at, across_at, head_at, blk_at, far_at ^ core_at, far_at, near_at]
    ).astype(jnp.int32)
    unit_rows = fc_in.shape[0] // 4
    units = 8 * unit_rows

    quarter = own // 4
    qkv_rows = lax.dynamic_slice_in_dim(w_qkv, seq_at * quarter, quarter, 0)
    qkv_rows = qkv_rows.reshape(quarter, 3, 8, own).transpose(2, 1, 0, 3)
    qkv_rows = qkv_rows.reshape(8, 3 * quarter, own)
    small = jnp.concatenate([vectors.T, fc_in_bias.reshape(-1, own)], axis=0)
    small = jnp.broadcast_to(small[None], (8, 12, own))
    to_swap = jnp.concatenate([qkv_rows, small, jnp.zeros((8, 4, own), LOW)], axis=1)
    out_quarter = lax.dynamic_slice_in_dim(w_out, seq_at * 2 * own, 2 * own, 1)
    out_quarter = out_quarter.reshape(own, 2, own).transpose(1, 0, 2).reshape(1, 2 * own, own)
    out_quarter = jnp.broadcast_to(out_quarter, (8, 2 * own, own))
    units_away = jnp.stack(
        [lax.dynamic_slice_in_dim(w, seq_at * unit_rows, unit_rows, 0) for w in (fc_in, fc_out)]
    )

    inner = inner_blk()
    first = lax.ppermute(tokens, "blk", PAIRS)
    middle = lax.ppermute(tokens, "blk", INNER)
    across_0 = flip_head(tokens)
    first, middle, across_0, to_swap = after((first, middle, across_0, to_swap))
    second_in = lax.ppermute(first, "blk", INNER)
    second_out = lax.ppermute(middle, "blk", OUTER)
    across_1 = flip_head(first)
    swapped = lax.all_to_all(to_swap, GROUP, 0, 0, tiled=True)
    second_in, second_out, across_1, swapped, out_quarter = after(
        (second_in, second_out, across_1, swapped, out_quarter)
    )
    out_quarter = lax.all_to_all(out_quarter, GROUP, 0, 0, tiled=True).reshape(8, 2, own, own)
    third = lax.ppermute(second_in, "blk", OUTER)
    second = jnp.where(inner, second_in, second_out)
    across_2 = flip_head(second)
    qkv_own = swapped[:, : 3 * quarter].reshape(8, 3, quarter, own)
    qkv_across = lax.ppermute(qkv_own, "seq", ACROSS)
    small = swapped[:, 3 * quarter : 3 * quarter + 12].astype(FULL)
    vec = small[:, :8].transpose(1, 0, 2).reshape(8, width)
    bias_all = small[:, 8:].reshape(32, 1, own)
    third, across_2, qkv_own, qkv_across = after((third, across_2, qkv_own, qkv_across))
    third = jnp.where(inner, middle, third)
    across_3 = flip_head(third)
    qkv_quarters = [qkv_own, lax.ppermute(qkv_own, "seq", CORE)]
    qkv_quarters += [qkv_across, lax.ppermute(qkv_across, "seq", CORE)]
    across_3, out_quarter, units_away, *qkv_quarters = after(
        [across_3, out_quarter, units_away] + qkv_quarters
    )
    beyond = flip_head(qkv_quarters[0])
    slots = [tokens, first, second, third, across_0, across_1, across_2, across_3]

    units_two_on = lax.ppermute(units_away, "blk", TWO_ON)
    bias = vectors.T.reshape(8, 1, own)[4:6].astype(FULL)
    seq_rows = 8 * rows
    heads = own // HEAD_DIM
    kept_shapes = [((seq_rows, own), LOW)] * 3 + [((seq_rows, own), FULL)] * 2
    kept_shapes.append(((width, 3 * own), LOW))
    kept_shapes.append(((heads, seq_rows, seq_rows), LOW))
    kept_scratch = [pltpu.VMEM(*shape) for shape in kept_shapes]
    context, *kept = call(
        attend_kernel,
        [shape_of((8, rows, own), LOW)] + [shape_of(*shape) for shape in kept_shapes],
        place, bias, *qkv_quarters, *slots,
        scratch=kept_scratch
        + [pltpu.VMEM((seq_rows, width), LOW), pltpu.VMEM((4, 8, 3, quarter, own), LOW)]
        + [pltpu.SemaphoreType.DMA((16,)), pltpu.SemaphoreType.DMA((12,))],
        flops=8 * 10**9,
        far_in=12,
        far_out=7,
        vmem=56,
    )
    out_across = lax.ppermute(out_quarter, "seq", ACROSS)
    context, out_across, out_quarter = after((context, out_across, out_quarter))
    out_slots = [out_quarter, lax.ppermute(out_quarter, "seq", CORE)]
    out_slots += [out_across, lax.ppermute(out_across, "seq", CORE)]
    context = lax.all_to_all(context, GROUP, 0, 0, tiled=True)
    beyond = after(beyond, *out_slots[1:])
    beyond_across = lax.ppermute(beyond, "seq", ACROSS)
    beyond_quarters = [beyond, lax.ppermute(beyond, "seq", CORE)]
    beyond_quarters += [beyond_across, lax.ppermute(beyond_across, "seq", CORE)]
    ffn_weights = [fc_in, fc_out] + gather_seq(units_two_on)
    out_scratch = [pltpu.VMEM((8, own, width), LOW), pltpu.SemaphoreType.DMA((8,))]

    per_row = shape_of((rows, width), FULL)
    per_row_low = shape_of((rows, width), LOW)
    middle, middle_low, norm_one, scale_one = call(
        mix_kernel,
        [per_row, per_row_low, per_row, shape_of((rows, 1), FULL)],
        place, context, tokens, vec, *out_slots,
        scratch=[pltpu.VMEM((rows, width), LOW)] + out_scratch,
        flops=2 * 10**9,
        far_in=4,
    )

    both_rows = shape_of((2 * rows, units), FULL)
    both_rows_low = shape_of((2 * rows, units), LOW)
    middle_slots = gather_four(middle_low)
    ffn_scratch = [pltpu.VMEM((2 * rows, width), FULL)]
    ffn_scratch += [pltpu.VMEM((2, 4 * unit_rows, width), LOW)] * 2
    ffn_scratch += [pltpu.SemaphoreType.DMA((10,))]
    ffn_parts = []
    for at in (0, 2):
        ffn_parts.append(
            call(
                ffn_kernel,
                [both_rows, both_rows_low, per_row, per_row_low],
                place, middle_slots[at], middle_slots[at + 1], bias_all, *ffn_weights,
                scratch=ffn_scratch,
                flops=3 * 10**9,
                far_in=6,
            )
        )

    def features_of(core, head):
        both = lax.dynamic_index_in_dim(context.reshape(2, 2, 2, rows, own), core, 1, False)
        return lax.dynamic_index_in_dim(both, head, 1, False)

    diagonal = []
    for seq in range(4):
        for head in range(2):
            diagonal.append((seq * 2 + head, (seq ^ 1) * 2 + 1 - head))
    parts = [
        features_of(core_at, head_at),
        features_of(1 - core_at, head_at),
        features_of(core_at, 1 - head_at),
        features_of(1 - core_at, 1 - head_at),
    ]
    parts[1:] = after(parts[1:], ffn_parts[0][1])
    parts = [
        parts[0],
        lax.ppermute(parts[1], "seq", CORE),
        flip_head(parts[2]),
        lax.ppermute(parts[3], ("seq", "head"), tuple(diagonal)),
    ]

    def scatter_parts(near_part, far_part):
        sent_far = lax.ppermute(far_part[1], "blk", PAIRS).astype(FULL)
        far = flip_head((far_part[0] + sent_far).astype(LOW))
        return near_part[0], lax.ppermute(near_part[1], "blk", PAIRS), far

    weight_scratch = [pltpu.VMEM((2 * rows, units), LOW)] * 2
    weight_scratch += [pltpu.VMEM((2 * rows, width), LOW)] * 2 + [pltpu.SemaphoreType.DMA((6,))]
    terms = [shape_of((4, unit_rows, width), FULL), shape_of((4, unit_rows, width), LOW)]

    def weight_grads(lefts, rights):
        return call(
            weight_grad_kernel, terms, place, *lefts, *rights,
            scratch=weight_scratch, flops=2 * 10**9, far_in=6,
        )

    def add_low(near, sent):
        return near + sent.astype(FULL)

    summed = scatter_parts(ffn_parts[0][2:4], ffn_parts[1][2:4])
    summed = after(summed, *beyond_quarters)
    three_sums = shape_of((3, width), FULL)
    layer_output, grad_two, grad_ffn, top_sums = call(
        top_kernel,
        [per_row, per_row, per_row_low, three_sums],
        place, *summed, middle, vec, out_grad,
        flops=10**9,
    )

    grad_ffn_slots = gather_four(grad_ffn)
    back_parts = []
    for at in (0, 2):
        pre = ffn_parts[at // 2][0]
        cdf = 0.5 * (1.0 + lax.erf(pre * (0.5**0.5)))
        slope = cdf + pre * jnp.exp(-0.5 * pre * pre) * ((2.0 * math.pi) ** -0.5)
        back_parts.append(
            call(
                ffn_back_kernel,
                [both_rows_low, per_row, per_row_low, shape_of((8, 1, unit_rows), FULL)],
                place, grad_ffn_slots[at], grad_ffn_slots[at + 1], slope, *ffn_weights,
                scratch=ffn_scratch,
                flops=3 * 10**9,
                far_in=6,
            )
        )
    summed = scatter_parts(back_parts[0][1:3], back_parts[1][1:3])
    acts = after((ffn_parts[0][1], ffn_parts[1][1]), back_parts[1][0])
    out_near_grad, out_away_grad = weight_grads(acts, grad_ffn_slots)
    out_sent = lax.ppermute(out_away_grad, "seq", CORE)
    summed = after(summed, out_sent)
    grad_one, grad_attn, grad_context, mid_sums = call(
        mix_back_kernel,
        [per_row, per_row_low, shape_of((8, rows, own), LOW), three_sums],
        place, *summed, grad_two, norm_one, scale_one, vec, *out_slots,
        scratch=out_scratch,
        flops=2 * 10**9,
        far_in=4,
    )
    grad_context = lax.all_to_all(grad_context, GROUP, 0, 0, tiled=True)
    out_across = lax.ppermute(
        add_low(out_near_grad[2:], out_sent[2:]).astype(LOW), "seq", ACROSS
    )
    in_near_grad, in_away_grad = weight_grads((back_parts[0][0], back_parts[1][0]), middle_slots)
    in_sent = lax.ppermute(in_away_grad, "seq", CORE)
    attn_across = flip_head(grad_attn)

    def kept_here(near, sent, across, at):
        return add_low(near[at] + sent[at].astype(FULL), across[at])

    in_across = add_low(in_near_grad[2:], in_sent[2:]).astype(LOW)
    out_last = kept_here(out_near_grad, out_sent, out_across, 1).astype(LOW)
    grad_context, in_across, out_last, attn_across = after(
        (grad_context, in_across, out_last, attn_across)
    )
    in_across = lax.ppermute(in_across, "seq", ACROSS)
    out_last = lax.ppermute(out_last, "blk", TWO_ON)
    grad_attn_slots = [grad_attn, lax.ppermute(grad_attn, "seq", CORE)]
    grad_attn_slots += [attn_across, lax.ppermute(attn_across, "seq", CORE)]
    (grad_cols,) = call(
        attend_back_kernel,
        [shape_of((8, rows, 3 * own), LOW)],
        place, grad_context, *kept[:5], kept[6],
        scratch=kept_scratch[:5]
        + kept_scratch[6:]
        + [pltpu.VMEM((own, seq_rows), FULL)] * 2
        + [pltpu.SemaphoreType.DMA((9,))],
        flops=8 * 10**9,
        far_in=6,
        vmem=56,
    )

    cols_sent = lax.dynamic_slice_in_dim(grad_cols, (1 - head_at) * 4, 4, 0)
    cols_sent = flip_head(cols_sent)
    in_last = kept_here(in_near_grad, in_sent, in_across, 1).astype(LOW)
    in_last = lax.ppermute(in_last, "blk", TWO_ON)
    payload_rows = 2 * own + 16
    near, away = call(
        qkv_grad_kernel,
        [shape_of((2, payload_rows, 3 * own), FULL), shape_of((2, payload_rows, 3 * own), LOW)],
        place, grad_cols, top_sums, mid_sums, back_parts[0][3], back_parts[1][3], *slots,
        scratch=[pltpu.VMEM((width, 3 * own), FULL), pltpu.VMEM((8, width), FULL)]
        + [pltpu.VMEM((seq_rows, width), LOW), pltpu.SemaphoreType.DMA((8,))],
        flops=2 * 10**9,
        far_in=8,
    )
    sent = lax.ppermute(away, "seq", CORE)
    near_terms, away_terms = call(
        input_terms_kernel,
        [
            shape_of((2, rows, width), FULL),
            shape_of((2, rows, width), LOW),
        ],
        place, cols_sent, grad_cols, kept[5], *beyond_quarters,
        scratch=[pltpu.VMEM((width, 3 * own), LOW)] * 2
        + [pltpu.VMEM((4, 8, 3, quarter, own), LOW), pltpu.SemaphoreType.DMA((5,))],
        flops=2 * 10**9,
        far_in=5,
    )
    sent_terms = lax.ppermute(away_terms, "blk", PAIRS)
    out_terms = [shape_of((4, own // 4, width), FULL), shape_of((4, own // 4, width), LOW)]
    near_rows, away_rows = call(
        out_grad_kernel, out_terms, place, *parts, *after(grad_attn_slots, away_terms),
        scratch=[pltpu.VMEM((4, 2, rows, own), LOW), pltpu.VMEM((4 * rows, width), LOW)]
        + [pltpu.SemaphoreType.DMA((8,))],
        flops=10**9,
        far_in=8,
    )
    sent_rows = lax.ppermute(away_rows, "seq", ACROSS)

    last_terms = after(add_low(near_terms[1], sent_terms[1]).astype(LOW), in_last)
    last_terms = lax.ppermute(last_terms, "blk", TWO_ON)
    out_rows = add_low(near_rows, sent_rows)
    sent_rows = lax.ppermute(out_rows.reshape(2, 2, -1, width)[:, 1].astype(LOW), "blk", PAIRS)
    last_rows = lax.ppermute(add_low(out_rows[2], sent_rows[1]).astype(LOW), "blk", TWO_ON)
    grad_w_out = add_low(add_low(out_rows[0], sent_rows[0]), last_rows)
    far = lax.ppermute(add_low(near[1], sent[1]).astype(LOW), "seq", ACROSS)
    unit_grads = jnp.stack(
        [
            add_low(kept_here(in_near_grad, in_sent, in_across, 0), in_last),
            add_low(kept_here(out_near_grad, out_sent, out_across, 0), out_last),
        ]
    )
    (payload,) = call(
        qkv_send_kernel,
        [shape_of((8, own // 4 + 16, 3 * own), LOW)],
        place, add_low(near[0], sent[0]), far,
    )
    payload = lax.all_to_all(payload, GROUP, 0, 0, tiled=True)
    input_grad = grad_one + add_low(add_low(near_terms[0], sent_terms[0]), last_terms)

    moves = []
    for across in range(2):
        for core in range(2):
            for head in range(2):
                for two_on in range(2):
                    for near_by in range(2):
                        start = (across * 2 + core) * 8 + head * 4 + two_on * 2 + near_by
                        stop = (head * 2 + core) * 8 + near_by * 4 + two_on * 2 + across
                        if start != stop:
                            moves.append((start, stop))
    stays = (across_at == head_at) & (head_at == near_at)

    moved = lax.ppermute(unit_grads.astype(LOW), ("seq", "head", "blk"), moves).astype(FULL)
    grad_fc_in, grad_fc_out = jnp.where(stays, unit_grads, moved)

    grad_w_qkv, sums = call(
        qkv_last_kernel,
        [shape_of((own // 4, 3 * width), FULL), shape_of((16, 3 * own), FULL)],
        place, payload,
    )
    grad_vectors = lax.dynamic_slice(sums, (0, rank * (own // 4)), (8, own // 4)).T
    grad_bias = lax.dynamic_slice(sums, (rank, 2 * own), (1, own)).reshape(own)
    return (
        layer_output,
        input_grad,
        grad_w_qkv,
        grad_w_out,
        grad_fc_in,
        grad_fc_out,
        grad_bias,
        grad_vectors,
    )


def solution(mesh):
    sizes = tuple(mesh.shape[name] for name in ("seq", "head", "blk"))
    return jax.shard_map(
        grouped_body if sizes == (4, 2, 4) else general_body,
        mesh=mesh,
        in_specs=(
            P(("seq", "head", "blk"), None),
            P(("seq", "head", "blk"), None),
            P(("head", "blk"), None),
            P(("head", "blk"), None),
            P(("head", "blk"), None),
            P(("head", "blk"), None),
            P(("head", "blk")),
            P(("head", "blk"), None),
        ),
        out_specs=(
            P(("seq", "head", "blk"), None),
            P(("seq", "head", "blk"), None),
            P(("seq", "head", "blk"), None),
            P(("seq", "head", "blk"), None),
            P(("seq", "head", "blk"), None),
            P(("seq", "head", "blk"), None),
            P(("seq", "head", "blk")),
            P(("seq", "head", "blk"), None),
        ),
        check_vma=False,
    )
```

```python
import math

import jax
import jax.numpy as jnp
from jax import lax
from jax.experimental import pallas as pl
from jax.experimental.pallas import tpu as pltpu
from jax.sharding import PartitionSpec as P

HEAD_DIM = 64


def layer_norm(values, gain_vec, shift_vec):
    center = values - jnp.mean(values, axis=-1, keepdims=True)
    spread = jnp.mean(center * center, axis=-1, keepdims=True)
    return center * lax.rsqrt(spread + 1e-05) * gain_vec + shift_vec


def gelu_exact(values):
    return jax.nn.gelu(values, approximate=False)


def split_heads(values):
    return values.reshape(values.shape[0], values.shape[1] // HEAD_DIM, HEAD_DIM)


def head_scores(left_rows, right_rows):
    return jnp.einsum("qhd,khd->hqk", left_rows, right_rows, preferred_element_type=jnp.float32)


def ffn_part(factors):
    middle_low, grad_pre_full, act_full, grad_ffn = factors
    return jnp.concatenate(
        [
            jnp.einsum("tf,td->fd", grad_pre_full, middle_low, preferred_element_type=jnp.float32),
            jnp.einsum("tf,td->fd", act_full, grad_ffn, preferred_element_type=jnp.float32),
        ],
        axis=1,
    )


def attn_part(factors, extra_cols):
    tokens, grad_proj, context, grad_attn = factors
    return jnp.concatenate(
        [
            jnp.einsum("tn,tc->nc", tokens, grad_proj, preferred_element_type=jnp.float32),
            jnp.einsum("tn,tc->nc", context, grad_attn, preferred_element_type=jnp.float32),
            extra_cols,
        ],
        axis=1,
    )


def general_body(tokens, out_grad, w_qkv, w_out, fc_in, fc_out, fc_in_bias, vectors):
    model_width = tokens.shape[1]
    hidden_units = fc_in.shape[0] * lax.axis_size(("head", "blk"))
    ratio = hidden_units // model_width
    scale = HEAD_DIM ** (-0.5)
    part_qkv = lax.all_gather(w_qkv, ("head", "blk"), axis=0, tiled=True)
    part_out = lax.all_gather(w_out, ("head", "blk"), axis=0, tiled=True)
    part_vec = lax.all_gather(vectors, ("head", "blk"), axis=0, tiled=True)
    part_rows = part_qkv.shape[0]
    projected = jnp.dot(tokens, part_qkv, preferred_element_type=jnp.float32)
    out_full = part_out
    attn_state = (projected, out_full, part_vec)
    projected = attn_state[0]
    out_full = attn_state[1]
    vec_float = attn_state[2].astype(jnp.float32)
    gain_one, gain_two = (vec_float[:, 0], vec_float[:, 1])
    shift_one, shift_two = (vec_float[:, 2], vec_float[:, 3])
    bias_query, bias_value = (vec_float[:, 4], vec_float[:, 5])
    bias_output, bias_ffn = (vec_float[:, 6], vec_float[:, 7])
    queries = ((projected[:, :model_width] + bias_query) * scale).astype(jnp.bfloat16)
    key_rows = projected[:, model_width : 2 * model_width].astype(jnp.bfloat16)
    value_rows = (projected[:, 2 * model_width :] + bias_value).astype(jnp.bfloat16)
    query_heads, key_heads, value_heads = (
        lax.all_to_all(queries, "head", split_axis=1, concat_axis=0, tiled=True),
        lax.all_to_all(key_rows, "head", split_axis=1, concat_axis=0, tiled=True),
        lax.all_to_all(value_rows, "head", split_axis=1, concat_axis=0, tiled=True),
    )
    query_split = split_heads(query_heads)
    group_rows = query_split.shape[0]
    group_width = key_heads.shape[1]
    seq_rows = group_rows * lax.axis_size("blk")
    portion = (
        lax.all_gather(key_heads, "blk", axis=0, tiled=True),
        lax.all_gather(value_heads, "blk", axis=0, tiled=True),
    )
    scores = head_scores(query_split, split_heads(portion[0]))
    run_sum = jnp.sum(jnp.exp(scores), axis=-1)
    key_all = portion[0]
    value_all = portion[1]
    run_sum, key_all, value_all = (run_sum, key_all, value_all)
    log_total = jnp.log(run_sum)
    block_rows = math.gcd(512, seq_rows)
    block_count = seq_rows // block_rows
    key_blocks = key_all.reshape(block_count, block_rows, group_width)
    value_blocks = value_all.reshape(block_count, block_rows, group_width)

    def mix_block(totals, pair):
        scores = head_scores(query_split, split_heads(pair[0]))
        probs_low = jnp.exp(scores - log_total[:, :, None]).astype(jnp.bfloat16)
        return (
            totals
            + jnp.einsum(
                "hqk,khd->qhd", probs_low, split_heads(pair[1]), preferred_element_type=jnp.float32
            ),
            None,
        )

    mixed, unused = lax.scan(
        mix_block, jnp.zeros(query_split.shape, jnp.float32), (key_blocks, value_blocks)
    )
    context = lax.all_to_all(
        mixed.reshape(group_rows, -1).astype(jnp.bfloat16),
        "head",
        split_axis=0,
        concat_axis=1,
        tiled=True,
    )
    attn_out = jnp.dot(context, out_full, preferred_element_type=jnp.float32) + bias_output
    residual_one = tokens.astype(jnp.float32) + attn_out
    middle, norm_one_back = jax.vjp(layer_norm, residual_one, gain_one, shift_one)
    middle_low = middle.astype(jnp.bfloat16)
    part_in = lax.all_gather(fc_in, ("head", "blk"), axis=0, tiled=True)
    part_out = lax.all_gather(fc_out, ("head", "blk"), axis=0, tiled=True)
    part_bias = lax.all_gather(fc_in_bias, ("head", "blk"), axis=0, tiled=True)
    pre_part = jnp.einsum("td,fd->tf", middle_low, part_in, preferred_element_type=jnp.float32)
    pre_part = pre_part + part_bias.astype(jnp.float32)
    act_part = gelu_exact(pre_part).astype(jnp.bfloat16)
    summed = jnp.dot(act_part, part_out, preferred_element_type=jnp.float32)
    ffn_pre_full = pre_part
    residual_two = middle + summed + bias_ffn
    layer_output, norm_two_back = jax.vjp(layer_norm, residual_two, gain_two, shift_two)
    grad_resid_two, grad_gain_two, grad_shift_two = norm_two_back(out_grad.astype(jnp.float32))
    grad_ffn = grad_resid_two.astype(jnp.bfloat16)
    qkv_flat = w_qkv.reshape(fc_in.shape[0], -1)
    portion = (
        lax.all_gather(fc_in, ("head", "blk"), axis=0, tiled=True),
        lax.all_gather(fc_out, ("head", "blk"), axis=0, tiled=True),
        lax.all_gather(qkv_flat, ("head", "blk"), axis=0, tiled=True),
    )
    part_in = portion[0]
    part_rows = part_in.shape[0]
    pre_part = ffn_pre_full
    grad_act = jnp.einsum("td,fd->tf", grad_ffn, portion[1], preferred_element_type=jnp.float32)
    grad_pre = jax.vjp(gelu_exact, pre_part)[1](grad_act)[0].astype(jnp.bfloat16)
    grad_mid = jnp.dot(grad_pre, part_in, preferred_element_type=jnp.float32)
    grad_mid, grad_pre_all = (grad_mid, grad_pre)
    qkv_gathered = portion[2]
    qkv_full = qkv_gathered.reshape(model_width, 3 * model_width)
    grad_resid_one, grad_gain_one, grad_shift_one = norm_one_back(grad_resid_two + grad_mid)
    grad_attn = grad_resid_one.astype(jnp.bfloat16)
    grad_context = jnp.einsum(
        "td,ed->te", grad_attn, out_full, preferred_element_type=jnp.float32
    ).astype(jnp.bfloat16)
    grad_ctx_heads = lax.all_to_all(grad_context, "head", split_axis=1, concat_axis=0, tiled=True)
    grad_ctx_split = split_heads(grad_ctx_heads)
    delta_heads = jnp.sum(grad_ctx_split.astype(jnp.float32) * mixed, axis=-1).T

    def back_block(grad_query, pair):
        key_part = split_heads(pair[0])
        value_part = split_heads(pair[1])
        scores = head_scores(query_split, key_part)
        probs = jnp.exp(scores - log_total[:, :, None])
        dprobs = head_scores(grad_ctx_split, value_part)
        dscores = (probs * (dprobs - delta_heads[:, :, None])).astype(jnp.bfloat16)
        grad_query = grad_query + jnp.einsum(
            "hqk,khd->qhd", dscores, key_part, preferred_element_type=jnp.float32
        )
        grad_key = jnp.einsum(
            "hqk,qhd->khd", dscores, query_split, preferred_element_type=jnp.float32
        )
        grad_value = jnp.einsum(
            "hqk,qhd->khd",
            probs.astype(jnp.bfloat16),
            grad_ctx_split,
            preferred_element_type=jnp.float32,
        )
        part_rows = pair[0].shape[0]
        return (
            grad_query,
            jnp.concatenate(
                [grad_key.reshape(part_rows, -1), grad_value.reshape(part_rows, -1)], axis=1
            ),
        )

    grad_query_heads, kv_terms = lax.scan(
        back_block, jnp.zeros(query_split.shape, jnp.float32), (key_blocks, value_blocks)
    )
    kv_own = lax.psum_scatter(
        kv_terms.reshape(seq_rows, 2 * group_width).astype(jnp.bfloat16),
        "blk",
        scatter_dimension=0,
        tiled=True,
    ).astype(jnp.float32)
    grad_query_tok, grad_key_tok, grad_value_tok = (
        lax.all_to_all(
            grad_query_heads.reshape(group_rows, -1).astype(jnp.bfloat16),
            "head",
            split_axis=0,
            concat_axis=1,
            tiled=True,
        ),
        lax.all_to_all(
            kv_own[:, :group_width].astype(jnp.bfloat16),
            "head",
            split_axis=0,
            concat_axis=1,
            tiled=True,
        ),
        lax.all_to_all(
            kv_own[:, group_width:].astype(jnp.bfloat16),
            "head",
            split_axis=0,
            concat_axis=1,
            tiled=True,
        ),
    )
    grad_proj = jnp.concatenate(
        [grad_query_tok * jnp.bfloat16(scale), grad_key_tok, grad_value_tok], axis=1
    )
    through_proj = jnp.einsum("tc,nc->tn", grad_proj, qkv_full, preferred_element_type=jnp.float32)
    input_grad = grad_resid_one + through_proj
    grad_proj_float = grad_proj.astype(jnp.float32)
    vec_term = jnp.stack(
        [
            grad_gain_one,
            grad_gain_two,
            grad_shift_one,
            grad_shift_two,
            jnp.sum(grad_proj_float[:, :model_width], axis=0),
            jnp.sum(grad_proj_float[:, 2 * model_width :], axis=0),
            jnp.sum(grad_attn.astype(jnp.float32), axis=0),
            jnp.sum(grad_ffn.astype(jnp.float32), axis=0),
        ],
        axis=1,
    )
    bias_term = jnp.sum(grad_pre_all.astype(jnp.float32), axis=0).reshape(model_width, -1)
    bias_cols = bias_term.shape[1]
    padding = jnp.zeros((model_width, 128 - 8 - bias_cols), jnp.float32)
    extra_cols = jnp.concatenate([vec_term, bias_term, padding], axis=1)
    rows_dev = hidden_units // lax.axis_size(("seq", "head", "blk"))
    ffn_block = ffn_part((middle_low, grad_pre_all, act_part, grad_ffn))
    attn_block = attn_part((tokens, grad_proj, context, grad_attn), extra_cols)
    merged = lax.psum_scatter(
        jnp.concatenate(
            [ffn_block, attn_block.reshape(lax.axis_size(("seq", "head", "blk")) * rows_dev, -1)],
            axis=1,
        ),
        ("seq", "head", "blk"),
        scatter_dimension=0,
        tiled=True,
    )
    grad_fc_in = merged[:, :model_width]
    grad_fc_out = merged[:, model_width : 2 * model_width]
    attn_grad = merged[:, 2 * model_width :].reshape(rows_dev // ratio, 4 * model_width + 128)
    grad_w_qkv = attn_grad[:, : 3 * model_width]
    grad_w_out = attn_grad[:, 3 * model_width : 4 * model_width]
    grad_vectors = attn_grad[:, 4 * model_width : 4 * model_width + 8]
    grad_fc_in_bias = attn_grad[:, 4 * model_width + 8 : 4 * model_width + 8 + bias_cols].reshape(
        -1
    )
    return (
        layer_output,
        input_grad,
        grad_w_qkv,
        grad_w_out,
        grad_fc_in,
        grad_fc_out,
        grad_fc_in_bias,
        grad_vectors,
    )


GROUP = ("head", "blk")
FLIP = ((0, 1), (1, 0))
PAIRS = ((0, 1), (1, 0), (2, 3), (3, 2))
INNER = ((1, 2), (2, 1))
OUTER = ((1, 0), (2, 3))
INWARD = ((0, 1), (3, 2))
TWO_ON = ((0, 2), (2, 0), (1, 3), (3, 1))
CORE = tuple((at, at ^ 1) for at in range(4))
ACROSS = tuple((at, at ^ 2) for at in range(4))
LOW = jnp.bfloat16
FULL = jnp.float32
ROWS_DIMS = (((1,), (1,)), ((), ()))
COLS_DIMS = (((0,), (0,)), ((), ()))


def dot(left, right):
    return jnp.dot(left, right, preferred_element_type=FULL)


def dot_rows(left, right):
    return lax.dot_general(left, right, ROWS_DIMS, preferred_element_type=FULL)


def dot_cols(left, right):
    return lax.dot_general(left, right, COLS_DIMS, preferred_element_type=FULL)


def after(values, *others):
    if not isinstance(values, (list, tuple)):
        return lax.optimization_barrier((values,) + others)[0]
    return lax.optimization_barrier(tuple(values) + others)[: len(values)]


def inner_blk():
    at = lax.axis_index("blk")
    return (at == 1) | (at == 2)


def flip_head(value):
    return lax.ppermute(value, "head", FLIP)


def gather_seq(own):
    across = lax.ppermute(own, "seq", ACROSS)
    return [own, lax.ppermute(own, "seq", CORE), across, lax.ppermute(across, "seq", CORE)]


def gather_four(own):
    across = flip_head(own)
    beside = lax.ppermute(own, "blk", PAIRS)
    return [own, beside, across, lax.ppermute(across, "blk", PAIRS)]


def gather_cores(own):
    across = flip_head(own)
    return [own, lax.ppermute(own, "seq", CORE), across, lax.ppermute(across, "seq", CORE)]


def shape_of(shape, dtype):
    return jax.ShapeDtypeStruct(shape, dtype)


def call(kernel, outs, place, *args, scratch=(), flops=0, vmem=28, far_in=0, far_out=0):
    moved = sum(arg.size * arg.dtype.itemsize for arg in args)
    moved += sum(math.prod(out.shape) * jnp.dtype(out.dtype).itemsize for out in outs)
    near = pl.BlockSpec(memory_space=pltpu.VMEM)
    far = pl.BlockSpec(memory_space=pltpu.HBM)
    return pl.pallas_call(
        kernel,
        out_shape=outs,
        in_specs=[pl.BlockSpec(memory_space=pltpu.SMEM)]
        + [near] * (len(args) - far_in)
        + [far] * far_in,
        out_specs=[near] * (len(outs) - far_out) + [far] * far_out,
        scratch_shapes=scratch,
        compiler_params=pltpu.CompilerParams(vmem_limit_bytes=vmem * 2**20),
        cost_estimate=pl.CostEstimate(flops=flops // 2, bytes_accessed=moved, transcendentals=0),
    )(place, *args)


def fetch(sources, held, sems):
    copies = [pltpu.make_async_copy(*both, sems.at[at]) for at, both in enumerate(zip(sources, held))]
    for copy in copies:
        copy.start()
    return copies


def put_columns(place, parts, cols_ref):
    step, width = parts.shape[3:]
    for at in range(8):
        for part in range(4):
            start = (4 * at + lax.bitwise_xor(place[1], part)) * step
            span = pl.ds(pl.multiple_of(start, step), step)
            for which in range(3):
                cols_ref[span, which * width : (which + 1) * width] = parts[part, at, which]


def attend_kernel(place, *refs):
    bias_ref, refs = refs[0], refs[1:]
    quarters, slots, refs = refs[:4], refs[4:12], refs[12:]
    context_ref, kept, refs = refs[0], refs[1:8], refs[8:]
    q_ref, k_ref, v_ref, mixed_ref, inverse_ref, cols_ref, weights_ref, tokens_ref = refs[:8]
    parts, sems, slot_sems = refs[8], refs[9], refs[10]
    rank = place[0]
    width = q_ref.shape[1]
    rows = context_ref.shape[1]
    step = parts.shape[3]
    spans = [slice(pair * 2 * rows, (pair + 1) * 2 * rows) for pair in range(4)]
    fetched = fetch(quarters, [parts.at[at] for at in range(4)], slot_sems)
    held = [tokens_ref.at[at * rows : (at + 1) * rows] for at in range(8)]
    fetched_slots = fetch(slots, held, slot_sems.at[4:12])
    for copy in fetched:
        copy.wait()
    put_columns(place, parts, cols_ref)
    scale = HEAD_DIM ** (-0.5)
    for pair, span in enumerate(spans):
        fetched_slots[2 * pair].wait()
        fetched_slots[2 * pair + 1].wait()
        projected = dot(tokens_ref[span], cols_ref[...])
        q_ref[span] = ((projected[:, :width] + bias_ref[0]) * scale).astype(LOW)
        k_ref[span] = projected[:, width : 2 * width].astype(LOW)
        v_ref[span] = (projected[:, 2 * width :] + bias_ref[1]).astype(LOW)
    copies = []
    for at, ref in enumerate((q_ref, k_ref, v_ref, cols_ref)):
        copies.append(pltpu.make_async_copy(ref, kept[at + 2 * (at == 3)], sems.at[12 + at]))
    for copy in copies:
        copy.start()

    def block_copies(pair, span):
        pairs = (
            (mixed_ref.at[span], kept[3].at[span]),
            (inverse_ref.at[span], kept[4].at[span]),
            (weights_ref.at[:, span], kept[6].at[:, span]),
        )
        return [
            pltpu.make_async_copy(*both, sems.at[pair + 4 * at]) for at, both in enumerate(pairs)
        ]

    @pl.loop(0, 4)
    def _(pair):
        span = pl.ds(pl.multiple_of(pair * 2 * rows, 2 * rows), 2 * rows)
        for at in range(width // HEAD_DIM):
            cols = slice(at * HEAD_DIM, (at + 1) * HEAD_DIM)
            scores = dot_rows(q_ref[span, cols], k_ref[:, cols])
            weights = jnp.exp(scores - jnp.max(scores, axis=-1, keepdims=True))
            inverse = 1.0 / jnp.sum(weights, axis=-1, keepdims=True)
            weights = weights.astype(LOW)
            weights_ref[at, span] = weights
            mixed_ref[span, cols] = dot(weights, v_ref[:, cols]) * inverse
            inverse_ref[span, cols] = jnp.broadcast_to(inverse, (2 * rows, HEAD_DIM))
        first = lax.bitwise_xor(rank, 2 * pair)
        mixed = mixed_ref[span].astype(LOW)
        context_ref[first] = mixed[:rows]
        context_ref[lax.bitwise_xor(first, 1)] = mixed[rows:]
        for copy in block_copies(pair, span):
            copy.start()

    for pair, span in enumerate(spans):
        copies += block_copies(pair, span)
    for copy in copies:
        copy.wait()


def attend_back_kernel(place, grad_ref, *refs):
    kept, refs = refs[:6], refs[6:]
    out_ref, q_ref, k_ref, v_ref, mixed_ref, inverse_ref, weights_ref = refs[:7]
    dk_sum, dv_sum, sems = refs[7:]
    rank = place[0]
    rows, width = grad_ref.shape[1:]
    scale = HEAD_DIM ** (-0.5)
    copies = []
    for at, ref in enumerate((q_ref, k_ref, v_ref, mixed_ref, inverse_ref)):
        copies.append(pltpu.make_async_copy(kept[at], ref, sems.at[4 + at]))

    def block_copy(pair, span):
        return pltpu.make_async_copy(kept[5].at[:, span], weights_ref.at[:, span], sems.at[pair])

    for copy in copies:
        copy.start()
    for pair in range(4):
        block_copy(pair, slice(pair * 2 * rows, (pair + 1) * 2 * rows)).start()
    dk_sum[...] = jnp.zeros_like(dk_sum)
    dv_sum[...] = jnp.zeros_like(dv_sum)
    for copy in copies:
        copy.wait()

    @pl.loop(0, 4)
    def _(pair):
        span = pl.ds(pl.multiple_of(pair * 2 * rows, 2 * rows), 2 * rows)
        block_copy(pair, span).wait()
        first = lax.bitwise_xor(rank, 2 * pair)
        second = lax.bitwise_xor(first, 1)
        grad_all = jnp.concatenate([grad_ref[first], grad_ref[second]], axis=0)
        inverse = inverse_ref[span]
        q_scaled = (q_ref[span].astype(FULL) * inverse).astype(LOW)
        g_scaled = (grad_all.astype(FULL) * inverse).astype(LOW)
        product = grad_all.astype(FULL) * mixed_ref[span]
        for at in range(width // HEAD_DIM):
            cols = slice(at * HEAD_DIM, (at + 1) * HEAD_DIM)
            delta = jnp.sum(product[:, cols], axis=-1, keepdims=True)
            weights = weights_ref[at, span]
            dprobs = dot_rows(grad_all[:, cols], v_ref[:, cols])
            dscores = (weights.astype(FULL) * (dprobs - delta)).astype(LOW)
            dq = (dot(dscores, k_ref[:, cols]) * inverse[:, cols]).astype(LOW) * LOW(scale)
            out_ref[first, :, cols] = dq[:rows]
            out_ref[second, :, cols] = dq[rows:]
            dk_sum[cols] += dot_cols(q_scaled[:, cols], dscores)
            dv_sum[cols] += dot_cols(g_scaled[:, cols], weights)

    dk = dk_sum[...].T.astype(LOW)
    dv = dv_sum[...].T.astype(LOW)
    for at in range(8):
        whose = lax.bitwise_xor(rank, at)
        out_ref[whose, :, width : 2 * width] = dk[at * rows : (at + 1) * rows]
        out_ref[whose, :, 2 * width :] = dv[at * rows : (at + 1) * rows]


def normalize(values):
    center = values - jnp.mean(values, axis=-1, keepdims=True)
    scale = lax.rsqrt(jnp.mean(center * center, axis=-1, keepdims=True) + 1e-05)
    return center * scale, scale


def normalize_back(cotangent, gain, normed, scale):
    dn = cotangent * gain
    inner = jnp.mean(dn, axis=-1, keepdims=True)
    outer = jnp.mean(dn * normed, axis=-1, keepdims=True)
    return scale * (dn - inner - normed * outer)


def quarter_span(place, at, size):
    return pl.ds(pl.multiple_of(lax.bitwise_xor(place[1], at) * size, size), size)


def fetch_out(place, sources, held, sems):
    own = held.shape[1]
    copies = []
    for at, source in enumerate(sources):
        for part in range(2):
            start = (2 * lax.bitwise_xor(place[1], at) + part) * own
            span = pl.ds(pl.multiple_of(start, own), own)
            copies.append(
                pltpu.make_async_copy(
                    source.at[:, part], held.at[:, :, span], sems.at[2 * at + part]
                )
            )
    for copy in copies:
        copy.start()
    return copies


def mix_kernel(
    place, context_ref, tokens_ref, vec_ref, *refs
):
    sources, refs = refs[:4], refs[4:]
    middle_ref, low_ref, norm_ref, scale_ref, left_ref, out_ref, sems = refs
    copies = fetch_out(place, sources, out_ref, sems)
    own = context_ref.shape[2]
    for at in range(8):
        left_ref[:, at * own : (at + 1) * own] = context_ref[at]
    for copy in copies:
        copy.wait()
    attended = dot(left_ref[...], out_ref[...].reshape(8 * own, 8 * own))
    norm, scale = normalize(tokens_ref[...].astype(FULL) + (attended + vec_ref[6:7]))
    middle = norm * vec_ref[0:1] + vec_ref[2:3]
    middle_ref[...] = middle
    low_ref[...] = middle.astype(LOW)
    norm_ref[...] = norm
    scale_ref[...] = scale


def fetch_units(place, sources, w_in, w_out, sems, first):
    ins = [(sources[0], w_in.at[0])]
    outs = [(sources[1], w_out.at[0])]
    for at, source in enumerate(sources[2:]):
        span = quarter_span(place, at, source.shape[1])
        ins.append((source.at[0], w_in.at[1, span]))
        outs.append((source.at[1], w_out.at[1, span]))
    order = ins[:1] + outs[:1] + ins[1:] + outs[1:]
    if first == 1:
        order = outs[:1] + ins[:1] + outs[1:] + ins[1:]
    copies = [pltpu.make_async_copy(*both, sems.at[at]) for at, both in enumerate(order)]
    for copy in copies:
        copy.start()

    def wait(part, which):
        if part % 2 == 0:
            start = 2 + 4 * which if part else which
            for copy in copies[start : start + 4] if part else copies[start : start + 1]:
                copy.wait()

    return wait


def ffn_kernel(place, first_ref, second_ref, *refs):
    bias_ref, sources, refs = refs[0], refs[1:7], refs[7:]
    pre_ref, act_ref, near_ref, away_ref, sum_ref, w_in, w_out, sems = refs
    wait = fetch_units(place, sources, w_in, w_out, sems, 0)
    rows = first_ref.shape[0]
    step = bias_ref.shape[2]
    both = jnp.concatenate([first_ref[...], second_ref[...]], axis=0)
    for part in range(4):
        span = slice(part * 2 * step, (part + 1) * 2 * step)
        shard, rows_of = part // 2, slice(part % 2 * 2 * step, (part % 2 + 1) * 2 * step)
        whose = place[4] * 4 + lax.bitwise_xor(place[5], 2 * shard)
        bias = [bias_ref[whose * 4 + part % 2 * 2 + at] for at in range(2)]
        wait(part, 0)
        pre = dot_rows(both, w_in[shard, rows_of]) + jnp.concatenate(bias, axis=1)
        pre_ref[:, span] = pre
        act = (pre * (0.5 * (1.0 + lax.erf(pre * (0.5**0.5))))).astype(LOW)
        act_ref[:, span] = act
        wait(part, 1)
        term = dot(act, w_out[shard, rows_of])
        if part == 0:
            sum_ref[...] = term
        else:
            sum_ref[...] += term
    near_ref[...] = sum_ref[:rows]
    away_ref[...] = sum_ref[rows:].astype(LOW)


def ffn_back_kernel(place, first_ref, second_ref, slope_ref, *refs):
    sources, refs = refs[:6], refs[6:]
    grad_ref, near_ref, away_ref, units_ref, sum_ref, w_in, w_out, sems = refs
    wait = fetch_units(place, sources, w_in, w_out, sems, 1)
    rows = first_ref.shape[0]
    step = units_ref.shape[2]
    both = jnp.concatenate([first_ref[...], second_ref[...]], axis=0)
    for part in range(4):
        span = slice(part * 2 * step, (part + 1) * 2 * step)
        shard, rows_of = part // 2, slice(part % 2 * 2 * step, (part % 2 + 1) * 2 * step)
        wait(part, 0)
        grad = (dot_rows(both, w_out[shard, rows_of]) * slope_ref[:, span]).astype(LOW)
        grad_ref[:, span] = grad
        sums = jnp.sum(grad.astype(FULL), axis=0, keepdims=True)
        for at in range(2):
            half = lax.bitwise_xor(place[7], shard)
            units_ref[half * 4 + part % 2 * 2 + at] = sums[:, at * step : (at + 1) * step]
        wait(part, 1)
        term = dot(grad, w_in[shard, rows_of])
        if part == 0:
            sum_ref[...] = term
        else:
            sum_ref[...] += term
    near_ref[...] = sum_ref[:rows]
    away_ref[...] = sum_ref[rows:].astype(LOW)


def top_kernel(
    place, near_ref, sent_ref, far_ref, middle_ref, vec_ref, cotangent_ref,
    layer_ref, grad_ref, low_ref, sums_ref,
):
    summed = near_ref[...] + sent_ref[...].astype(FULL) + far_ref[...].astype(FULL)
    norm, scale = normalize(middle_ref[...] + summed + vec_ref[7:8])
    layer_ref[...] = norm * vec_ref[1:2] + vec_ref[3:4]
    cotangent = cotangent_ref[...].astype(FULL)
    grad = normalize_back(cotangent, vec_ref[1:2], norm, scale)
    grad_ref[...] = grad
    low_ref[...] = grad.astype(LOW)
    sums_ref[0:1] = jnp.sum(cotangent * norm, axis=0, keepdims=True)
    sums_ref[1:2] = jnp.sum(cotangent, axis=0, keepdims=True)
    sums_ref[2:3] = jnp.sum(grad.astype(LOW).astype(FULL), axis=0, keepdims=True)


def mix_back_kernel(
    place, near_ref, sent_ref, far_ref, grad_two_ref, norm_ref, scale_ref, vec_ref, *refs
):
    sources, refs = refs[:4], refs[4:]
    grad_ref, low_ref, context_ref, sums_ref, out_ref, sems = refs
    copies = fetch_out(place, sources, out_ref, sems)
    summed = near_ref[...] + sent_ref[...].astype(FULL) + far_ref[...].astype(FULL)
    grad_mid = grad_two_ref[...] + summed
    norm = norm_ref[...]
    grad = normalize_back(grad_mid, vec_ref[0:1], norm, scale_ref[...])
    grad_ref[...] = grad
    low_ref[...] = grad.astype(LOW)
    sums_ref[0:1] = jnp.sum(grad_mid * norm, axis=0, keepdims=True)
    sums_ref[1:2] = jnp.sum(grad_mid, axis=0, keepdims=True)
    sums_ref[2:3] = jnp.sum(grad.astype(LOW).astype(FULL), axis=0, keepdims=True)
    own = context_ref.shape[2]
    for copy in copies:
        copy.wait()
    total = dot_rows(low_ref[...], out_ref[...].reshape(8 * own, 8 * own)).astype(LOW)
    own = context_ref.shape[2]
    for at in range(8):
        context_ref[at] = total[:, at * own : (at + 1) * own]


def weight_grad_kernel(place, left_0, left_1, *refs):
    right, near_ref, away_ref = refs[:4], refs[4], refs[5]
    held_0, held_1, first, second, sems = refs[6:]
    rows = near_ref.shape[1]
    parts = [side.at[at * rows : (at + 1) * rows] for side in (first, second) for at in range(2)]
    for copy in fetch((left_0, left_1) + tuple(right), [held_0, held_1] + parts, sems):
        copy.wait()
    for stays in range(2):
        shard = place[6] if stays else 1 - place[6]
        for half in range(2):
            span = pl.ds(pl.multiple_of((2 * shard + half) * 2 * rows, 2 * rows), 2 * rows)
            both = dot_cols(held_0[:, span], first[...])
            both += dot_cols(held_1[:, span], second[...])
            for at in range(2):
                part = both[at * rows : (at + 1) * rows]
                slot = 2 * lax.bitwise_xor(place[3], at) + lax.bitwise_xor(place[7], half)
                if stays:
                    near_ref[slot] = part
                else:
                    away_ref[slot] = part.astype(LOW)


def out_grad_kernel(place, *refs):
    parts, grads, near_ref, away_ref, held, right, sems = refs[:4], refs[4:8], *refs[8:]
    step = near_ref.shape[1]
    rows = held.shape[2]
    sides = [right.at[at * rows : (at + 1) * rows] for at in range(4)]
    for copy in fetch(parts + grads, [held.at[at] for at in range(4)] + sides, sems):
        copy.wait()
    for stays in range(2):
        which = place[3] if stays else 1 - place[3]
        left = jnp.concatenate([held[at, which] for at in range(4)], axis=0)
        total = dot_cols(left, right[...])
        for at in range(4):
            slot = lax.bitwise_xor(place[5], at)
            if stays:
                near_ref[slot] = total[at * step : (at + 1) * step]
            else:
                away_ref[slot] = total[at * step : (at + 1) * step].astype(LOW)


def qkv_grad_kernel(place, *refs):
    grad_ref, top_ref, mid_ref, units_a, units_b = refs[:5]
    slots, refs = refs[5:13], refs[13:]
    near_ref, away_ref, total_ref, sums_ref, tokens_ref, sems = refs
    rows = grad_ref.shape[1]
    held = [tokens_ref.at[at * rows : (at + 1) * rows] for at in range(8)]
    copies = fetch(slots, held, sems)
    rank, seq_at = place[0], place[1]
    width = sums_ref.shape[1]
    own = width // 8
    quarter = width // 4
    col_sum = 0.0
    for pair in range(4):
        grads = [grad_ref[lax.bitwise_xor(rank, 2 * pair + at)] for at in range(2)]
        grads = jnp.concatenate(grads, axis=0)
        copies[2 * pair].wait()
        copies[2 * pair + 1].wait()
        term = dot_cols(tokens_ref[2 * pair * rows : 2 * (pair + 1) * rows], grads)
        col_sum += jnp.sum(grads.astype(FULL), axis=0, keepdims=True)
        if pair == 0:
            total_ref[...] = term
        else:
            total_ref[...] += term
    sums_ref[...] = jnp.zeros_like(sums_ref)
    sums_ref[0:1] = mid_ref[0:1]
    sums_ref[1:2] = top_ref[0:1]
    sums_ref[2:3] = mid_ref[1:2]
    sums_ref[3:4] = top_ref[1:2]
    own_cols = pl.ds(pl.multiple_of(rank * own, own), own)
    sums_ref[4:5, own_cols] = col_sum[:, :own]
    sums_ref[5:6, own_cols] = col_sum[:, 2 * own :]
    sums_ref[6:7] = mid_ref[2:3]
    sums_ref[7:8] = top_ref[2:3]
    row_at = lax.broadcasted_iota(jnp.int32, (8, own), 0)
    for at in (1, 3, 0, 2):
        whose = lax.bitwise_xor(seq_at, at)
        part = total_ref[quarter_span(place, at, quarter)]
        sums = sums_ref[:, quarter_span(place, at, quarter)]
        here = lax.shift_right_logical(whose, 1) == place[4]
        first = 4 * lax.bitwise_and(whose, 1)
        units = [units_a[first + row] + units_b[first + row] for row in range(4)]
        mine = (row_at >= 4 * place[8]) & (row_at < 4 * place[8] + 4)
        units = jnp.where(mine & here, jnp.concatenate(units + units, axis=0), 0.0)
        sums = jnp.concatenate([sums, units], axis=1)
        sums = jnp.concatenate([sums, jnp.zeros_like(sums)], axis=0)
        if at % 2:
            away_ref[at // 2, :quarter] = part.astype(LOW)
            away_ref[at // 2, quarter:] = sums.astype(LOW)
        else:
            near_ref[at // 2, :quarter] = part
            near_ref[at // 2, quarter:] = sums


def input_terms_kernel(place, across_ref, own_ref, *refs):
    sources, refs = refs[:5], refs[5:]
    near_ref, away_ref, cols_ref, beyond_ref, parts, sems = refs
    copies = fetch(sources, [cols_ref] + [parts.at[at] for at in range(4)], sems)
    rows = own_ref.shape[1]
    for copy in copies:
        copy.wait()
    put_columns(place, parts, beyond_ref)
    for slots in ((1, 3), (0, 2)):
        whose = [lax.bitwise_xor(place[5], slot) for slot in slots]
        left = jnp.concatenate([own_ref[place[4] * 4 + at] for at in whose], axis=0)
        term = dot_rows(left, cols_ref[...])
        left = jnp.concatenate([across_ref[at] for at in whose], axis=0)
        term += dot_rows(left, beyond_ref[...])
        for at, slot in enumerate(slots):
            part = term[at * rows : (at + 1) * rows]
            if slot % 2:
                away_ref[at] = part.astype(LOW)
            else:
                near_ref[at] = part


def qkv_send_kernel(place, near_ref, far_ref, out_ref):
    total = near_ref[...] + far_ref[...].astype(FULL)
    rows = total.shape[0] - 16
    step = rows // 8
    sums = total[rows:].astype(LOW)
    for at in range(8):
        out_ref[at, :step] = total[at * step : (at + 1) * step].astype(LOW)
        out_ref[at, step:] = sums


def qkv_last_kernel(place, parts_ref, grad_ref, sums_ref):
    step = grad_ref.shape[0]
    own = parts_ref.shape[2] // 3
    for at in range(8):
        for which in range(3):
            cols = slice((which * 8 + at) * own, (which * 8 + at + 1) * own)
            grad_ref[:, cols] = parts_ref[at, :step, which * own : (which + 1) * own].astype(FULL)
    sums = parts_ref[0, step:].astype(FULL)
    for at in range(1, 8):
        sums += parts_ref[at, step:].astype(FULL)
    sums_ref[...] = sums


def grouped_body(tokens, out_grad, w_qkv, w_out, fc_in, fc_out, fc_in_bias, vectors):
    rows, width = tokens.shape
    own = width // 8
    seq_at = lax.axis_index("seq")
    core_at, across_at = lax.rem(seq_at, 2), seq_at // 2
    head_at, blk_at = lax.axis_index("head"), lax.axis_index("blk")
    rank = head_at * 4 + blk_at
    far_at, near_at = blk_at // 2, lax.rem(blk_at, 2)
    place = jnp.stack(
        [rank, seq_at, core_at, across_at, head_at, blk_at, far_at ^ core_at, far_at, near_at]
    ).astype(jnp.int32)
    unit_rows = fc_in.shape[0] // 4
    units = 8 * unit_rows

    quarter = own // 4
    qkv_rows = lax.dynamic_slice_in_dim(w_qkv, seq_at * quarter, quarter, 0)
    qkv_rows = qkv_rows.reshape(quarter, 3, 8, own).transpose(2, 1, 0, 3)
    qkv_rows = qkv_rows.reshape(8, 3 * quarter, own)
    small = jnp.concatenate([vectors.T, fc_in_bias.reshape(-1, own)], axis=0)
    small = jnp.broadcast_to(small[None], (8, 12, own))
    to_swap = jnp.concatenate([qkv_rows, small, jnp.zeros((8, 4, own), LOW)], axis=1)
    out_quarter = lax.dynamic_slice_in_dim(w_out, seq_at * 2 * own, 2 * own, 1)
    out_quarter = out_quarter.reshape(own, 2, own).transpose(1, 0, 2).reshape(1, 2 * own, own)
    out_quarter = jnp.broadcast_to(out_quarter, (8, 2 * own, own))
    units_away = jnp.stack(
        [lax.dynamic_slice_in_dim(w, seq_at * unit_rows, unit_rows, 0) for w in (fc_in, fc_out)]
    )

    inner = inner_blk()
    first = lax.ppermute(tokens, "blk", PAIRS)
    middle = lax.ppermute(tokens, "blk", INNER)
    across_0 = flip_head(tokens)
    first, middle, across_0, to_swap = after((first, middle, across_0, to_swap))
    second_in = lax.ppermute(first, "blk", INNER)
    second_out = lax.ppermute(middle, "blk", OUTER)
    across_1 = flip_head(first)
    swapped = lax.all_to_all(to_swap, GROUP, 0, 0, tiled=True)
    second_in, second_out, across_1, swapped, out_quarter = after(
        (second_in, second_out, across_1, swapped, out_quarter)
    )
    out_quarter = lax.all_to_all(out_quarter, GROUP, 0, 0, tiled=True).reshape(8, 2, own, own)
    third = lax.ppermute(second_in, "blk", OUTER)
    second = jnp.where(inner, second_in, second_out)
    across_2 = flip_head(second)
    qkv_own = swapped[:, : 3 * quarter].reshape(8, 3, quarter, own)
    qkv_across = lax.ppermute(qkv_own, "seq", ACROSS)
    small = swapped[:, 3 * quarter : 3 * quarter + 12].astype(FULL)
    vec = small[:, :8].transpose(1, 0, 2).reshape(8, width)
    bias_all = small[:, 8:].reshape(32, 1, own)
    third, across_2, qkv_own, qkv_across = after((third, across_2, qkv_own, qkv_across))
    third = jnp.where(inner, middle, third)
    across_3 = flip_head(third)
    qkv_quarters = [qkv_own, lax.ppermute(qkv_own, "seq", CORE)]
    qkv_quarters += [qkv_across, lax.ppermute(qkv_across, "seq", CORE)]
    across_3, out_quarter, units_away, *qkv_quarters = after(
        [across_3, out_quarter, units_away] + qkv_quarters
    )
    beyond = flip_head(qkv_quarters[0])
    slots = [tokens, first, second, third, across_0, across_1, across_2, across_3]

    units_two_on = lax.ppermute(units_away, "blk", TWO_ON)
    bias = vectors.T.reshape(8, 1, own)[4:6].astype(FULL)
    seq_rows = 8 * rows
    heads = own // HEAD_DIM
    kept_shapes = [((seq_rows, own), LOW)] * 3 + [((seq_rows, own), FULL)] * 2
    kept_shapes.append(((width, 3 * own), LOW))
    kept_shapes.append(((heads, seq_rows, seq_rows), LOW))
    kept_scratch = [pltpu.VMEM(*shape) for shape in kept_shapes]
    context, *kept = call(
        attend_kernel,
        [shape_of((8, rows, own), LOW)] + [shape_of(*shape) for shape in kept_shapes],
        place, bias, *qkv_quarters, *slots,
        scratch=kept_scratch
        + [pltpu.VMEM((seq_rows, width), LOW), pltpu.VMEM((4, 8, 3, quarter, own), LOW)]
        + [pltpu.SemaphoreType.DMA((16,)), pltpu.SemaphoreType.DMA((12,))],
        flops=8 * 10**9,
        far_in=12,
        far_out=7,
        vmem=56,
    )
    out_across = lax.ppermute(out_quarter, "seq", ACROSS)
    context, out_across, out_quarter = after((context, out_across, out_quarter))
    out_slots = [out_quarter, lax.ppermute(out_quarter, "seq", CORE)]
    out_slots += [out_across, lax.ppermute(out_across, "seq", CORE)]
    context = lax.all_to_all(context, GROUP, 0, 0, tiled=True)
    beyond = after(beyond, *out_slots[1:])
    beyond_across = lax.ppermute(beyond, "seq", ACROSS)
    beyond_quarters = [beyond, lax.ppermute(beyond, "seq", CORE)]
    beyond_quarters += [beyond_across, lax.ppermute(beyond_across, "seq", CORE)]
    ffn_weights = [fc_in, fc_out] + gather_seq(units_two_on)
    out_scratch = [pltpu.VMEM((8, own, width), LOW), pltpu.SemaphoreType.DMA((8,))]

    per_row = shape_of((rows, width), FULL)
    per_row_low = shape_of((rows, width), LOW)
    middle, middle_low, norm_one, scale_one = call(
        mix_kernel,
        [per_row, per_row_low, per_row, shape_of((rows, 1), FULL)],
        place, context, tokens, vec, *out_slots,
        scratch=[pltpu.VMEM((rows, width), LOW)] + out_scratch,
        flops=2 * 10**9,
        far_in=4,
    )

    both_rows = shape_of((2 * rows, units), FULL)
    both_rows_low = shape_of((2 * rows, units), LOW)
    middle_slots = gather_four(middle_low)
    ffn_scratch = [pltpu.VMEM((2 * rows, width), FULL)]
    ffn_scratch += [pltpu.VMEM((2, 4 * unit_rows, width), LOW)] * 2
    ffn_scratch += [pltpu.SemaphoreType.DMA((10,))]
    ffn_parts = []
    for at in (0, 2):
        ffn_parts.append(
            call(
                ffn_kernel,
                [both_rows, both_rows_low, per_row, per_row_low],
                place, middle_slots[at], middle_slots[at + 1], bias_all, *ffn_weights,
                scratch=ffn_scratch,
                flops=3 * 10**9,
                far_in=6,
            )
        )

    def features_of(core, head):
        both = lax.dynamic_index_in_dim(context.reshape(2, 2, 2, rows, own), core, 1, False)
        return lax.dynamic_index_in_dim(both, head, 1, False)

    diagonal = []
    for seq in range(4):
        for head in range(2):
            diagonal.append((seq * 2 + head, (seq ^ 1) * 2 + 1 - head))
    parts = [
        features_of(core_at, head_at),
        features_of(1 - core_at, head_at),
        features_of(core_at, 1 - head_at),
        features_of(1 - core_at, 1 - head_at),
    ]
    parts[1:] = after(parts[1:], ffn_parts[0][1])
    parts = [
        parts[0],
        lax.ppermute(parts[1], "seq", CORE),
        flip_head(parts[2]),
        lax.ppermute(parts[3], ("seq", "head"), tuple(diagonal)),
    ]

    def scatter_parts(near_part, far_part):
        sent_far = lax.ppermute(far_part[1], "blk", PAIRS).astype(FULL)
        far = flip_head((far_part[0] + sent_far).astype(LOW))
        return near_part[0], lax.ppermute(near_part[1], "blk", PAIRS), far

    weight_scratch = [pltpu.VMEM((2 * rows, units), LOW)] * 2
    weight_scratch += [pltpu.VMEM((2 * rows, width), LOW)] * 2 + [pltpu.SemaphoreType.DMA((6,))]
    terms = [shape_of((4, unit_rows, width), FULL), shape_of((4, unit_rows, width), LOW)]

    def weight_grads(lefts, rights):
        return call(
            weight_grad_kernel, terms, place, *lefts, *rights,
            scratch=weight_scratch, flops=2 * 10**9, far_in=6,
        )

    def add_low(near, sent):
        return near + sent.astype(FULL)

    summed = scatter_parts(ffn_parts[0][2:4], ffn_parts[1][2:4])
    summed = after(summed, *beyond_quarters)
    three_sums = shape_of((3, width), FULL)
    layer_output, grad_two, grad_ffn, top_sums = call(
        top_kernel,
        [per_row, per_row, per_row_low, three_sums],
        place, *summed, middle, vec, out_grad,
        flops=10**9,
    )

    grad_ffn_slots = gather_four(grad_ffn)
    back_parts = []
    for at in (0, 2):
        pre = ffn_parts[at // 2][0]
        cdf = 0.5 * (1.0 + lax.erf(pre * (0.5**0.5)))
        slope = cdf + pre * jnp.exp(-0.5 * pre * pre) * ((2.0 * math.pi) ** -0.5)
        back_parts.append(
            call(
                ffn_back_kernel,
                [both_rows_low, per_row, per_row_low, shape_of((8, 1, unit_rows), FULL)],
                place, grad_ffn_slots[at], grad_ffn_slots[at + 1], slope, *ffn_weights,
                scratch=ffn_scratch,
                flops=3 * 10**9,
                far_in=6,
            )
        )
    summed = scatter_parts(back_parts[0][1:3], back_parts[1][1:3])
    grad_one, grad_attn, grad_context, mid_sums = call(
        mix_back_kernel,
        [per_row, per_row_low, shape_of((8, rows, own), LOW), three_sums],
        place, *summed, grad_two, norm_one, scale_one, vec, *out_slots,
        scratch=out_scratch,
        flops=2 * 10**9,
        far_in=4,
    )
    grad_context = lax.all_to_all(grad_context, GROUP, 0, 0, tiled=True)
    acts = after((ffn_parts[0][1], ffn_parts[1][1]), grad_one)
    out_near_grad, out_away_grad = weight_grads(acts, grad_ffn_slots)
    out_sent = lax.ppermute(out_away_grad, "seq", CORE)
    out_across = lax.ppermute(
        add_low(out_near_grad[2:], out_sent[2:]).astype(LOW), "seq", ACROSS
    )
    in_near_grad, in_away_grad = weight_grads((back_parts[0][0], back_parts[1][0]), middle_slots)
    in_sent = lax.ppermute(in_away_grad, "seq", CORE)
    attn_across = flip_head(grad_attn)

    def kept_here(near, sent, across, at):
        return add_low(near[at] + sent[at].astype(FULL), across[at])

    in_across = add_low(in_near_grad[2:], in_sent[2:]).astype(LOW)
    out_last = kept_here(out_near_grad, out_sent, out_across, 1).astype(LOW)
    grad_context, in_across, out_last, attn_across = after(
        (grad_context, in_across, out_last, attn_across)
    )
    in_across = lax.ppermute(in_across, "seq", ACROSS)
    out_last = lax.ppermute(out_last, "blk", TWO_ON)
    grad_attn_slots = [grad_attn, lax.ppermute(grad_attn, "seq", CORE)]
    grad_attn_slots += [attn_across, lax.ppermute(attn_across, "seq", CORE)]
    (grad_cols,) = call(
        attend_back_kernel,
        [shape_of((8, rows, 3 * own), LOW)],
        place, grad_context, *kept[:5], kept[6],
        scratch=kept_scratch[:5]
        + kept_scratch[6:]
        + [pltpu.VMEM((own, seq_rows), FULL)] * 2
        + [pltpu.SemaphoreType.DMA((9,))],
        flops=8 * 10**9,
        far_in=6,
        vmem=56,
    )

    cols_sent = lax.dynamic_slice_in_dim(grad_cols, (1 - head_at) * 4, 4, 0)
    cols_sent = flip_head(cols_sent)
    in_last = kept_here(in_near_grad, in_sent, in_across, 1).astype(LOW)
    in_last = lax.ppermute(in_last, "blk", TWO_ON)
    payload_rows = 2 * own + 16
    near, away = call(
        qkv_grad_kernel,
        [shape_of((2, payload_rows, 3 * own), FULL), shape_of((2, payload_rows, 3 * own), LOW)],
        place, grad_cols, top_sums, mid_sums, back_parts[0][3], back_parts[1][3], *slots,
        scratch=[pltpu.VMEM((width, 3 * own), FULL), pltpu.VMEM((8, width), FULL)]
        + [pltpu.VMEM((seq_rows, width), LOW), pltpu.SemaphoreType.DMA((8,))],
        flops=2 * 10**9,
        far_in=8,
    )
    sent = lax.ppermute(away, "seq", CORE)
    near_terms, away_terms = call(
        input_terms_kernel,
        [
            shape_of((2, rows, width), FULL),
            shape_of((2, rows, width), LOW),
        ],
        place, cols_sent, grad_cols, kept[5], *beyond_quarters,
        scratch=[pltpu.VMEM((width, 3 * own), LOW)] * 2
        + [pltpu.VMEM((4, 8, 3, quarter, own), LOW), pltpu.SemaphoreType.DMA((5,))],
        flops=2 * 10**9,
        far_in=5,
    )
    sent_terms = lax.ppermute(away_terms, "blk", PAIRS)
    out_terms = [shape_of((4, own // 4, width), FULL), shape_of((4, own // 4, width), LOW)]
    near_rows, away_rows = call(
        out_grad_kernel, out_terms, place, *parts, *after(grad_attn_slots, away_terms),
        scratch=[pltpu.VMEM((4, 2, rows, own), LOW), pltpu.VMEM((4 * rows, width), LOW)]
        + [pltpu.SemaphoreType.DMA((8,))],
        flops=10**9,
        far_in=8,
    )
    sent_rows = lax.ppermute(away_rows, "seq", ACROSS)

    last_terms = after(add_low(near_terms[1], sent_terms[1]).astype(LOW), in_last)
    last_terms = lax.ppermute(last_terms, "blk", TWO_ON)
    out_rows = add_low(near_rows, sent_rows)
    sent_rows = lax.ppermute(out_rows.reshape(2, 2, -1, width)[:, 1].astype(LOW), "blk", PAIRS)
    last_rows = lax.ppermute(add_low(out_rows[2], sent_rows[1]).astype(LOW), "blk", TWO_ON)
    grad_w_out = add_low(add_low(out_rows[0], sent_rows[0]), last_rows)
    far = lax.ppermute(add_low(near[1], sent[1]).astype(LOW), "seq", ACROSS)
    unit_grads = jnp.stack(
        [
            add_low(kept_here(in_near_grad, in_sent, in_across, 0), in_last),
            add_low(kept_here(out_near_grad, out_sent, out_across, 0), out_last),
        ]
    )
    (payload,) = call(
        qkv_send_kernel,
        [shape_of((8, own // 4 + 16, 3 * own), LOW)],
        place, add_low(near[0], sent[0]), far,
    )
    payload = lax.all_to_all(payload, GROUP, 0, 0, tiled=True)
    input_grad = grad_one + add_low(add_low(near_terms[0], sent_terms[0]), last_terms)

    moves = []
    for across in range(2):
        for core in range(2):
            for head in range(2):
                for two_on in range(2):
                    for near_by in range(2):
                        start = (across * 2 + core) * 8 + head * 4 + two_on * 2 + near_by
                        stop = (head * 2 + core) * 8 + near_by * 4 + two_on * 2 + across
                        if start != stop:
                            moves.append((start, stop))
    stays = (across_at == head_at) & (head_at == near_at)

    moved = lax.ppermute(unit_grads.astype(LOW), ("seq", "head", "blk"), moves).astype(FULL)
    grad_fc_in, grad_fc_out = jnp.where(stays, unit_grads, moved)

    grad_w_qkv, sums = call(
        qkv_last_kernel,
        [shape_of((own // 4, 3 * width), FULL), shape_of((16, 3 * own), FULL)],
        place, payload,
    )
    grad_vectors = lax.dynamic_slice(sums, (0, rank * (own // 4)), (8, own // 4)).T
    grad_bias = lax.dynamic_slice(sums, (rank, 2 * own), (1, own)).reshape(own)
    return (
        layer_output,
        input_grad,
        grad_w_qkv,
        grad_w_out,
        grad_fc_in,
        grad_fc_out,
        grad_bias,
        grad_vectors,
    )


def solution(mesh):
    sizes = tuple(mesh.shape[name] for name in ("seq", "head", "blk"))
    return jax.shard_map(
        grouped_body if sizes == (4, 2, 4) else general_body,
        mesh=mesh,
        in_specs=(
            P(("seq", "head", "blk"), None),
            P(("seq", "head", "blk"), None),
            P(("head", "blk"), None),
            P(("head", "blk"), None),
            P(("head", "blk"), None),
            P(("head", "blk"), None),
            P(("head", "blk")),
            P(("head", "blk"), None),
        ),
        out_specs=(
            P(("seq", "head", "blk"), None),
            P(("seq", "head", "blk"), None),
            P(("seq", "head", "blk"), None),
            P(("seq", "head", "blk"), None),
            P(("seq", "head", "blk"), None),
            P(("seq", "head", "blk"), None),
            P(("seq", "head", "blk")),
            P(("seq", "head", "blk"), None),
        ),
        check_vma=False,
    )
```

```python
import math

import jax
import jax.numpy as jnp
from jax import lax
from jax.experimental import pallas as pl
from jax.experimental.pallas import tpu as pltpu
from jax.sharding import PartitionSpec as P

HEAD_DIM = 64


def layer_norm(values, gain_vec, shift_vec):
    center = values - jnp.mean(values, axis=-1, keepdims=True)
    spread = jnp.mean(center * center, axis=-1, keepdims=True)
    return center * lax.rsqrt(spread + 1e-05) * gain_vec + shift_vec


def gelu_exact(values):
    return jax.nn.gelu(values, approximate=False)


def split_heads(values):
    return values.reshape(values.shape[0], values.shape[1] // HEAD_DIM, HEAD_DIM)


def head_scores(left_rows, right_rows):
    return jnp.einsum("qhd,khd->hqk", left_rows, right_rows, preferred_element_type=jnp.float32)


def ffn_part(factors):
    middle_low, grad_pre_full, act_full, grad_ffn = factors
    return jnp.concatenate(
        [
            jnp.einsum("tf,td->fd", grad_pre_full, middle_low, preferred_element_type=jnp.float32),
            jnp.einsum("tf,td->fd", act_full, grad_ffn, preferred_element_type=jnp.float32),
        ],
        axis=1,
    )


def attn_part(factors, extra_cols):
    tokens, grad_proj, context, grad_attn = factors
    return jnp.concatenate(
        [
            jnp.einsum("tn,tc->nc", tokens, grad_proj, preferred_element_type=jnp.float32),
            jnp.einsum("tn,tc->nc", context, grad_attn, preferred_element_type=jnp.float32),
            extra_cols,
        ],
        axis=1,
    )


def general_body(tokens, out_grad, w_qkv, w_out, fc_in, fc_out, fc_in_bias, vectors):
    model_width = tokens.shape[1]
    hidden_units = fc_in.shape[0] * lax.axis_size(("head", "blk"))
    ratio = hidden_units // model_width
    scale = HEAD_DIM ** (-0.5)
    part_qkv = lax.all_gather(w_qkv, ("head", "blk"), axis=0, tiled=True)
    part_out = lax.all_gather(w_out, ("head", "blk"), axis=0, tiled=True)
    part_vec = lax.all_gather(vectors, ("head", "blk"), axis=0, tiled=True)
    part_rows = part_qkv.shape[0]
    projected = jnp.dot(tokens, part_qkv, preferred_element_type=jnp.float32)
    out_full = part_out
    attn_state = (projected, out_full, part_vec)
    projected = attn_state[0]
    out_full = attn_state[1]
    vec_float = attn_state[2].astype(jnp.float32)
    gain_one, gain_two = (vec_float[:, 0], vec_float[:, 1])
    shift_one, shift_two = (vec_float[:, 2], vec_float[:, 3])
    bias_query, bias_value = (vec_float[:, 4], vec_float[:, 5])
    bias_output, bias_ffn = (vec_float[:, 6], vec_float[:, 7])
    queries = ((projected[:, :model_width] + bias_query) * scale).astype(jnp.bfloat16)
    key_rows = projected[:, model_width : 2 * model_width].astype(jnp.bfloat16)
    value_rows = (projected[:, 2 * model_width :] + bias_value).astype(jnp.bfloat16)
    query_heads, key_heads, value_heads = (
        lax.all_to_all(queries, "head", split_axis=1, concat_axis=0, tiled=True),
        lax.all_to_all(key_rows, "head", split_axis=1, concat_axis=0, tiled=True),
        lax.all_to_all(value_rows, "head", split_axis=1, concat_axis=0, tiled=True),
    )
    query_split = split_heads(query_heads)
    group_rows = query_split.shape[0]
    group_width = key_heads.shape[1]
    seq_rows = group_rows * lax.axis_size("blk")
    portion = (
        lax.all_gather(key_heads, "blk", axis=0, tiled=True),
        lax.all_gather(value_heads, "blk", axis=0, tiled=True),
    )
    scores = head_scores(query_split, split_heads(portion[0]))
    run_sum = jnp.sum(jnp.exp(scores), axis=-1)
    key_all = portion[0]
    value_all = portion[1]
    run_sum, key_all, value_all = (run_sum, key_all, value_all)
    log_total = jnp.log(run_sum)
    block_rows = math.gcd(512, seq_rows)
    block_count = seq_rows // block_rows
    key_blocks = key_all.reshape(block_count, block_rows, group_width)
    value_blocks = value_all.reshape(block_count, block_rows, group_width)

    def mix_block(totals, pair):
        scores = head_scores(query_split, split_heads(pair[0]))
        probs_low = jnp.exp(scores - log_total[:, :, None]).astype(jnp.bfloat16)
        return (
            totals
            + jnp.einsum(
                "hqk,khd->qhd", probs_low, split_heads(pair[1]), preferred_element_type=jnp.float32
            ),
            None,
        )

    mixed, unused = lax.scan(
        mix_block, jnp.zeros(query_split.shape, jnp.float32), (key_blocks, value_blocks)
    )
    context = lax.all_to_all(
        mixed.reshape(group_rows, -1).astype(jnp.bfloat16),
        "head",
        split_axis=0,
        concat_axis=1,
        tiled=True,
    )
    attn_out = jnp.dot(context, out_full, preferred_element_type=jnp.float32) + bias_output
    residual_one = tokens.astype(jnp.float32) + attn_out
    middle, norm_one_back = jax.vjp(layer_norm, residual_one, gain_one, shift_one)
    middle_low = middle.astype(jnp.bfloat16)
    part_in = lax.all_gather(fc_in, ("head", "blk"), axis=0, tiled=True)
    part_out = lax.all_gather(fc_out, ("head", "blk"), axis=0, tiled=True)
    part_bias = lax.all_gather(fc_in_bias, ("head", "blk"), axis=0, tiled=True)
    pre_part = jnp.einsum("td,fd->tf", middle_low, part_in, preferred_element_type=jnp.float32)
    pre_part = pre_part + part_bias.astype(jnp.float32)
    act_part = gelu_exact(pre_part).astype(jnp.bfloat16)
    summed = jnp.dot(act_part, part_out, preferred_element_type=jnp.float32)
    ffn_pre_full = pre_part
    residual_two = middle + summed + bias_ffn
    layer_output, norm_two_back = jax.vjp(layer_norm, residual_two, gain_two, shift_two)
    grad_resid_two, grad_gain_two, grad_shift_two = norm_two_back(out_grad.astype(jnp.float32))
    grad_ffn = grad_resid_two.astype(jnp.bfloat16)
    qkv_flat = w_qkv.reshape(fc_in.shape[0], -1)
    portion = (
        lax.all_gather(fc_in, ("head", "blk"), axis=0, tiled=True),
        lax.all_gather(fc_out, ("head", "blk"), axis=0, tiled=True),
        lax.all_gather(qkv_flat, ("head", "blk"), axis=0, tiled=True),
    )
    part_in = portion[0]
    part_rows = part_in.shape[0]
    pre_part = ffn_pre_full
    grad_act = jnp.einsum("td,fd->tf", grad_ffn, portion[1], preferred_element_type=jnp.float32)
    grad_pre = jax.vjp(gelu_exact, pre_part)[1](grad_act)[0].astype(jnp.bfloat16)
    grad_mid = jnp.dot(grad_pre, part_in, preferred_element_type=jnp.float32)
    grad_mid, grad_pre_all = (grad_mid, grad_pre)
    qkv_gathered = portion[2]
    qkv_full = qkv_gathered.reshape(model_width, 3 * model_width)
    grad_resid_one, grad_gain_one, grad_shift_one = norm_one_back(grad_resid_two + grad_mid)
    grad_attn = grad_resid_one.astype(jnp.bfloat16)
    grad_context = jnp.einsum(
        "td,ed->te", grad_attn, out_full, preferred_element_type=jnp.float32
    ).astype(jnp.bfloat16)
    grad_ctx_heads = lax.all_to_all(grad_context, "head", split_axis=1, concat_axis=0, tiled=True)
    grad_ctx_split = split_heads(grad_ctx_heads)
    delta_heads = jnp.sum(grad_ctx_split.astype(jnp.float32) * mixed, axis=-1).T

    def back_block(grad_query, pair):
        key_part = split_heads(pair[0])
        value_part = split_heads(pair[1])
        scores = head_scores(query_split, key_part)
        probs = jnp.exp(scores - log_total[:, :, None])
        dprobs = head_scores(grad_ctx_split, value_part)
        dscores = (probs * (dprobs - delta_heads[:, :, None])).astype(jnp.bfloat16)
        grad_query = grad_query + jnp.einsum(
            "hqk,khd->qhd", dscores, key_part, preferred_element_type=jnp.float32
        )
        grad_key = jnp.einsum(
            "hqk,qhd->khd", dscores, query_split, preferred_element_type=jnp.float32
        )
        grad_value = jnp.einsum(
            "hqk,qhd->khd",
            probs.astype(jnp.bfloat16),
            grad_ctx_split,
            preferred_element_type=jnp.float32,
        )
        part_rows = pair[0].shape[0]
        return (
            grad_query,
            jnp.concatenate(
                [grad_key.reshape(part_rows, -1), grad_value.reshape(part_rows, -1)], axis=1
            ),
        )

    grad_query_heads, kv_terms = lax.scan(
        back_block, jnp.zeros(query_split.shape, jnp.float32), (key_blocks, value_blocks)
    )
    kv_own = lax.psum_scatter(
        kv_terms.reshape(seq_rows, 2 * group_width).astype(jnp.bfloat16),
        "blk",
        scatter_dimension=0,
        tiled=True,
    ).astype(jnp.float32)
    grad_query_tok, grad_key_tok, grad_value_tok = (
        lax.all_to_all(
            grad_query_heads.reshape(group_rows, -1).astype(jnp.bfloat16),
            "head",
            split_axis=0,
            concat_axis=1,
            tiled=True,
        ),
        lax.all_to_all(
            kv_own[:, :group_width].astype(jnp.bfloat16),
            "head",
            split_axis=0,
            concat_axis=1,
            tiled=True,
        ),
        lax.all_to_all(
            kv_own[:, group_width:].astype(jnp.bfloat16),
            "head",
            split_axis=0,
            concat_axis=1,
            tiled=True,
        ),
    )
    grad_proj = jnp.concatenate(
        [grad_query_tok * jnp.bfloat16(scale), grad_key_tok, grad_value_tok], axis=1
    )
    through_proj = jnp.einsum("tc,nc->tn", grad_proj, qkv_full, preferred_element_type=jnp.float32)
    input_grad = grad_resid_one + through_proj
    grad_proj_float = grad_proj.astype(jnp.float32)
    vec_term = jnp.stack(
        [
            grad_gain_one,
            grad_gain_two,
            grad_shift_one,
            grad_shift_two,
            jnp.sum(grad_proj_float[:, :model_width], axis=0),
            jnp.sum(grad_proj_float[:, 2 * model_width :], axis=0),
            jnp.sum(grad_attn.astype(jnp.float32), axis=0),
            jnp.sum(grad_ffn.astype(jnp.float32), axis=0),
        ],
        axis=1,
    )
    bias_term = jnp.sum(grad_pre_all.astype(jnp.float32), axis=0).reshape(model_width, -1)
    bias_cols = bias_term.shape[1]
    padding = jnp.zeros((model_width, 128 - 8 - bias_cols), jnp.float32)
    extra_cols = jnp.concatenate([vec_term, bias_term, padding], axis=1)
    rows_dev = hidden_units // lax.axis_size(("seq", "head", "blk"))
    ffn_block = ffn_part((middle_low, grad_pre_all, act_part, grad_ffn))
    attn_block = attn_part((tokens, grad_proj, context, grad_attn), extra_cols)
    merged = lax.psum_scatter(
        jnp.concatenate(
            [ffn_block, attn_block.reshape(lax.axis_size(("seq", "head", "blk")) * rows_dev, -1)],
            axis=1,
        ),
        ("seq", "head", "blk"),
        scatter_dimension=0,
        tiled=True,
    )
    grad_fc_in = merged[:, :model_width]
    grad_fc_out = merged[:, model_width : 2 * model_width]
    attn_grad = merged[:, 2 * model_width :].reshape(rows_dev // ratio, 4 * model_width + 128)
    grad_w_qkv = attn_grad[:, : 3 * model_width]
    grad_w_out = attn_grad[:, 3 * model_width : 4 * model_width]
    grad_vectors = attn_grad[:, 4 * model_width : 4 * model_width + 8]
    grad_fc_in_bias = attn_grad[:, 4 * model_width + 8 : 4 * model_width + 8 + bias_cols].reshape(
        -1
    )
    return (
        layer_output,
        input_grad,
        grad_w_qkv,
        grad_w_out,
        grad_fc_in,
        grad_fc_out,
        grad_fc_in_bias,
        grad_vectors,
    )


GROUP = ("head", "blk")
FLIP = ((0, 1), (1, 0))
PAIRS = ((0, 1), (1, 0), (2, 3), (3, 2))
INNER = ((1, 2), (2, 1))
OUTER = ((1, 0), (2, 3))
INWARD = ((0, 1), (3, 2))
TWO_ON = ((0, 2), (2, 0), (1, 3), (3, 1))
CORE = tuple((at, at ^ 1) for at in range(4))
ACROSS = tuple((at, at ^ 2) for at in range(4))
LOW = jnp.bfloat16
FULL = jnp.float32
ROWS_DIMS = (((1,), (1,)), ((), ()))
COLS_DIMS = (((0,), (0,)), ((), ()))


def dot(left, right):
    return jnp.dot(left, right, preferred_element_type=FULL)


def dot_rows(left, right):
    return lax.dot_general(left, right, ROWS_DIMS, preferred_element_type=FULL)


def dot_cols(left, right):
    return lax.dot_general(left, right, COLS_DIMS, preferred_element_type=FULL)


def after(values, *others):
    if not isinstance(values, (list, tuple)):
        return lax.optimization_barrier((values,) + others)[0]
    return lax.optimization_barrier(tuple(values) + others)[: len(values)]


def inner_blk():
    at = lax.axis_index("blk")
    return (at == 1) | (at == 2)


def flip_head(value):
    return lax.ppermute(value, "head", FLIP)


def gather_seq(own):
    across = lax.ppermute(own, "seq", ACROSS)
    return [own, lax.ppermute(own, "seq", CORE), across, lax.ppermute(across, "seq", CORE)]


def gather_four(own):
    across = flip_head(own)
    beside = lax.ppermute(own, "blk", PAIRS)
    return [own, beside, across, lax.ppermute(across, "blk", PAIRS)]


def gather_cores(own):
    across = flip_head(own)
    return [own, lax.ppermute(own, "seq", CORE), across, lax.ppermute(across, "seq", CORE)]


def shape_of(shape, dtype):
    return jax.ShapeDtypeStruct(shape, dtype)


def call(kernel, outs, place, *args, scratch=(), flops=0, vmem=28, far_in=0, far_out=0):
    moved = sum(arg.size * arg.dtype.itemsize for arg in args)
    moved += sum(math.prod(out.shape) * jnp.dtype(out.dtype).itemsize for out in outs)
    near = pl.BlockSpec(memory_space=pltpu.VMEM)
    far = pl.BlockSpec(memory_space=pltpu.HBM)
    return pl.pallas_call(
        kernel,
        out_shape=outs,
        in_specs=[pl.BlockSpec(memory_space=pltpu.SMEM)]
        + [near] * (len(args) - far_in)
        + [far] * far_in,
        out_specs=[near] * (len(outs) - far_out) + [far] * far_out,
        scratch_shapes=scratch,
        compiler_params=pltpu.CompilerParams(vmem_limit_bytes=vmem * 2**20),
        cost_estimate=pl.CostEstimate(flops=flops // 2, bytes_accessed=moved, transcendentals=0),
    )(place, *args)


def fetch(sources, held, sems):
    copies = [pltpu.make_async_copy(*both, sems.at[at]) for at, both in enumerate(zip(sources, held))]
    for copy in copies:
        copy.start()
    return copies


def put_columns(place, parts, cols_ref):
    step, width = parts.shape[3:]
    for at in range(8):
        for part in range(4):
            start = (4 * at + lax.bitwise_xor(place[1], part)) * step
            span = pl.ds(pl.multiple_of(start, step), step)
            for which in range(3):
                cols_ref[span, which * width : (which + 1) * width] = parts[part, at, which]


def attend_kernel(place, *refs):
    bias_ref, refs = refs[0], refs[1:]
    quarters, slots, refs = refs[:4], refs[4:12], refs[12:]
    context_ref, kept, refs = refs[0], refs[1:8], refs[8:]
    q_ref, k_ref, v_ref, mixed_ref, inverse_ref, cols_ref, weights_ref, tokens_ref = refs[:8]
    parts, sems, slot_sems = refs[8], refs[9], refs[10]
    rank = place[0]
    width = q_ref.shape[1]
    rows = context_ref.shape[1]
    step = parts.shape[3]
    spans = [slice(pair * 2 * rows, (pair + 1) * 2 * rows) for pair in range(4)]
    fetched = fetch(quarters, [parts.at[at] for at in range(4)], slot_sems)
    held = [tokens_ref.at[at * rows : (at + 1) * rows] for at in range(8)]
    fetched_slots = fetch(slots, held, slot_sems.at[4:12])
    for copy in fetched:
        copy.wait()
    put_columns(place, parts, cols_ref)
    scale = HEAD_DIM ** (-0.5)
    for pair, span in enumerate(spans):
        fetched_slots[2 * pair].wait()
        fetched_slots[2 * pair + 1].wait()
        projected = dot(tokens_ref[span], cols_ref[...])
        q_ref[span] = ((projected[:, :width] + bias_ref[0]) * scale).astype(LOW)
        k_ref[span] = projected[:, width : 2 * width].astype(LOW)
        v_ref[span] = (projected[:, 2 * width :] + bias_ref[1]).astype(LOW)
    copies = []
    for at, ref in enumerate((q_ref, k_ref, v_ref, cols_ref)):
        copies.append(pltpu.make_async_copy(ref, kept[at + 2 * (at == 3)], sems.at[12 + at]))
    for copy in copies:
        copy.start()

    def block_copies(pair, span):
        pairs = (
            (mixed_ref.at[span], kept[3].at[span]),
            (inverse_ref.at[span], kept[4].at[span]),
            (weights_ref.at[:, span], kept[6].at[:, span]),
        )
        return [
            pltpu.make_async_copy(*both, sems.at[pair + 4 * at]) for at, both in enumerate(pairs)
        ]

    @pl.loop(0, 4)
    def _(pair):
        span = pl.ds(pl.multiple_of(pair * 2 * rows, 2 * rows), 2 * rows)
        for at in range(width // HEAD_DIM):
            cols = slice(at * HEAD_DIM, (at + 1) * HEAD_DIM)
            scores = dot_rows(q_ref[span, cols], k_ref[:, cols])
            weights = jnp.exp(scores - jnp.max(scores, axis=-1, keepdims=True))
            inverse = 1.0 / jnp.sum(weights, axis=-1, keepdims=True)
            weights = weights.astype(LOW)
            weights_ref[at, span] = weights
            mixed_ref[span, cols] = dot(weights, v_ref[:, cols]) * inverse
            inverse_ref[span, cols] = jnp.broadcast_to(inverse, (2 * rows, HEAD_DIM))
        first = lax.bitwise_xor(rank, 2 * pair)
        mixed = mixed_ref[span].astype(LOW)
        context_ref[first] = mixed[:rows]
        context_ref[lax.bitwise_xor(first, 1)] = mixed[rows:]
        for copy in block_copies(pair, span):
            copy.start()

    for pair, span in enumerate(spans):
        copies += block_copies(pair, span)
    for copy in copies:
        copy.wait()


def attend_back_kernel(place, grad_ref, *refs):
    kept, refs = refs[:6], refs[6:]
    out_ref, q_ref, k_ref, v_ref, mixed_ref, inverse_ref, weights_ref = refs[:7]
    dk_sum, dv_sum, sems = refs[7:]
    rank = place[0]
    rows, width = grad_ref.shape[1:]
    scale = HEAD_DIM ** (-0.5)
    copies = []
    for at, ref in enumerate((q_ref, k_ref, v_ref, mixed_ref, inverse_ref)):
        copies.append(pltpu.make_async_copy(kept[at], ref, sems.at[4 + at]))

    def block_copy(pair, span):
        return pltpu.make_async_copy(kept[5].at[:, span], weights_ref.at[:, span], sems.at[pair])

    for copy in copies:
        copy.start()
    for pair in range(4):
        block_copy(pair, slice(pair * 2 * rows, (pair + 1) * 2 * rows)).start()
    dk_sum[...] = jnp.zeros_like(dk_sum)
    dv_sum[...] = jnp.zeros_like(dv_sum)
    for copy in copies:
        copy.wait()

    @pl.loop(0, 4)
    def _(pair):
        span = pl.ds(pl.multiple_of(pair * 2 * rows, 2 * rows), 2 * rows)
        block_copy(pair, span).wait()
        first = lax.bitwise_xor(rank, 2 * pair)
        second = lax.bitwise_xor(first, 1)
        grad_all = jnp.concatenate([grad_ref[first], grad_ref[second]], axis=0)
        inverse = inverse_ref[span]
        q_scaled = (q_ref[span].astype(FULL) * inverse).astype(LOW)
        g_scaled = (grad_all.astype(FULL) * inverse).astype(LOW)
        product = grad_all.astype(FULL) * mixed_ref[span]
        for at in range(width // HEAD_DIM):
            cols = slice(at * HEAD_DIM, (at + 1) * HEAD_DIM)
            delta = jnp.sum(product[:, cols], axis=-1, keepdims=True)
            weights = weights_ref[at, span]
            dprobs = dot_rows(grad_all[:, cols], v_ref[:, cols])
            dscores = (weights.astype(FULL) * (dprobs - delta)).astype(LOW)
            dq = (dot(dscores, k_ref[:, cols]) * inverse[:, cols]).astype(LOW) * LOW(scale)
            out_ref[first, :, cols] = dq[:rows]
            out_ref[second, :, cols] = dq[rows:]
            dk_sum[cols] += dot_cols(q_scaled[:, cols], dscores)
            dv_sum[cols] += dot_cols(g_scaled[:, cols], weights)

    dk = dk_sum[...].T.astype(LOW)
    dv = dv_sum[...].T.astype(LOW)
    for at in range(8):
        whose = lax.bitwise_xor(rank, at)
        out_ref[whose, :, width : 2 * width] = dk[at * rows : (at + 1) * rows]
        out_ref[whose, :, 2 * width :] = dv[at * rows : (at + 1) * rows]


def normalize(values):
    center = values - jnp.mean(values, axis=-1, keepdims=True)
    scale = lax.rsqrt(jnp.mean(center * center, axis=-1, keepdims=True) + 1e-05)
    return center * scale, scale


def normalize_back(cotangent, gain, normed, scale):
    dn = cotangent * gain
    inner = jnp.mean(dn, axis=-1, keepdims=True)
    outer = jnp.mean(dn * normed, axis=-1, keepdims=True)
    return scale * (dn - inner - normed * outer)


def quarter_span(place, at, size):
    return pl.ds(pl.multiple_of(lax.bitwise_xor(place[1], at) * size, size), size)


def fetch_out(place, sources, held, sems):
    own = held.shape[1]
    copies = []
    for at, source in enumerate(sources):
        for part in range(2):
            start = (2 * lax.bitwise_xor(place[1], at) + part) * own
            span = pl.ds(pl.multiple_of(start, own), own)
            copies.append(
                pltpu.make_async_copy(
                    source.at[:, part], held.at[:, :, span], sems.at[2 * at + part]
                )
            )
    for copy in copies:
        copy.start()
    return copies


def mix_kernel(
    place, context_ref, tokens_ref, vec_ref, *refs
):
    sources, refs = refs[:4], refs[4:]
    middle_ref, low_ref, norm_ref, scale_ref, left_ref, out_ref, sems = refs
    copies = fetch_out(place, sources, out_ref, sems)
    own = context_ref.shape[2]
    for at in range(8):
        left_ref[:, at * own : (at + 1) * own] = context_ref[at]
    for copy in copies:
        copy.wait()
    attended = dot(left_ref[...], out_ref[...].reshape(8 * own, 8 * own))
    norm, scale = normalize(tokens_ref[...].astype(FULL) + (attended + vec_ref[6:7]))
    middle = norm * vec_ref[0:1] + vec_ref[2:3]
    middle_ref[...] = middle
    low_ref[...] = middle.astype(LOW)
    norm_ref[...] = norm
    scale_ref[...] = scale


def fetch_units(place, sources, w_in, w_out, sems, first):
    ins = [(sources[0], w_in.at[0])]
    outs = [(sources[1], w_out.at[0])]
    for at, source in enumerate(sources[2:]):
        span = quarter_span(place, at, source.shape[1])
        ins.append((source.at[0], w_in.at[1, span]))
        outs.append((source.at[1], w_out.at[1, span]))
    order = ins[:1] + outs[:1] + ins[1:] + outs[1:]
    if first == 1:
        order = outs[:1] + ins[:1] + outs[1:] + ins[1:]
    copies = [pltpu.make_async_copy(*both, sems.at[at]) for at, both in enumerate(order)]
    for copy in copies:
        copy.start()

    def wait(part, which):
        if part % 2 == 0:
            start = 2 + 4 * which if part else which
            for copy in copies[start : start + 4] if part else copies[start : start + 1]:
                copy.wait()

    return wait


def ffn_kernel(place, first_ref, second_ref, *refs):
    bias_ref, sources, refs = refs[0], refs[1:7], refs[7:]
    pre_ref, act_ref, near_ref, away_ref, sum_ref, w_in, w_out, sems = refs
    wait = fetch_units(place, sources, w_in, w_out, sems, 0)
    rows = first_ref.shape[0]
    step = bias_ref.shape[2]
    both = jnp.concatenate([first_ref[...], second_ref[...]], axis=0)
    for part in range(4):
        span = slice(part * 2 * step, (part + 1) * 2 * step)
        shard, rows_of = part // 2, slice(part % 2 * 2 * step, (part % 2 + 1) * 2 * step)
        whose = place[4] * 4 + lax.bitwise_xor(place[5], 2 * shard)
        bias = [bias_ref[whose * 4 + part % 2 * 2 + at] for at in range(2)]
        wait(part, 0)
        pre = dot_rows(both, w_in[shard, rows_of]) + jnp.concatenate(bias, axis=1)
        pre_ref[:, span] = pre
        act = (pre * (0.5 * (1.0 + lax.erf(pre * (0.5**0.5))))).astype(LOW)
        act_ref[:, span] = act
        wait(part, 1)
        term = dot(act, w_out[shard, rows_of])
        if part == 0:
            sum_ref[...] = term
        else:
            sum_ref[...] += term
    near_ref[...] = sum_ref[:rows]
    away_ref[...] = sum_ref[rows:].astype(LOW)


def ffn_back_kernel(place, first_ref, second_ref, slope_ref, *refs):
    sources, refs = refs[:6], refs[6:]
    grad_ref, near_ref, away_ref, units_ref, sum_ref, w_in, w_out, sems = refs
    wait = fetch_units(place, sources, w_in, w_out, sems, 1)
    rows = first_ref.shape[0]
    step = units_ref.shape[2]
    both = jnp.concatenate([first_ref[...], second_ref[...]], axis=0)
    for part in range(4):
        span = slice(part * 2 * step, (part + 1) * 2 * step)
        shard, rows_of = part // 2, slice(part % 2 * 2 * step, (part % 2 + 1) * 2 * step)
        wait(part, 0)
        grad = (dot_rows(both, w_out[shard, rows_of]) * slope_ref[:, span]).astype(LOW)
        grad_ref[:, span] = grad
        sums = jnp.sum(grad.astype(FULL), axis=0, keepdims=True)
        for at in range(2):
            half = lax.bitwise_xor(place[7], shard)
            units_ref[half * 4 + part % 2 * 2 + at] = sums[:, at * step : (at + 1) * step]
        wait(part, 1)
        term = dot(grad, w_in[shard, rows_of])
        if part == 0:
            sum_ref[...] = term
        else:
            sum_ref[...] += term
    near_ref[...] = sum_ref[:rows]
    away_ref[...] = sum_ref[rows:].astype(LOW)


def top_kernel(
    place, near_ref, sent_ref, far_ref, middle_ref, vec_ref, cotangent_ref,
    layer_ref, grad_ref, low_ref, sums_ref,
):
    summed = near_ref[...] + sent_ref[...].astype(FULL) + far_ref[...].astype(FULL)
    norm, scale = normalize(middle_ref[...] + summed + vec_ref[7:8])
    layer_ref[...] = norm * vec_ref[1:2] + vec_ref[3:4]
    cotangent = cotangent_ref[...].astype(FULL)
    grad = normalize_back(cotangent, vec_ref[1:2], norm, scale)
    grad_ref[...] = grad
    low_ref[...] = grad.astype(LOW)
    sums_ref[0:1] = jnp.sum(cotangent * norm, axis=0, keepdims=True)
    sums_ref[1:2] = jnp.sum(cotangent, axis=0, keepdims=True)
    sums_ref[2:3] = jnp.sum(grad.astype(LOW).astype(FULL), axis=0, keepdims=True)


def mix_back_kernel(
    place, near_ref, sent_ref, far_ref, grad_two_ref, norm_ref, scale_ref, vec_ref, *refs
):
    sources, refs = refs[:4], refs[4:]
    grad_ref, low_ref, context_ref, sums_ref, out_ref, sems = refs
    copies = fetch_out(place, sources, out_ref, sems)
    summed = near_ref[...] + sent_ref[...].astype(FULL) + far_ref[...].astype(FULL)
    grad_mid = grad_two_ref[...] + summed
    norm = norm_ref[...]
    grad = normalize_back(grad_mid, vec_ref[0:1], norm, scale_ref[...])
    grad_ref[...] = grad
    low_ref[...] = grad.astype(LOW)
    sums_ref[0:1] = jnp.sum(grad_mid * norm, axis=0, keepdims=True)
    sums_ref[1:2] = jnp.sum(grad_mid, axis=0, keepdims=True)
    sums_ref[2:3] = jnp.sum(grad.astype(LOW).astype(FULL), axis=0, keepdims=True)
    own = context_ref.shape[2]
    for copy in copies:
        copy.wait()
    total = dot_rows(low_ref[...], out_ref[...].reshape(8 * own, 8 * own)).astype(LOW)
    own = context_ref.shape[2]
    for at in range(8):
        context_ref[at] = total[:, at * own : (at + 1) * own]


def weight_grad_kernel(place, left_0, left_1, *refs):
    right, near_ref, away_ref = refs[:4], refs[4], refs[5]
    held_0, held_1, first, second, sems = refs[6:]
    rows = near_ref.shape[1]
    parts = [side.at[at * rows : (at + 1) * rows] for side in (first, second) for at in range(2)]
    for copy in fetch((left_0, left_1) + tuple(right), [held_0, held_1] + parts, sems):
        copy.wait()
    for stays in range(2):
        shard = place[6] if stays else 1 - place[6]
        for half in range(2):
            span = pl.ds(pl.multiple_of((2 * shard + half) * 2 * rows, 2 * rows), 2 * rows)
            both = dot_cols(held_0[:, span], first[...])
            both += dot_cols(held_1[:, span], second[...])
            for at in range(2):
                part = both[at * rows : (at + 1) * rows]
                slot = 2 * lax.bitwise_xor(place[3], at) + lax.bitwise_xor(place[7], half)
                if stays:
                    near_ref[slot] = part
                else:
                    away_ref[slot] = part.astype(LOW)


def out_grad_kernel(place, *refs):
    parts, grads, near_ref, away_ref, held, right, sems = refs[:4], refs[4:8], *refs[8:]
    step = near_ref.shape[1]
    rows = held.shape[2]
    sides = [right.at[at * rows : (at + 1) * rows] for at in range(4)]
    for copy in fetch(parts + grads, [held.at[at] for at in range(4)] + sides, sems):
        copy.wait()
    for stays in range(2):
        which = place[3] if stays else 1 - place[3]
        left = jnp.concatenate([held[at, which] for at in range(4)], axis=0)
        total = dot_cols(left, right[...])
        for at in range(4):
            slot = lax.bitwise_xor(place[5], at)
            if stays:
                near_ref[slot] = total[at * step : (at + 1) * step]
            else:
                away_ref[slot] = total[at * step : (at + 1) * step].astype(LOW)


def qkv_grad_kernel(place, *refs):
    grad_ref, top_ref, mid_ref, units_a, units_b = refs[:5]
    slots, refs = refs[5:13], refs[13:]
    near_ref, away_ref, total_ref, sums_ref, tokens_ref, sems = refs
    rows = grad_ref.shape[1]
    held = [tokens_ref.at[at * rows : (at + 1) * rows] for at in range(8)]
    copies = fetch(slots, held, sems)
    rank, seq_at = place[0], place[1]
    width = sums_ref.shape[1]
    own = width // 8
    quarter = width // 4
    col_sum = 0.0
    for pair in range(4):
        grads = [grad_ref[lax.bitwise_xor(rank, 2 * pair + at)] for at in range(2)]
        grads = jnp.concatenate(grads, axis=0)
        copies[2 * pair].wait()
        copies[2 * pair + 1].wait()
        term = dot_cols(tokens_ref[2 * pair * rows : 2 * (pair + 1) * rows], grads)
        col_sum += jnp.sum(grads.astype(FULL), axis=0, keepdims=True)
        if pair == 0:
            total_ref[...] = term
        else:
            total_ref[...] += term
    sums_ref[...] = jnp.zeros_like(sums_ref)
    sums_ref[0:1] = mid_ref[0:1]
    sums_ref[1:2] = top_ref[0:1]
    sums_ref[2:3] = mid_ref[1:2]
    sums_ref[3:4] = top_ref[1:2]
    own_cols = pl.ds(pl.multiple_of(rank * own, own), own)
    sums_ref[4:5, own_cols] = col_sum[:, :own]
    sums_ref[5:6, own_cols] = col_sum[:, 2 * own :]
    sums_ref[6:7] = mid_ref[2:3]
    sums_ref[7:8] = top_ref[2:3]
    row_at = lax.broadcasted_iota(jnp.int32, (8, own), 0)
    for at in (1, 3, 0, 2):
        whose = lax.bitwise_xor(seq_at, at)
        part = total_ref[quarter_span(place, at, quarter)]
        sums = sums_ref[:, quarter_span(place, at, quarter)]
        here = lax.shift_right_logical(whose, 1) == place[4]
        first = 4 * lax.bitwise_and(whose, 1)
        units = [units_a[first + row] + units_b[first + row] for row in range(4)]
        mine = (row_at >= 4 * place[8]) & (row_at < 4 * place[8] + 4)
        units = jnp.where(mine & here, jnp.concatenate(units + units, axis=0), 0.0)
        sums = jnp.concatenate([sums, units], axis=1)
        sums = jnp.concatenate([sums, jnp.zeros_like(sums)], axis=0)
        if at % 2:
            away_ref[at // 2, :quarter] = part.astype(LOW)
            away_ref[at // 2, quarter:] = sums.astype(LOW)
        else:
            near_ref[at // 2, :quarter] = part
            near_ref[at // 2, quarter:] = sums


def input_terms_kernel(place, across_ref, own_ref, *refs):
    sources, refs = refs[:5], refs[5:]
    near_ref, away_ref, cols_ref, beyond_ref, parts, sems = refs
    copies = fetch(sources, [cols_ref] + [parts.at[at] for at in range(4)], sems)
    rows = own_ref.shape[1]
    for copy in copies:
        copy.wait()
    put_columns(place, parts, beyond_ref)
    for slots in ((1, 3), (0, 2)):
        whose = [lax.bitwise_xor(place[5], slot) for slot in slots]
        left = jnp.concatenate([own_ref[place[4] * 4 + at] for at in whose], axis=0)
        term = dot_rows(left, cols_ref[...])
        left = jnp.concatenate([across_ref[at] for at in whose], axis=0)
        term += dot_rows(left, beyond_ref[...])
        for at, slot in enumerate(slots):
            part = term[at * rows : (at + 1) * rows]
            if slot % 2:
                away_ref[at] = part.astype(LOW)
            else:
                near_ref[at] = part


def qkv_send_kernel(place, near_ref, far_ref, out_ref):
    total = near_ref[...] + far_ref[...].astype(FULL)
    rows = total.shape[0] - 16
    step = rows // 8
    sums = total[rows:].astype(LOW)
    for at in range(8):
        out_ref[at, :step] = total[at * step : (at + 1) * step].astype(LOW)
        out_ref[at, step:] = sums


def qkv_last_kernel(place, parts_ref, grad_ref, sums_ref):
    step = grad_ref.shape[0]
    own = parts_ref.shape[2] // 3
    for at in range(8):
        for which in range(3):
            cols = slice((which * 8 + at) * own, (which * 8 + at + 1) * own)
            grad_ref[:, cols] = parts_ref[at, :step, which * own : (which + 1) * own].astype(FULL)
    sums = parts_ref[0, step:].astype(FULL)
    for at in range(1, 8):
        sums += parts_ref[at, step:].astype(FULL)
    sums_ref[...] = sums


def grouped_body(tokens, out_grad, w_qkv, w_out, fc_in, fc_out, fc_in_bias, vectors):
    rows, width = tokens.shape
    own = width // 8
    seq_at = lax.axis_index("seq")
    core_at, across_at = lax.rem(seq_at, 2), seq_at // 2
    head_at, blk_at = lax.axis_index("head"), lax.axis_index("blk")
    rank = head_at * 4 + blk_at
    far_at, near_at = blk_at // 2, lax.rem(blk_at, 2)
    place = jnp.stack(
        [rank, seq_at, core_at, across_at, head_at, blk_at, far_at ^ core_at, far_at, near_at]
    ).astype(jnp.int32)
    unit_rows = fc_in.shape[0] // 4
    units = 8 * unit_rows

    quarter = own // 4
    qkv_rows = lax.dynamic_slice_in_dim(w_qkv, seq_at * quarter, quarter, 0)
    qkv_rows = qkv_rows.reshape(quarter, 3, 8, own).transpose(2, 1, 0, 3)
    qkv_rows = qkv_rows.reshape(8, 3 * quarter, own)
    small = jnp.concatenate([vectors.T, fc_in_bias.reshape(-1, own)], axis=0)
    small = jnp.broadcast_to(small[None], (8, 12, own))
    to_swap = jnp.concatenate([qkv_rows, small, jnp.zeros((8, 4, own), LOW)], axis=1)
    out_quarter = lax.dynamic_slice_in_dim(w_out, seq_at * 2 * own, 2 * own, 1)
    out_quarter = out_quarter.reshape(own, 2, own).transpose(1, 0, 2).reshape(1, 2 * own, own)
    out_quarter = jnp.broadcast_to(out_quarter, (8, 2 * own, own))
    units_away = jnp.stack(
        [lax.dynamic_slice_in_dim(w, seq_at * unit_rows, unit_rows, 0) for w in (fc_in, fc_out)]
    )

    inner = inner_blk()
    first = lax.ppermute(tokens, "blk", PAIRS)
    middle = lax.ppermute(tokens, "blk", INNER)
    across_0 = flip_head(tokens)
    first, middle, across_0, to_swap = after((first, middle, across_0, to_swap))
    second_in = lax.ppermute(first, "blk", INNER)
    second_out = lax.ppermute(middle, "blk", OUTER)
    across_1 = flip_head(first)
    swapped = lax.all_to_all(to_swap, GROUP, 0, 0, tiled=True)
    second_in, second_out, across_1, swapped, out_quarter = after(
        (second_in, second_out, across_1, swapped, out_quarter)
    )
    out_quarter = lax.all_to_all(out_quarter, GROUP, 0, 0, tiled=True).reshape(8, 2, own, own)
    third = lax.ppermute(second_in, "blk", OUTER)
    second = jnp.where(inner, second_in, second_out)
    across_2 = flip_head(second)
    qkv_own = swapped[:, : 3 * quarter].reshape(8, 3, quarter, own)
    qkv_across = lax.ppermute(qkv_own, "seq", ACROSS)
    small = swapped[:, 3 * quarter : 3 * quarter + 12].astype(FULL)
    vec = small[:, :8].transpose(1, 0, 2).reshape(8, width)
    bias_all = small[:, 8:].reshape(32, 1, own)
    third, across_2, qkv_own, qkv_across = after((third, across_2, qkv_own, qkv_across))
    third = jnp.where(inner, middle, third)
    across_3 = flip_head(third)
    qkv_quarters = [qkv_own, lax.ppermute(qkv_own, "seq", CORE)]
    qkv_quarters += [qkv_across, lax.ppermute(qkv_across, "seq", CORE)]
    across_3, out_quarter, units_away, *qkv_quarters = after(
        [across_3, out_quarter, units_away] + qkv_quarters
    )
    beyond = flip_head(qkv_quarters[0])
    slots = [tokens, first, second, third, across_0, across_1, across_2, across_3]

    units_two_on = lax.ppermute(units_away, "blk", TWO_ON)
    bias = vectors.T.reshape(8, 1, own)[4:6].astype(FULL)
    seq_rows = 8 * rows
    heads = own // HEAD_DIM
    kept_shapes = [((seq_rows, own), LOW)] * 3 + [((seq_rows, own), FULL)] * 2
    kept_shapes.append(((width, 3 * own), LOW))
    kept_shapes.append(((heads, seq_rows, seq_rows), LOW))
    kept_scratch = [pltpu.VMEM(*shape) for shape in kept_shapes]
    context, *kept = call(
        attend_kernel,
        [shape_of((8, rows, own), LOW)] + [shape_of(*shape) for shape in kept_shapes],
        place, bias, *qkv_quarters, *slots,
        scratch=kept_scratch
        + [pltpu.VMEM((seq_rows, width), LOW), pltpu.VMEM((4, 8, 3, quarter, own), LOW)]
        + [pltpu.SemaphoreType.DMA((16,)), pltpu.SemaphoreType.DMA((12,))],
        flops=8 * 10**9,
        far_in=12,
        far_out=7,
        vmem=56,
    )
    out_across = lax.ppermute(out_quarter, "seq", ACROSS)
    context, out_across, out_quarter = after((context, out_across, out_quarter))
    out_slots = [out_quarter, lax.ppermute(out_quarter, "seq", CORE)]
    out_slots += [out_across, lax.ppermute(out_across, "seq", CORE)]
    context = lax.all_to_all(context, GROUP, 0, 0, tiled=True)
    beyond = after(beyond, *out_slots[1:])
    beyond_across = lax.ppermute(beyond, "seq", ACROSS)
    beyond_quarters = [beyond, lax.ppermute(beyond, "seq", CORE)]
    beyond_quarters += [beyond_across, lax.ppermute(beyond_across, "seq", CORE)]
    ffn_weights = [fc_in, fc_out] + gather_seq(units_two_on)
    out_scratch = [pltpu.VMEM((8, own, width), LOW), pltpu.SemaphoreType.DMA((8,))]

    per_row = shape_of((rows, width), FULL)
    per_row_low = shape_of((rows, width), LOW)
    middle, middle_low, norm_one, scale_one = call(
        mix_kernel,
        [per_row, per_row_low, per_row, shape_of((rows, 1), FULL)],
        place, context, tokens, vec, *out_slots,
        scratch=[pltpu.VMEM((rows, width), LOW)] + out_scratch,
        flops=2 * 10**9,
        far_in=4,
    )

    both_rows = shape_of((2 * rows, units), FULL)
    both_rows_low = shape_of((2 * rows, units), LOW)
    middle_slots = gather_four(middle_low)
    ffn_scratch = [pltpu.VMEM((2 * rows, width), FULL)]
    ffn_scratch += [pltpu.VMEM((2, 4 * unit_rows, width), LOW)] * 2
    ffn_scratch += [pltpu.SemaphoreType.DMA((10,))]
    ffn_parts = []
    for at in (0, 2):
        ffn_parts.append(
            call(
                ffn_kernel,
                [both_rows, both_rows_low, per_row, per_row_low],
                place, middle_slots[at], middle_slots[at + 1], bias_all, *ffn_weights,
                scratch=ffn_scratch,
                flops=3 * 10**9,
                far_in=6,
            )
        )

    def features_of(core, head):
        both = lax.dynamic_index_in_dim(context.reshape(2, 2, 2, rows, own), core, 1, False)
        return lax.dynamic_index_in_dim(both, head, 1, False)

    diagonal = []
    for seq in range(4):
        for head in range(2):
            diagonal.append((seq * 2 + head, (seq ^ 1) * 2 + 1 - head))
    parts = [
        features_of(core_at, head_at),
        features_of(1 - core_at, head_at),
        features_of(core_at, 1 - head_at),
        features_of(1 - core_at, 1 - head_at),
    ]
    parts[1:] = after(parts[1:], ffn_parts[0][1])
    parts = [
        parts[0],
        lax.ppermute(parts[1], "seq", CORE),
        flip_head(parts[2]),
        lax.ppermute(parts[3], ("seq", "head"), tuple(diagonal)),
    ]

    def scatter_parts(near_part, far_part):
        sent_far = lax.ppermute(far_part[1], "blk", PAIRS).astype(FULL)
        far = flip_head((far_part[0] + sent_far).astype(LOW))
        return near_part[0], lax.ppermute(near_part[1], "blk", PAIRS), far

    weight_scratch = [pltpu.VMEM((2 * rows, units), LOW)] * 2
    weight_scratch += [pltpu.VMEM((2 * rows, width), LOW)] * 2 + [pltpu.SemaphoreType.DMA((6,))]
    terms = [shape_of((4, unit_rows, width), FULL), shape_of((4, unit_rows, width), LOW)]

    def weight_grads(lefts, rights):
        return call(
            weight_grad_kernel, terms, place, *lefts, *rights,
            scratch=weight_scratch, flops=2 * 10**9, far_in=6,
        )

    def add_low(near, sent):
        return near + sent.astype(FULL)

    summed = scatter_parts(ffn_parts[0][2:4], ffn_parts[1][2:4])
    summed = after(summed, *beyond_quarters)
    three_sums = shape_of((3, width), FULL)
    layer_output, grad_two, grad_ffn, top_sums = call(
        top_kernel,
        [per_row, per_row, per_row_low, three_sums],
        place, *summed, middle, vec, out_grad,
        flops=10**9,
    )

    grad_ffn_slots = gather_four(grad_ffn)
    back_parts = []
    for at in (0, 2):
        pre = ffn_parts[at // 2][0]
        cdf = 0.5 * (1.0 + lax.erf(pre * (0.5**0.5)))
        slope = cdf + pre * jnp.exp(-0.5 * pre * pre) * ((2.0 * math.pi) ** -0.5)
        back_parts.append(
            call(
                ffn_back_kernel,
                [both_rows_low, per_row, per_row_low, shape_of((8, 1, unit_rows), FULL)],
                place, grad_ffn_slots[at], grad_ffn_slots[at + 1], slope, *ffn_weights,
                scratch=ffn_scratch,
                flops=3 * 10**9,
                far_in=6,
            )
        )
    summed = scatter_parts(back_parts[0][1:3], back_parts[1][1:3])
    grad_one, grad_attn, grad_context, mid_sums = call(
        mix_back_kernel,
        [per_row, per_row_low, shape_of((8, rows, own), LOW), three_sums],
        place, *summed, grad_two, norm_one, scale_one, vec, *out_slots,
        scratch=out_scratch,
        flops=2 * 10**9,
        far_in=4,
    )
    grad_context = lax.all_to_all(grad_context, GROUP, 0, 0, tiled=True)
    acts = after((ffn_parts[0][1], ffn_parts[1][1]), grad_one)
    out_near_grad, out_away_grad = weight_grads(acts, grad_ffn_slots)
    out_sent = lax.ppermute(out_away_grad, "seq", CORE)
    out_across = lax.ppermute(
        add_low(out_near_grad[2:], out_sent[2:]).astype(LOW), "seq", ACROSS
    )
    in_near_grad, in_away_grad = weight_grads((back_parts[0][0], back_parts[1][0]), middle_slots)
    in_sent = lax.ppermute(in_away_grad, "seq", CORE)
    attn_across = flip_head(grad_attn)

    def kept_here(near, sent, across, at):
        return add_low(near[at] + sent[at].astype(FULL), across[at])

    in_across = add_low(in_near_grad[2:], in_sent[2:]).astype(LOW)
    out_last = kept_here(out_near_grad, out_sent, out_across, 1).astype(LOW)
    grad_context, in_across, out_last, attn_across = after(
        (grad_context, in_across, out_last, attn_across)
    )
    in_across = lax.ppermute(in_across, "seq", ACROSS)
    out_last = lax.ppermute(out_last, "blk", TWO_ON)
    grad_attn_slots = [grad_attn, lax.ppermute(grad_attn, "seq", CORE)]
    grad_attn_slots += [attn_across, lax.ppermute(attn_across, "seq", CORE)]
    (grad_cols,) = call(
        attend_back_kernel,
        [shape_of((8, rows, 3 * own), LOW)],
        place, grad_context, *kept[:5], kept[6],
        scratch=kept_scratch[:5]
        + kept_scratch[6:]
        + [pltpu.VMEM((own, seq_rows), FULL)] * 2
        + [pltpu.SemaphoreType.DMA((9,))],
        flops=8 * 10**9,
        far_in=6,
        vmem=56,
    )

    cols_sent = lax.dynamic_slice_in_dim(grad_cols, (1 - head_at) * 4, 4, 0)
    cols_sent = flip_head(cols_sent)
    in_last = kept_here(in_near_grad, in_sent, in_across, 1).astype(LOW)
    in_last = lax.ppermute(in_last, "blk", TWO_ON)
    payload_rows = 2 * own + 16
    near, away = call(
        qkv_grad_kernel,
        [shape_of((2, payload_rows, 3 * own), FULL), shape_of((2, payload_rows, 3 * own), LOW)],
        place, grad_cols, top_sums, mid_sums, back_parts[0][3], back_parts[1][3], *slots,
        scratch=[pltpu.VMEM((width, 3 * own), FULL), pltpu.VMEM((8, width), FULL)]
        + [pltpu.VMEM((seq_rows, width), LOW), pltpu.SemaphoreType.DMA((8,))],
        vmem=56, flops=2 * 10**9,
        far_in=8,
    )
    sent = lax.ppermute(away, "seq", CORE)
    near_terms, away_terms = call(
        input_terms_kernel,
        [
            shape_of((2, rows, width), FULL),
            shape_of((2, rows, width), LOW),
        ],
        place, cols_sent, grad_cols, kept[5], *beyond_quarters,
        scratch=[pltpu.VMEM((width, 3 * own), LOW)] * 2
        + [pltpu.VMEM((4, 8, 3, quarter, own), LOW), pltpu.SemaphoreType.DMA((5,))],
        flops=2 * 10**9,
        far_in=5,
    )
    sent_terms = lax.ppermute(away_terms, "blk", PAIRS)
    out_terms = [shape_of((4, own // 4, width), FULL), shape_of((4, own // 4, width), LOW)]
    near_rows, away_rows = call(
        out_grad_kernel, out_terms, place, *parts, *after(grad_attn_slots, away_terms),
        scratch=[pltpu.VMEM((4, 2, rows, own), LOW), pltpu.VMEM((4 * rows, width), LOW)]
        + [pltpu.SemaphoreType.DMA((8,))],
        flops=10**9,
        far_in=8,
    )
    sent_rows = lax.ppermute(away_rows, "seq", ACROSS)

    last_terms = after(add_low(near_terms[1], sent_terms[1]).astype(LOW), in_last)
    last_terms = lax.ppermute(last_terms, "blk", TWO_ON)
    out_rows = add_low(near_rows, sent_rows)
    odd_rows = after(out_rows.reshape(2, 2, -1, width)[:, 1].astype(LOW), sent_terms)
    sent_rows = lax.ppermute(odd_rows, "blk", PAIRS)
    last_rows = lax.ppermute(add_low(out_rows[2], sent_rows[1]).astype(LOW), "blk", TWO_ON)
    grad_w_out = add_low(add_low(out_rows[0], sent_rows[0]), last_rows)
    far = lax.ppermute(add_low(near[1], sent[1]).astype(LOW), "seq", ACROSS)
    unit_grads = jnp.stack(
        [
            add_low(kept_here(in_near_grad, in_sent, in_across, 0), in_last),
            add_low(kept_here(out_near_grad, out_sent, out_across, 0), out_last),
        ]
    )
    (payload,) = call(
        qkv_send_kernel,
        [shape_of((8, own // 4 + 16, 3 * own), LOW)],
        place, add_low(near[0], sent[0]), far,
    )
    payload = lax.all_to_all(payload, GROUP, 0, 0, tiled=True)
    input_grad = grad_one + add_low(add_low(near_terms[0], sent_terms[0]), last_terms)

    moves = []
    for across in range(2):
        for core in range(2):
            for head in range(2):
                for two_on in range(2):
                    for near_by in range(2):
                        start = (across * 2 + core) * 8 + head * 4 + two_on * 2 + near_by
                        stop = (head * 2 + core) * 8 + near_by * 4 + two_on * 2 + across
                        if start != stop:
                            moves.append((start, stop))
    stays = (across_at == head_at) & (head_at == near_at)

    moved = lax.ppermute(unit_grads.astype(LOW), ("seq", "head", "blk"), moves).astype(FULL)
    grad_fc_in, grad_fc_out = jnp.where(stays, unit_grads, moved)

    grad_w_qkv, sums = call(
        qkv_last_kernel,
        [shape_of((own // 4, 3 * width), FULL), shape_of((16, 3 * own), FULL)],
        place, payload,
    )
    grad_vectors = lax.dynamic_slice(sums, (0, rank * (own // 4)), (8, own // 4)).T
    grad_bias = lax.dynamic_slice(sums, (rank, 2 * own), (1, own)).reshape(own)
    return (
        layer_output,
        input_grad,
        grad_w_qkv,
        grad_w_out,
        grad_fc_in,
        grad_fc_out,
        grad_bias,
        grad_vectors,
    )


def solution(mesh):
    sizes = tuple(mesh.shape[name] for name in ("seq", "head", "blk"))
    return jax.shard_map(
        grouped_body if sizes == (4, 2, 4) else general_body,
        mesh=mesh,
        in_specs=(
            P(("seq", "head", "blk"), None),
            P(("seq", "head", "blk"), None),
            P(("head", "blk"), None),
            P(("head", "blk"), None),
            P(("head", "blk"), None),
            P(("head", "blk"), None),
            P(("head", "blk")),
            P(("head", "blk"), None),
        ),
        out_specs=(
            P(("seq", "head", "blk"), None),
            P(("seq", "head", "blk"), None),
            P(("seq", "head", "blk"), None),
            P(("seq", "head", "blk"), None),
            P(("seq", "head", "blk"), None),
            P(("seq", "head", "blk"), None),
            P(("seq", "head", "blk")),
            P(("seq", "head", "blk"), None),
        ),
        check_vma=False,
    )
```
